32 devices in a mesh: skill: 16 (over z, y, x), tensor: 2 (over core).
Axes of the slice: x: 2, y: 2, z: 4, core: 2. Of those that a mesh axis runs over, the one named last changes fastest.
Arguments:
- stored_inputs: bfloat16 [16, 256, 8192], P('skill', None, 'tensor'), may hold values from -6 to 6
- stored_output_gradient: bfloat16 [16, 256, 15360], P('skill', None, 'tensor'), may hold values from -6 to 6
- training_token_index: int32 [16, 256], P('skill'), may hold values from 0 to 255
- validation_inputs: bfloat16 [16, 512, 8192], P('skill', None, 'tensor'), may hold values from -6 to 6
- validation_output_gradient: bfloat16 [16, 512, 15360], P('skill', None, 'tensor'), may hold values from -6 to 6
- validation_row_skill: int32 [16, 512], P('skill'), may hold values from 0 to 15
- adapter_down_init: bfloat16 [16, 8192, 64], P('skill', 'tensor'), may hold values from -0.0625 to 0.0625
Outputs:
- own_delta: float32 [16, 5], P('skill')
- other_delta: float32 [16, 5], P('skill')
The draws below stay inside these ranges and needn't reach their ends.
All inputs are finite; a program needn't handle non-finite values.
Results may differ from the reference program's by a relative error of at most 0.0042.
Values may be sent and summed in bfloat16 or wider, within the bound.
No kernel may reach another device: no remote copies, remote signals or barrier semaphores. Data moves between devices by JAX's collectives and lax.ppermute only.
A program may use at most 64 MiB of HBM per device.

```python
import jax
import jax.numpy as jnp
from jax import lax

MODEL_WIDTH = 8192
FW = 15360
ADAPTER_RANK = 64
TRAIN = 256
VAL = 512
SKILL_COUNT = 16
REACH = 2
COLUMNS = 5


def draw_validation_row_skill(key, part):
    flip_key = jax.random.fold_in(key, 11)
    pick_key = jax.random.fold_in(key, 12)
    coin_flip = jax.random.randint(flip_key, (SKILL_COUNT, VAL), 0, 2)
    random_skill = jax.random.randint(pick_key, (SKILL_COUNT, VAL), 0, SKILL_COUNT)
    home_skill = lax.broadcasted_iota(jnp.int32, (SKILL_COUNT, VAL), 0)
    return jnp.where(coin_flip == 1, home_skill, random_skill).astype(jnp.int32)


def touch_ends(drawn, key, smallest, high):
    dims = drawn.shape
    spot = [jax.random.randint(jax.random.fold_in(key, axis), (), 0, dims[axis]) for axis in range(len(dims))]
    drawn = drawn.at[tuple(spot)].set(smallest)
    longest = dims.index(max(dims))
    spot[longest] = (spot[longest] + 1) % dims[longest]
    return drawn.at[tuple(spot)].set(high)


def steps_of(stream_key, dims, cuts, low, top_value):
    gain, own = 1.0, jax.random.fold_in(stream_key, 6)
    for dim, shards_of in cuts:
        steps = jnp.exp(jax.random.uniform(jax.random.fold_in(own, dim), (shards_of,), jnp.float32, low / len(cuts), top_value / len(cuts)))
        gain = gain * jnp.repeat(steps, dims[dim] // shards_of).reshape([-1 if axis == dim else 1 for axis in range(len(dims))])
    return gain


def scatter_about(stream_key, extent, deviation, limit, pieces=(), kind=jnp.bfloat16):
    factor_of = steps_of(stream_key, extent, pieces, -0.22, 0.18) if pieces else 1.0
    array = jax.random.normal(stream_key, extent, jnp.float32) * deviation * factor_of
    return jnp.minimum(jnp.maximum(array, -limit), limit).astype(kind)


def setup_inputs(seed: int = 0) -> dict:
    seeds = jax.random.split(jax.random.key(seed), 8)
    stored_inputs = scatter_about(seeds[0], (SKILL_COUNT, TRAIN, MODEL_WIDTH), 1.0, 6.0, ((0, 16), (2, 2)))
    stored_output_gradient = scatter_about(seeds[1], (SKILL_COUNT, TRAIN, FW), 1.0, 6.0, ((0, 16), (2, 2)))
    training_token_index = touch_ends(jax.random.randint(seeds[2], (SKILL_COUNT, TRAIN), 0, TRAIN), jax.random.fold_in(seeds[2], 1), 0, TRAIN - 1).astype(jnp.int32)
    validation_inputs = scatter_about(seeds[3], (SKILL_COUNT, VAL, MODEL_WIDTH), 1.0, 6.0, ((0, 16), (2, 2)))
    validation_output_gradient = scatter_about(seeds[4], (SKILL_COUNT, VAL, FW), 1.0, 6.0, ((0, 16), (2, 2)))
    validation_row_skill = draw_validation_row_skill(jax.random.fold_in(seeds[7], 71), 0)
    adapter_down_init = scatter_about(seeds[6], (SKILL_COUNT, MODEL_WIDTH, ADAPTER_RANK), MODEL_WIDTH ** -0.5, 0.0625, ((0, 16), (1, 2)))
    return dict(stored_inputs=stored_inputs, stored_output_gradient=stored_output_gradient, training_token_index=training_token_index, validation_inputs=validation_inputs, validation_output_gradient=validation_output_gradient, validation_row_skill=validation_row_skill, adapter_down_init=adapter_down_init)


def train_single_skill(inputs):
    stored_act, stored_cot, chosen, down_factor = inputs
    train_act = jnp.take(stored_act, chosen, axis=0)
    train_cot = jnp.take(stored_cot, chosen, axis=0)
    proj = jnp.dot(train_act, down_factor, preferred_element_type=jnp.float32).astype(jnp.bfloat16)
    product = lax.dot_general(proj, train_cot, (((0,), (0,)), ((), ())), preferred_element_type=jnp.float32)
    return (product * (-1.0 / TRAIN)).astype(jnp.bfloat16)


def reference(stored_inputs, stored_output_gradient, training_token_index, validation_inputs, validation_output_gradient, validation_row_skill, adapter_down_init):
    adapter_up_init = lax.map(train_single_skill, (stored_inputs, stored_output_gradient, training_token_index, adapter_down_init))

    def score_skill(skill_index):
        target_skills = (skill_index + jnp.arange(COLUMNS, dtype=jnp.int32) - REACH) % SKILL_COUNT
        selected_down = jnp.take(adapter_down_init, target_skills, axis=0).astype(jnp.float32)
        selected_up = jnp.take(adapter_up_init, target_skills, axis=0).astype(jnp.float32)
        valid_act = lax.dynamic_index_in_dim(validation_inputs, skill_index, 0, keepdims=False).astype(jnp.float32)
        valid_cot = lax.dynamic_index_in_dim(validation_output_gradient, skill_index, 0, keepdims=False).astype(jnp.float32)
        labels = lax.dynamic_index_in_dim(validation_row_skill, skill_index, 0, keepdims=False)
        own_mask = (labels == skill_index).astype(jnp.float32)
        other_mask = 1.0 - own_mask
        val_proj = jnp.einsum("vd,kdr->kvr", valid_act, selected_down, precision=lax.Precision.HIGHEST)
        cot_proj = jnp.einsum("vf,krf->kvr", valid_cot, selected_up, precision=lax.Precision.HIGHEST)
        row_change = jnp.sum(val_proj * cot_proj, axis=2)
        own_sum = jnp.sum(row_change * own_mask[None, :], axis=1)
        other_sum = jnp.sum(row_change * other_mask[None, :], axis=1)
        own_count = jnp.maximum(jnp.sum(own_mask), 1.0)
        other_count = jnp.maximum(jnp.sum(other_mask), 1.0)
        return own_sum / own_count, other_sum / other_count

    own_delta, other_delta = lax.map(score_skill, jnp.arange(SKILL_COUNT, dtype=jnp.int32))
    return own_delta, other_delta
```

```python
import functools

import jax
import jax.numpy as jnp
from jax import lax
from jax.experimental import pallas as pl
from jax.experimental.pallas import tpu as pltpu
from jax.sharding import PartitionSpec as P

VMEM_LIMIT = 40 * 1024 * 1024
NT = (((1,), (1,)), ((), ()))


def tile_of(width, most):
    fits = [size for size in range(128, min(width, most) + 1, 128) if width % size == 0]
    return fits[-1] if fits else width


def params():
    return pltpu.CompilerParams(
        dimension_semantics=("arbitrary",), vmem_limit_bytes=VMEM_LIMIT
    )


def project_kernel(count, rows_ref, *refs):
    factors, out_ref = refs[:count], refs[count]
    stacked = jnp.concatenate([f[...] for f in factors], axis=0) if count > 1 else factors[0][...]
    part = lax.dot_general(rows_ref[...], stacked, NT, preferred_element_type=jnp.float32)

    @pl.when(pl.program_id(0) == 0)
    def _():
        out_ref[...] = part

    @pl.when(pl.program_id(0) > 0)
    def _():
        out_ref[...] += part


def project(rows, factors):
    n, width = rows.shape
    rank = factors[0].shape[0]
    count = len(factors)
    tile = tile_of(width, 1024)
    return pl.pallas_call(
        functools.partial(project_kernel, count),
        grid=(width // tile,),
        in_specs=[pl.BlockSpec((n, tile), lambda k: (0, k))]
        + [pl.BlockSpec((rank, tile), lambda k: (0, k))] * count,
        out_specs=pl.BlockSpec((n, rank * count), lambda k: (0, 0)),
        out_shape=jax.ShapeDtypeStruct((n, rank * count), jnp.float32),
        compiler_params=params(),
        cost_estimate=pl.CostEstimate(
            flops=2 * n * width * rank * count,
            bytes_accessed=2 * width * (n + rank * count) + 4 * n * rank * count,
            transcendentals=0,
        ),
        name="project",
    )(rows, *factors)


def up_kernel(scale, mine_ref, other_ref, counts_ref, cot_ref, out_ref):
    rank = mine_ref.shape[0]
    proj = (mine_ref[...] + other_ref[...]).astype(jnp.bfloat16).astype(jnp.float32)
    weighted = proj * counts_ref[...]
    high = weighted.astype(jnp.bfloat16)
    low = (weighted - high.astype(jnp.float32)).astype(jnp.bfloat16)
    both = jnp.concatenate([high, low], axis=0)
    product = jnp.dot(both, cot_ref[...], preferred_element_type=jnp.float32)
    out_ref[...] = ((product[:rank] + product[rank:]) * scale).astype(jnp.bfloat16)


def up_factor(mine, other, counts, cot):
    rank, train = mine.shape
    width = cot.shape[1]
    tile = tile_of(width, 1536)
    whole = lambda k: (0, 0)
    return pl.pallas_call(
        functools.partial(up_kernel, -1.0 / train),
        grid=(width // tile,),
        in_specs=[
            pl.BlockSpec((rank, train), whole),
            pl.BlockSpec((rank, train), whole),
            pl.BlockSpec((1, train), whole),
            pl.BlockSpec((train, tile), lambda k: (0, k)),
        ],
        out_specs=pl.BlockSpec((rank, tile), lambda k: (0, k)),
        out_shape=jax.ShapeDtypeStruct((rank, width), jnp.bfloat16),
        compiler_params=params(),
        cost_estimate=pl.CostEstimate(
            flops=4 * rank * train * width,
            bytes_accessed=2 * width * (train + rank),
            transcendentals=0,
        ),
        name="up_factor",
    )(mine, other, counts, cot)


def score_kernel(count, first, masks_ref, mine_ref, other_ref, cot_ref, *refs):
    factors, out_ref, total = refs[:count], refs[count], refs[count + 1]
    rank = factors[0].shape[0]
    stacked = jnp.concatenate([f[...] for f in factors], axis=0) if count > 1 else factors[0][...]
    part = lax.dot_general(cot_ref[...], stacked, NT, preferred_element_type=jnp.float32)

    @pl.when(pl.program_id(0) == 0)
    def _():
        total[...] = part

    @pl.when(pl.program_id(0) > 0)
    def _():
        total[...] += part

    @pl.when(pl.program_id(0) == pl.num_programs(0) - 1)
    def _():
        columns = slice(first * rank, (first + count) * rank)
        change = total[...] * (mine_ref[:, columns] + other_ref[:, columns])
        own = change * masks_ref[:, 0:1]
        rest = change * masks_ref[:, 1:2]
        out_ref[0:1, :] = jnp.sum(own, axis=0, keepdims=True)
        out_ref[1:2, :] = jnp.sum(rest, axis=0, keepdims=True)


def score(masks, mine, other, cot, factors, first):
    n, width = cot.shape
    rank = factors[0].shape[0]
    count = len(factors)
    tile = tile_of(width, 1536)
    whole = lambda k: (0, 0)
    sums = pl.pallas_call(
        functools.partial(score_kernel, count, first),
        grid=(width // tile,),
        in_specs=[
            pl.BlockSpec(masks.shape, whole),
            pl.BlockSpec(mine.shape, whole),
            pl.BlockSpec(other.shape, whole),
            pl.BlockSpec((n, tile), lambda k: (0, k)),
        ]
        + [pl.BlockSpec((rank, tile), lambda k: (0, k))] * count,
        out_specs=pl.BlockSpec((2, rank * count), whole),
        out_shape=jax.ShapeDtypeStruct((2, rank * count), jnp.float32),
        scratch_shapes=[pltpu.VMEM((n, rank * count), jnp.float32)],
        compiler_params=params(),
        cost_estimate=pl.CostEstimate(
            flops=2 * n * width * rank * count,
            bytes_accessed=2 * width * (n + rank * count) + 8 * n * rank * count,
            transcendentals=0,
        ),
        name="score",
    )(masks, mine, other, cot, *factors)
    return jnp.sum(sums.reshape(2, count, rank), axis=2)


def rest_of_sum(block):
    parts = lax.axis_size("tensor")
    if parts == 2:
        return lax.ppermute(block, "tensor", [(0, 1), (1, 0)])
    return lax.psum(block, "tensor") - block


def send(block, target):
    count = lax.axis_size("skill")
    return lax.ppermute(block, "skill", [(s, target(s) % count) for s in range(count)])


def spread_quads(block, corner):
    by_x = send(block, lambda s: s ^ 1)
    by_y = send(block, lambda s: s ^ 2)
    by_z = send(by_y, lambda s: s - 4 if s & 2 else s + 4)
    ends = (corner == 0) | (corner == 3)
    last = send(jnp.where(ends, by_y, by_z), lambda s: s ^ 1)
    return [block, by_x, by_y, by_z, last]


QUAD_OFFSETS = ((0, 1, 2, -2, -1), (0, -1, 2, -2, 1), (0, 1, -2, 2, -1), (0, -1, -2, 2, 1))


def spread_ring(block, reach):
    slots, ahead, behind = [block], block, block
    for _ in range(reach):
        ahead = send(ahead, lambda s: s - 1)
        behind = send(behind, lambda s: s + 1)
        slots += [ahead, behind]
    return slots


def on_device(
    stored_inputs,
    stored_output_gradient,
    training_token_index,
    validation_inputs,
    validation_output_gradient,
    validation_row_skill,
    adapter_down_init,
):
    skills = lax.axis_size("skill")
    reach = skills // 8
    my_skill = lax.axis_index("skill")
    corner = my_skill % 4
    quads = reach == 2
    down = adapter_down_init[0].T
    train = stored_inputs.shape[1]

    labels = validation_row_skill[0]
    own_mask = (labels == my_skill).astype(jnp.float32)
    other_mask = 1.0 - own_mask
    masks = jnp.stack([own_mask, other_mask], axis=1)
    counts = jnp.sum(
        (training_token_index[0][:, None] == jnp.arange(train)[None, :]).astype(jnp.float32),
        axis=0, keepdims=True,
    )

    spread = (lambda b: spread_quads(b, corner)) if quads else (lambda b: spread_ring(b, reach))
    downs = spread(down)
    partial_proj = project(down, [stored_inputs[0]])
    up = up_factor(partial_proj, rest_of_sum(partial_proj), counts, stored_output_gradient[0])
    ups = spread(up)

    mine = project(validation_inputs[0], downs)
    other = rest_of_sum(mine)
    groups = [(0, 3), (3, 4), (4, 5)] if quads else [(0, len(ups))]
    table = jnp.concatenate(
        [
            score(masks, mine, other, validation_output_gradient[0], ups[a:b], a)
            for a, b in groups
        ],
        axis=1,
    )
    totals = lax.psum(table, "tensor")

    if quads:
        offsets = jnp.array(QUAD_OFFSETS, jnp.int32)[corner]
    else:
        offsets = jnp.array([0] + [o for d in range(reach) for o in (d + 1, -d - 1)], jnp.int32)
    column = jnp.arange(2 * reach + 1, dtype=jnp.int32) - reach
    place = (offsets[None, :] == column[:, None]).astype(jnp.float32)
    ordered = jnp.sum(place[None, :, :] * totals[:, None, :], axis=2)
    own_count = jnp.maximum(jnp.sum(own_mask), 1.0)
    other_count = jnp.maximum(jnp.sum(other_mask), 1.0)
    return (ordered[0:1] / own_count, ordered[1:2] / other_count)


def solution(mesh):
    in_specs = (
        P("skill", None, "tensor"),
        P("skill", None, "tensor"),
        P("skill", None),
        P("skill", None, "tensor"),
        P("skill", None, "tensor"),
        P("skill", None),
        P("skill", "tensor", None),
    )
    out_specs = (P("skill", None), P("skill", None))
    return jax.shard_map(
        on_device, mesh=mesh, in_specs=in_specs, out_specs=out_specs, check_vma=False
    )
```

```python
import functools

import jax
import jax.numpy as jnp
from jax import lax
from jax.experimental import pallas as pl
from jax.experimental.pallas import tpu as pltpu
from jax.sharding import PartitionSpec as P

VMEM_LIMIT = 56 * 1024 * 1024
LANES = 128
NT = (((1,), (1,)), ((), ()))


def tile_of(width, most):
    fits = [size for size in range(LANES, min(width, most) + 1, LANES) if width % size == 0]
    return fits[-1] if fits else width


def params():
    return pltpu.CompilerParams(
        dimension_semantics=("arbitrary",), vmem_limit_bytes=VMEM_LIMIT
    )


def cost(flops, size):
    return pl.CostEstimate(flops=flops, bytes_accessed=size, transcendentals=0)


def whole(k):
    return (0, 0)


def stack(refs):
    return jnp.concatenate([r[...] for r in refs], axis=0) if len(refs) > 1 else refs[0][...]


def fold(block):
    total = block[:, :LANES]
    for start in range(LANES, block.shape[1], LANES):
        total = total + block[:, start : start + LANES]
    return jnp.sum(total, axis=0, keepdims=True)


def project_kernel(count, *refs):
    factors, rows_ref, out_ref = refs[:count], refs[count], refs[count + 1]
    part = lax.dot_general(
        stack(factors), rows_ref[...], NT, preferred_element_type=jnp.float32
    )

    @pl.when(pl.program_id(0) == 0)
    def _():
        out_ref[...] = part

    @pl.when(pl.program_id(0) > 0)
    def _():
        out_ref[...] += part


def project(factors, rows):
    n, width = rows.shape
    count, rank = len(factors), factors[0].shape[0]
    tile = tile_of(width, 1024)
    return pl.pallas_call(
        functools.partial(project_kernel, count),
        grid=(width // tile,),
        in_specs=[pl.BlockSpec((rank, tile), lambda k: (0, k))] * count
        + [pl.BlockSpec((n, tile), lambda k: (0, k))],
        out_specs=pl.BlockSpec((rank * count, n), whole),
        out_shape=jax.ShapeDtypeStruct((rank * count, n), jnp.float32),
        compiler_params=params(),
        cost_estimate=cost(2 * n * width * rank * count, 2 * width * (n + rank * count)),
        name="project",
    )(*factors, rows)


def up_kernel(scale, mine_ref, other_ref, counts_ref, cot_ref, out_ref):
    rank = mine_ref.shape[0]
    proj = (mine_ref[...] + other_ref[...]).astype(jnp.bfloat16).astype(jnp.float32)
    weighted = proj * counts_ref[...]
    high = weighted.astype(jnp.bfloat16)
    low = (weighted - high.astype(jnp.float32)).astype(jnp.bfloat16)
    both = jnp.concatenate([high, low], axis=0)
    product = jnp.dot(both, cot_ref[...], preferred_element_type=jnp.float32)
    out_ref[...] = ((product[:rank] + product[rank:]) * scale).astype(jnp.bfloat16)


def up_factor(mine, other, counts, cot, start, width):
    rank, train = mine.shape
    tile = tile_of(width, 1280)
    first = start // tile
    return pl.pallas_call(
        functools.partial(up_kernel, -1.0 / train),
        grid=(width // tile,),
        in_specs=[
            pl.BlockSpec((rank, train), whole),
            pl.BlockSpec((rank, train), whole),
            pl.BlockSpec((1, train), whole),
            pl.BlockSpec((train, tile), lambda k: (0, first + k)),
        ],
        out_specs=pl.BlockSpec((rank, tile), lambda k: (0, k)),
        out_shape=jax.ShapeDtypeStruct((rank, width), jnp.bfloat16),
        compiler_params=params(),
        cost_estimate=cost(4 * rank * train * width, 2 * width * (train + rank)),
        name="up_factor",
    )(mine, other, counts, cot)


def weigh(masks_ref, mine_ref, other_ref, weighted):
    half = mine_ref.shape[0]
    proj = mine_ref[...] + other_ref[...]
    weighted[:half] = (proj * masks_ref[0:1, :]).astype(jnp.bfloat16)
    weighted[half:] = (proj * masks_ref[1:2, :]).astype(jnp.bfloat16)


def score_kernel(count, masks_ref, mine_ref, other_ref, cot_ref, *refs):
    ups, out_ref, weighted = refs[:count], refs[count], refs[count + 1]
    rank = ups[0].shape[0]

    @pl.when(pl.program_id(0) == 0)
    def _():
        weigh(masks_ref, mine_ref, other_ref, weighted)
        out_ref[...] = jnp.zeros_like(out_ref)

    against = jnp.dot(weighted[...], cot_ref[...], preferred_element_type=jnp.float32)
    for kind in range(2):
        for slot in range(count):
            row = kind * count + slot
            product = against[row * rank : (row + 1) * rank] * ups[slot][...].astype(jnp.float32)
            out_ref[row : row + 1, :] += fold(product)


def score(masks, mine, other, cot, ups, start):
    n = cot.shape[0]
    count, (rank, width) = len(ups), ups[0].shape
    tile = tile_of(width, 1280)
    first = start // tile
    rows = 2 * count * rank
    return pl.pallas_call(
        functools.partial(score_kernel, count),
        grid=(width // tile,),
        in_specs=[
            pl.BlockSpec(masks.shape, whole),
            pl.BlockSpec(mine.shape, whole),
            pl.BlockSpec(other.shape, whole),
            pl.BlockSpec((n, tile), lambda k: (0, first + k)),
        ]
        + [pl.BlockSpec((rank, tile), lambda k: (0, k))] * count,
        out_specs=pl.BlockSpec((2 * count, LANES), whole),
        out_shape=jax.ShapeDtypeStruct((2 * count, LANES), jnp.float32),
        scratch_shapes=[pltpu.VMEM((rows, n), jnp.bfloat16)],
        compiler_params=params(),
        cost_estimate=cost(2 * n * width * rows, 2 * width * (n + rank * count)),
        name="score",
    )(masks, mine, other, cot, *ups)


def against_kernel(masks_ref, mine_ref, other_ref, cot_ref, out_ref, weighted):
    @pl.when(pl.program_id(0) == 0)
    def _():
        weigh(masks_ref, mine_ref, other_ref, weighted)

    out_ref[...] = jnp.dot(weighted[...], cot_ref[...], preferred_element_type=jnp.float32)


def against(masks, mine, other, cot):
    n, width = cot.shape
    rows = 2 * mine.shape[0]
    tile = tile_of(width, 1280)
    return pl.pallas_call(
        against_kernel,
        grid=(width // tile,),
        in_specs=[
            pl.BlockSpec(masks.shape, whole),
            pl.BlockSpec(mine.shape, whole),
            pl.BlockSpec(other.shape, whole),
            pl.BlockSpec((n, tile), lambda k: (0, k)),
        ],
        out_specs=pl.BlockSpec((rows, tile), lambda k: (0, k)),
        out_shape=jax.ShapeDtypeStruct((rows, width), jnp.float32),
        scratch_shapes=[pltpu.VMEM((rows, n), jnp.bfloat16)],
        compiler_params=params(),
        cost_estimate=cost(2 * n * width * rows, width * (2 * n + 4 * rows)),
        name="against",
    )(masks, mine, other, cot)


def dot_kernel(pick_ref, own_ref, rest_ref, first_ref, *refs):
    out_ref = refs[-1]

    @pl.when(pl.program_id(0) == 0)
    def _():
        out_ref[...] = jnp.zeros_like(out_ref)

    up = first_ref[...]
    if len(refs) == 2:
        up = jnp.where(pick_ref[0] > 0, up, refs[0][...])
    up = up.astype(jnp.float32)
    out_ref[0:1, :] += fold(up * own_ref[...])
    out_ref[1:2, :] += fold(up * rest_ref[...])


def dot(pick, pulled, slot, slots, start, *ups):
    rank, width = ups[0].shape
    tile = tile_of(width, 1280)
    first = start // tile
    return pl.pallas_call(
        dot_kernel,
        grid=(width // tile,),
        in_specs=[
            pl.BlockSpec(memory_space=pltpu.SMEM),
            pl.BlockSpec((rank, tile), lambda k: (slot, first + k)),
            pl.BlockSpec((rank, tile), lambda k: (slots + slot, first + k)),
        ]
        + [pl.BlockSpec((rank, tile), lambda k: (0, k))] * len(ups),
        out_specs=pl.BlockSpec((2, LANES), whole),
        out_shape=jax.ShapeDtypeStruct((2, LANES), jnp.float32),
        compiler_params=params(),
        cost_estimate=cost(4 * rank * width, rank * width * (8 + 2 * len(ups))),
        name="dot",
    )(pick, pulled, pulled, *ups)


def table_kernel(layout, pad, *refs):
    parts, out_ref = refs[:-1], refs[-1]
    out_ref[...] = jnp.zeros_like(out_ref)
    for part, slots in zip(parts, layout):
        block = jnp.sum(part[...], axis=1, keepdims=True)
        for at, slot in enumerate(slots):
            for kind in range(2):
                row = kind * pad + slot
                source = kind * len(slots) + at
                out_ref[row : row + 1, :] += jnp.broadcast_to(
                    block[source : source + 1], (1, LANES)
                )


def table_of(parts, layout, pad):
    return pl.pallas_call(
        functools.partial(table_kernel, layout, pad),
        out_shape=jax.ShapeDtypeStruct((2 * pad, LANES), jnp.float32),
        compiler_params=pltpu.CompilerParams(vmem_limit_bytes=VMEM_LIMIT),
        cost_estimate=cost(1024, 1024),
        name="table",
    )(*parts)


def finish_kernel(columns, mine_ref, other_ref, place_ref, counts_ref, own_ref, rest_ref):
    pad = place_ref.shape[0]
    total = mine_ref[...] + other_ref[...]
    own = jnp.sum(total[:pad] * place_ref[...], axis=0, keepdims=True) / counts_ref[0:1, :]
    rest = jnp.sum(total[pad:] * place_ref[...], axis=0, keepdims=True) / counts_ref[1:2, :]
    own_ref[...] = own[:, :columns]
    rest_ref[...] = rest[:, :columns]


def finish(mine, other, place, counts, columns):
    shape = jax.ShapeDtypeStruct((1, columns), jnp.float32)
    return pl.pallas_call(
        functools.partial(finish_kernel, columns),
        out_shape=(shape, shape),
        compiler_params=pltpu.CompilerParams(vmem_limit_bytes=VMEM_LIMIT),
        cost_estimate=cost(1024, 1024),
        name="finish",
    )(mine, other, place, counts)


def rest_of_sum(block):
    parts = lax.axis_size("tensor")
    if parts == 2:
        return lax.ppermute(block, "tensor", [(0, 1), (1, 0)])
    return lax.psum(block, "tensor") - block


def send(block, target, corners=None):
    count = lax.axis_size("skill")
    pairs = [(s, target(s) % count) for s in range(count) if corners is None or s % 4 in corners]
    return lax.ppermute(block, "skill", pairs)


def across(s):
    return s ^ 1


def down(s):
    return s ^ 2


def next_quad(s):
    return s - 4 if s & 2 else s + 4


QUAD_OFFSETS = ((0, 1, 2, -2, -1), (0, -1, 2, -2, 1), (0, 1, -2, 2, -1), (0, -1, -2, 2, 1))


def spread_across(block, ends):
    by_x = send(block, across)
    by_y = send(block, down)
    by_z = send(by_y, next_quad)
    last = send(jnp.where(ends, by_y, by_z), across)
    return [block, by_x, by_y, by_z, (last,)]


def spread_down(block):
    by_x = send(block, across)
    by_y = send(block, down)
    by_z = send(by_y, next_quad)
    diagonal = send(by_x, down)
    passed_on = send(diagonal, next_quad, (0, 3))
    return [block, by_x, by_y, by_z, (passed_on, diagonal)]


def spread_ring(block, reach):
    slots, ahead, behind = [block], block, block
    for _ in range(reach):
        ahead = send(ahead, lambda s: s - 1)
        behind = send(behind, lambda s: s + 1)
        slots += [ahead, behind]
    return slots


def on_device(
    stored_inputs,
    stored_output_gradient,
    training_token_index,
    validation_inputs,
    validation_output_gradient,
    validation_row_skill,
    adapter_down_init,
):
    reach = lax.axis_size("skill") // 8
    columns = 2 * reach + 1
    pad = -(-columns // 8) * 8
    my_skill = lax.axis_index("skill")
    corner = my_skill % 4
    ends = (corner == 0) | (corner == 3)
    pick = ends.astype(jnp.int32)[None]
    quads = reach == 2
    factor = adapter_down_init[0].T
    valid_act = validation_inputs[0]
    valid_cot = validation_output_gradient[0]
    cot = stored_output_gradient[0]
    train, hidden = cot.shape

    own_mask = (validation_row_skill == my_skill).astype(jnp.float32)
    masks = jnp.concatenate([own_mask, 1.0 - own_mask], axis=0)
    row_counts = jnp.broadcast_to(
        jnp.maximum(jnp.sum(masks, axis=1, keepdims=True), 1.0), (2, LANES)
    )
    if quads:
        offsets = jnp.array(QUAD_OFFSETS, jnp.int32)[corner]
    else:
        offsets = jnp.array([0] + [o for d in range(reach) for o in (d + 1, -d - 1)], jnp.int32)
    offsets = jnp.pad(offsets, (0, pad - columns), constant_values=columns)
    lane = jnp.arange(LANES, dtype=jnp.int32) - reach
    place = (offsets[:, None] == lane[None, :]).astype(jnp.float32)
    counts = jnp.sum(
        (training_token_index[0][:, None] == jnp.arange(train)[None, :]).astype(jnp.float32),
        axis=0, keepdims=True,
    )

    downs = spread_across(factor, ends) if quads else spread_ring(factor, reach)
    proj = project([factor], stored_inputs[0])
    proj_rest = rest_of_sum(proj)
    parts, layout = [], []

    def add(part, slots):
        parts.append(part)
        layout.append(tuple(slots))

    if quads:
        half = hidden // 2
        first = spread_across(up_factor(proj, proj_rest, counts, cot, 0, half), ends)
        second = spread_down(up_factor(proj, proj_rest, counts, cot, half, half))
        near = project(downs[:3], valid_act)
        near_rest = rest_of_sum(near)
        far = project([downs[3], downs[4][0]], valid_act)
        far_rest = rest_of_sum(far)
        add(score(masks, near, near_rest, valid_cot, first[:3], 0), (0, 1, 2))
        add(score(masks, near, near_rest, valid_cot, second[:3], half), (0, 1, 2))
        pulled = against(masks, far, far_rest, valid_cot)
        add(dot(pick, pulled, 0, 2, 0, first[3]), (3,))
        add(dot(pick, pulled, 0, 2, half, second[3]), (3,))
        add(dot(pick, pulled, 1, 2, 0, *first[4]), (4,))
        add(dot(pick, pulled, 1, 2, half, *second[4]), (4,))
    else:
        ups = spread_ring(up_factor(proj, proj_rest, counts, cot, 0, hidden), reach)
        for at in range(0, columns, 3):
            slots = range(at, min(at + 3, columns))
            mine = project([downs[s] for s in slots], valid_act)
            other = rest_of_sum(mine)
            add(score(masks, mine, other, valid_cot, [ups[s] for s in slots], 0), slots)

    table = table_of(parts, layout, pad)
    return finish(table, rest_of_sum(table), place, row_counts, columns)


def solution(mesh):
    in_specs = (
        P("skill", None, "tensor"),
        P("skill", None, "tensor"),
        P("skill", None),
        P("skill", None, "tensor"),
        P("skill", None, "tensor"),
        P("skill", None),
        P("skill", "tensor", None),
    )
    out_specs = (P("skill", None), P("skill", None))
    return jax.shard_map(
        on_device, mesh=mesh, in_specs=in_specs, out_specs=out_specs, check_vma=False
    )
```

```python
import functools

import jax
import jax.numpy as jnp
from jax import lax
from jax.experimental import pallas as pl
from jax.experimental.pallas import tpu as pltpu
from jax.sharding import PartitionSpec as P

VMEM_LIMIT = 56 * 1024 * 1024
LANES = 128
BYTES_PER_US = 3_000_000
NT = (((1,), (1,)), ((), ()))


def tile_of(width, most):
    fits = [size for size in range(LANES, min(width, most) + 1, LANES) if width % size == 0]
    return fits[-1] if fits else width


def params():
    return pltpu.CompilerParams(vmem_limit_bytes=VMEM_LIMIT)


def cost(microseconds):
    return pl.CostEstimate(
        flops=0, bytes_accessed=int(microseconds * BYTES_PER_US), transcendentals=0
    )


def total_of(parts):
    return functools.reduce(lambda a, b: a + b, parts)


def fetch(pairs, sems):
    copies = [pltpu.make_async_copy(a, b, sems.at[at]) for at, (a, b) in enumerate(pairs)]
    for copy in copies:
        copy.start()
    return copies


def call(kernel, name, operands, out_shape, scratch, copies, microseconds):
    return pl.pallas_call(
        kernel,
        in_specs=[pl.BlockSpec(memory_space=pl.ANY)] * len(operands),
        out_shape=out_shape,
        scratch_shapes=list(scratch) + [pltpu.SemaphoreType.DMA((copies,))],
        compiler_params=params(),
        cost_estimate=cost(microseconds),
        name=name,
    )(*operands)


def project_kernel(count, tile, *refs):
    rows_ref, factor_refs = refs[0], refs[1 : 1 + count]
    out_ref, rows, factors, sems = refs[-4:]
    rank = factor_refs[0].shape[0]
    columns = [slice(at, at + tile) for at in range(0, rows_ref.shape[1], tile)]
    copies = fetch(
        [(f, factors.at[at * rank : (at + 1) * rank]) for at, f in enumerate(factor_refs)]
        + [(rows_ref.at[:, c], rows.at[:, c]) for c in columns],
        sems,
    )
    for copy in copies[:count]:
        copy.wait()
    for at, c in enumerate(columns):
        copies[count + at].wait()
        part = lax.dot_general(
            rows[:, c], factors[:, c], NT, preferred_element_type=jnp.float32
        )
        if at == 0:
            out_ref[...] = part
        else:
            out_ref[...] += part


def project(rows, factors, microseconds, *after):
    n, width = rows.shape
    count, rank = len(factors), factors[0].shape[0]
    tile = tile_of(width, 1024)
    return call(
        functools.partial(project_kernel, count, tile),
        "project",
        (rows, *factors, *after),
        jax.ShapeDtypeStruct((n, rank * count), jnp.float32),
        [pltpu.VMEM((n, width), rows.dtype), pltpu.VMEM((rank * count, width), rows.dtype)],
        count + width // tile,
        microseconds,
    )


def up_kernel(scale, start, width, tile, mine_ref, other_ref, counts_ref, cot_ref, *refs):
    out_ref, mine, other, counts, cot, sems = refs[-6:]
    columns = [slice(at, at + tile) for at in range(0, width, tile)]
    copies = fetch(
        [(mine_ref, mine), (other_ref, other), (counts_ref, counts)]
        + [(cot_ref.at[:, start + c.start : start + c.stop], cot.at[:, c]) for c in columns],
        sems,
    )
    for copy in copies[:3]:
        copy.wait()
    proj = (mine[...] + other[...]).astype(jnp.bfloat16).astype(jnp.float32)
    weighted = proj * counts[...]
    high = weighted.astype(jnp.bfloat16)
    low = (weighted - high.astype(jnp.float32)).astype(jnp.bfloat16)
    both = jnp.concatenate([high, low], axis=0)
    rank = proj.shape[0]
    for copy, c in zip(copies[3:], columns):
        copy.wait()
        product = jnp.dot(both, cot[:, c], preferred_element_type=jnp.float32)
        out_ref[:, c] = ((product[:rank] + product[rank:]) * scale).astype(jnp.bfloat16)


def up_factor(mine, other, counts, cot, start, width, *after):
    rank, train = mine.shape
    tile = tile_of(width, 1280)
    return call(
        functools.partial(up_kernel, -1.0 / train, start, width, tile),
        "up_factor",
        (mine, other, counts, cot, *after),
        jax.ShapeDtypeStruct((rank, width), jnp.bfloat16),
        [
            pltpu.VMEM(mine.shape, jnp.float32),
            pltpu.VMEM(mine.shape, jnp.float32),
            pltpu.VMEM(counts.shape, jnp.float32),
            pltpu.VMEM((train, width), cot.dtype),
        ],
        3 + width // tile,
        2.0,
    )


def score_kernel(slots, picked, pad, start, tile, *refs):
    pick_ref, masks_ref, mine_ref, other_ref, cot_ref, table_ref = refs[:6]
    up_refs = refs[6:-7]
    out_ref, masks, mine, other, cot, ups, sems = refs[-7:]
    rank, width = up_refs[0].shape
    used = len(up_refs)
    columns = [slice(at, at + tile) for at in range(0, width, tile)]
    copies = fetch(
        [(u, ups.at[at * rank : (at + 1) * rank]) for at, u in enumerate(up_refs)]
        + [(cot_ref.at[:, start + c.start : start + c.stop], cot.at[:, c]) for c in columns]
        + [(masks_ref, masks), (mine_ref, mine), (other_ref, other), (table_ref, out_ref)],
        sems,
    )
    for copy in copies[:used]:
        copy.wait()
    last = (len(slots) - 1) * rank
    if picked:
        pick = pick_ref[0] > 0
    parts = []
    for copy, c in zip(copies[used:], columns):
        copy.wait()
        factors = ups[: last + rank, c]
        if picked:
            factors = jnp.concatenate(
                [ups[:last, c], jnp.where(pick, ups[last : last + rank, c], ups[last + rank :, c])],
                axis=0,
            )
        parts.append(
            lax.dot_general(cot[:, c], factors, NT, preferred_element_type=jnp.float32)
        )
    for copy in copies[used + len(columns) :]:
        copy.wait()
    change = total_of(parts) * (mine[...] + other[...])
    for kind in range(2):
        sums = jnp.sum(change * masks[:, kind : kind + 1], axis=0, keepdims=True)
        for at, slot in enumerate(slots):
            row = kind * pad + slot
            added = jnp.sum(sums[:, at * rank : (at + 1) * rank], axis=1, keepdims=True)
            out_ref[row : row + 1, :] += jnp.broadcast_to(added, (1, LANES))


def score(table, slots, pick, masks, mine, other, cot, ups, start, microseconds):
    rank, width = ups[0].shape
    tile = tile_of(width, 1280)
    operands = (pick, masks, mine, other, cot, table, *ups)
    vmem = pl.BlockSpec(memory_space=pl.ANY)
    return pl.pallas_call(
        functools.partial(
            score_kernel, tuple(slots), len(ups) > len(slots), table.shape[0] // 2, start, tile
        ),
        in_specs=[pl.BlockSpec(memory_space=pltpu.SMEM)] + [vmem] * (len(operands) - 1),
        out_shape=jax.ShapeDtypeStruct(table.shape, jnp.float32),
        scratch_shapes=[
            pltpu.VMEM(masks.shape, jnp.float32),
            pltpu.VMEM(mine.shape, jnp.float32),
            pltpu.VMEM(mine.shape, jnp.float32),
            pltpu.VMEM((cot.shape[0], width), cot.dtype),
            pltpu.VMEM((rank * len(ups), width), cot.dtype),
            pltpu.SemaphoreType.DMA((len(ups) + width // tile + 4,)),
        ],
        compiler_params=params(),
        cost_estimate=cost(microseconds),
        name="score",
    )(*operands)


def finish_kernel(columns, mine_ref, other_ref, place_ref, counts_ref, own_ref, rest_ref):
    pad = place_ref.shape[0]
    total = mine_ref[...] + other_ref[...]
    own = jnp.sum(total[:pad] * place_ref[...], axis=0, keepdims=True) / counts_ref[0:1, :]
    rest = jnp.sum(total[pad:] * place_ref[...], axis=0, keepdims=True) / counts_ref[1:2, :]
    own_ref[...] = own[:, :columns]
    rest_ref[...] = rest[:, :columns]


def finish(mine, other, place, counts, columns):
    shape = jax.ShapeDtypeStruct((1, columns), jnp.float32)
    return pl.pallas_call(
        functools.partial(finish_kernel, columns),
        out_shape=(shape, shape),
        compiler_params=params(),
        cost_estimate=cost(1.0),
        name="finish",
    )(mine, other, place, counts)


def rest_of_sum(block):
    parts = lax.axis_size("tensor")
    if parts == 2:
        return lax.ppermute(block, "tensor", [(0, 1), (1, 0)])
    return lax.psum(block, "tensor") - block


def send(block, target, corners=None):
    count = lax.axis_size("skill")
    pairs = [(s, target(s) % count) for s in range(count) if corners is None or s % 4 in corners]
    return lax.ppermute(block, "skill", pairs)


def across(s):
    return s ^ 1


def down(s):
    return s ^ 2


def next_quad(s):
    return s - 4 if s & 2 else s + 4


QUAD_OFFSETS = ((0, 1, 2, -2, -1), (0, -1, 2, -2, 1), (0, 1, -2, 2, -1), (0, -1, -2, 2, 1))


def spread_across(block, ends):
    by_x = send(block, across)
    by_y = send(block, down)
    by_z = send(by_y, next_quad)
    last = send(jnp.where(ends, by_y, by_z), across)
    return [block, by_x, by_y, by_z, (last,)]


def spread_down(block):
    by_x = send(block, across)
    by_y = send(block, down)
    by_z = send(by_y, next_quad)
    diagonal = send(by_x, down)
    passed_on = send(diagonal, next_quad, (0, 3))
    return [block, by_x, by_y, by_z, (passed_on, diagonal)]


def spread_ring(block, reach):
    slots, ahead, behind = [block], block, block
    for _ in range(reach):
        ahead = send(ahead, lambda s: s - 1)
        behind = send(behind, lambda s: s + 1)
        slots += [ahead, behind]
    return slots


def on_device(
    stored_inputs,
    stored_output_gradient,
    training_token_index,
    validation_inputs,
    validation_output_gradient,
    validation_row_skill,
    adapter_down_init,
):
    reach = lax.axis_size("skill") // 8
    columns = 2 * reach + 1
    pad = -(-columns // 8) * 8
    my_skill = lax.axis_index("skill")
    corner = my_skill % 4
    ends = (corner == 0) | (corner == 3)
    pick = ends.astype(jnp.int32)[None]
    quads = reach == 2
    factor = adapter_down_init[0].T
    valid_act = validation_inputs[0]
    valid_cot = validation_output_gradient[0]
    cot = stored_output_gradient[0]
    train, hidden = cot.shape

    own_mask = (validation_row_skill == my_skill).astype(jnp.float32)
    masks = jnp.concatenate([own_mask, 1.0 - own_mask], axis=0)
    row_counts = jnp.broadcast_to(
        jnp.maximum(jnp.sum(masks, axis=1, keepdims=True), 1.0), (2, LANES)
    )
    masks = masks.T
    if quads:
        offsets = jnp.array(QUAD_OFFSETS, jnp.int32)[corner]
    else:
        offsets = jnp.array([0] + [o for d in range(reach) for o in (d + 1, -d - 1)], jnp.int32)
    offsets = jnp.pad(offsets, (0, pad - columns), constant_values=columns)
    lane = jnp.arange(LANES, dtype=jnp.int32) - reach
    place = (offsets[:, None] == lane[None, :]).astype(jnp.float32)
    counts = jnp.sum(
        (training_token_index[0][:, None] == jnp.arange(train)[None, :]).astype(jnp.float32),
        axis=0, keepdims=True,
    )

    downs = spread_across(factor, ends) if quads else spread_ring(factor, reach)
    proj = project(stored_inputs[0], [factor], 2.5).T
    proj_rest = rest_of_sum(proj)
    table = jnp.zeros((2 * pad, LANES), jnp.float32)

    if quads:
        half = hidden // 2
        up = up_factor(proj, proj_rest, counts, cot, 0, half)
        first = spread_across(up, ends)
        near = project(valid_act, downs[:3], 4.0, up)
        near_rest = rest_of_sum(near)
        up = up_factor(proj, proj_rest, counts, cot, half, half, near)
        second = spread_down(up)
        gather = functools.partial(score, pick=pick, masks=masks, cot=valid_cot)
        table = gather(table, (0, 1, 2), mine=near, other=near_rest, ups=first[:3], start=0, microseconds=3.0)
        table = gather(table, (0, 1, 2), mine=near, other=near_rest, ups=second[:3], start=half, microseconds=3.0)
        far = project(valid_act, [downs[3], downs[4][0]], 4.0, table)
        far_rest = rest_of_sum(far)
        table = gather(table, (3, 4), mine=far, other=far_rest, ups=[first[3], *first[4]], start=0, microseconds=3.0)
        table = gather(table, (3, 4), mine=far, other=far_rest, ups=[second[3], *second[4]], start=half, microseconds=3.0)
    else:
        ups = spread_ring(up_factor(proj, proj_rest, counts, cot, 0, hidden), reach)
        for at in range(0, columns, 3):
            slots = range(at, min(at + 3, columns))
            mine = project(valid_act, [downs[s] for s in slots], 2.0)
            table = score(
                table, slots, pick, masks, mine, rest_of_sum(mine), valid_cot,
                [ups[s] for s in slots], 0, 2.0,
            )

    return finish(table, rest_of_sum(table), place, row_counts, columns)


def solution(mesh):
    in_specs = (
        P("skill", None, "tensor"),
        P("skill", None, "tensor"),
        P("skill", None),
        P("skill", None, "tensor"),
        P("skill", None, "tensor"),
        P("skill", None),
        P("skill", "tensor", None),
    )
    out_specs = (P("skill", None), P("skill", None))
    return jax.shard_map(
        on_device, mesh=mesh, in_specs=in_specs, out_specs=out_specs, check_vma=False
    )
```

```python
import functools

import jax
import jax.numpy as jnp
from jax import lax
from jax.experimental import pallas as pl
from jax.experimental.pallas import tpu as pltpu
from jax.sharding import PartitionSpec as P

VMEM_LIMIT = 56 * 1024 * 1024
LANES = 128
BYTES_PER_US = 3_000_000
COST = 1.0
NT = (((1,), (1,)), ((), ()))


def tile_of(width, most):
    fits = [size for size in range(LANES, min(width, most) + 1, LANES) if width % size == 0]
    return fits[-1] if fits else width


def params():
    return pltpu.CompilerParams(vmem_limit_bytes=VMEM_LIMIT)


def cost(microseconds):
    return pl.CostEstimate(
        flops=0, bytes_accessed=int(microseconds * BYTES_PER_US), transcendentals=0
    )


def total_of(parts):
    return functools.reduce(lambda a, b: a + b, parts)


def fetch(pairs, sems):
    copies = [pltpu.make_async_copy(a, b, sems.at[at]) for at, (a, b) in enumerate(pairs)]
    for copy in copies:
        copy.start()
    return copies


def call(kernel, name, operands, out_shape, scratch, copies, microseconds):
    return pl.pallas_call(
        kernel,
        in_specs=[pl.BlockSpec(memory_space=pl.ANY)] * len(operands),
        out_shape=out_shape,
        scratch_shapes=list(scratch) + [pltpu.SemaphoreType.DMA((copies,))],
        compiler_params=params(),
        cost_estimate=cost(microseconds),
        name=name,
    )(*operands)


def project_kernel(count, tile, flip, *refs):
    rows_ref, factor_refs = refs[0], refs[1 : 1 + count]
    out_ref, rows, factors, sems = refs[-4:]
    rank = factor_refs[0].shape[0]
    columns = [slice(at, at + tile) for at in range(0, rows_ref.shape[1], tile)]
    copies = fetch(
        [(f, factors.at[at * rank : (at + 1) * rank]) for at, f in enumerate(factor_refs)]
        + [(rows_ref.at[:, c], rows.at[:, c]) for c in columns],
        sems,
    )
    for copy in copies[:count]:
        copy.wait()
    for at, c in enumerate(columns):
        copies[count + at].wait()
        ends = (factors[:, c], rows[:, c]) if flip else (rows[:, c], factors[:, c])
        part = lax.dot_general(*ends, NT, preferred_element_type=jnp.float32)
        if at == 0:
            out_ref[...] = part
        else:
            out_ref[...] += part


def project(rows, factors, microseconds, *after, flip=False):
    n, width = rows.shape
    count, rank = len(factors), factors[0].shape[0]
    tile = tile_of(width, 1024)
    return call(
        functools.partial(project_kernel, count, tile, flip),
        "project",
        (rows, *factors, *after),
        jax.ShapeDtypeStruct((rank * count, n) if flip else (n, rank * count), jnp.float32),
        [pltpu.VMEM((n, width), rows.dtype), pltpu.VMEM((rank * count, width), rows.dtype)],
        count + width // tile,
        microseconds,
    )


def up_kernel(scale, start, width, tile, mine_ref, other_ref, counts_ref, cot_ref, *refs):
    out_ref, mine, other, counts, cot, sems = refs[-6:]
    columns = [slice(at, at + tile) for at in range(0, width, tile)]
    copies = fetch(
        [(mine_ref, mine), (other_ref, other), (counts_ref, counts)]
        + [(cot_ref.at[:, start + c.start : start + c.stop], cot.at[:, c]) for c in columns],
        sems,
    )
    for copy in copies[:3]:
        copy.wait()
    proj = (mine[...] + other[...]).astype(jnp.bfloat16).astype(jnp.float32)
    weighted = proj * counts[...]
    high = weighted.astype(jnp.bfloat16)
    low = (weighted - high.astype(jnp.float32)).astype(jnp.bfloat16)
    both = jnp.concatenate([high, low], axis=0)
    rank = proj.shape[0]
    for copy, c in zip(copies[3:], columns):
        copy.wait()
        product = jnp.dot(both, cot[:, c], preferred_element_type=jnp.float32)
        out_ref[:, c] = ((product[:rank] + product[rank:]) * scale).astype(jnp.bfloat16)


def up_factor(mine, other, counts, cot, start, width, *after):
    rank, train = mine.shape
    tile = tile_of(width, 1280)
    return call(
        functools.partial(up_kernel, -1.0 / train, start, width, tile),
        "up_factor",
        (mine, other, counts, cot, *after),
        jax.ShapeDtypeStruct((rank, width), jnp.bfloat16),
        [
            pltpu.VMEM(mine.shape, jnp.float32),
            pltpu.VMEM(mine.shape, jnp.float32),
            pltpu.VMEM(counts.shape, jnp.float32),
            pltpu.VMEM((train, width), cot.dtype),
        ],
        3 + width // tile,
        COST,
    )


def score_kernel(slots, picked, pad, start, tile, *refs):
    pick_ref, masks_ref, mine_ref, other_ref, cot_ref, table_ref = refs[:6]
    up_refs = refs[6:-7]
    out_ref, masks, mine, other, cot, ups, sems = refs[-7:]
    rank, width = up_refs[0].shape
    used = len(up_refs)
    columns = [slice(at, at + tile) for at in range(0, width, tile)]
    copies = fetch(
        [(u, ups.at[at * rank : (at + 1) * rank]) for at, u in enumerate(up_refs)]
        + [(cot_ref.at[:, start + c.start : start + c.stop], cot.at[:, c]) for c in columns]
        + [(masks_ref, masks), (mine_ref, mine), (other_ref, other), (table_ref, out_ref)],
        sems,
    )
    for copy in copies[:used]:
        copy.wait()
    last = (len(slots) - 1) * rank
    if picked:
        pick = pick_ref[0] > 0
    parts = []
    for copy, c in zip(copies[used:], columns):
        copy.wait()
        factors = ups[: last + rank, c]
        if picked:
            factors = jnp.concatenate(
                [ups[:last, c], jnp.where(pick, ups[last : last + rank, c], ups[last + rank :, c])],
                axis=0,
            )
        parts.append(
            lax.dot_general(cot[:, c], factors, NT, preferred_element_type=jnp.float32)
        )
    for copy in copies[used + len(columns) :]:
        copy.wait()
    change = total_of(parts) * (mine[...] + other[...])
    for kind in range(2):
        sums = jnp.sum(change * masks[:, kind : kind + 1], axis=0, keepdims=True)
        for at, slot in enumerate(slots):
            row = kind * pad + slot
            added = jnp.sum(sums[:, at * rank : (at + 1) * rank], axis=1, keepdims=True)
            out_ref[row : row + 1, :] += jnp.broadcast_to(added, (1, LANES))


def score(table, slots, pick, masks, mine, other, cot, ups, start, microseconds):
    rank, width = ups[0].shape
    tile = tile_of(width, 1280)
    operands = (pick, masks, mine, other, cot, table, *ups)
    vmem = pl.BlockSpec(memory_space=pl.ANY)
    return pl.pallas_call(
        functools.partial(
            score_kernel, tuple(slots), len(ups) > len(slots), table.shape[0] // 2, start, tile
        ),
        in_specs=[pl.BlockSpec(memory_space=pltpu.SMEM)] + [vmem] * (len(operands) - 1),
        out_shape=jax.ShapeDtypeStruct(table.shape, jnp.float32),
        scratch_shapes=[
            pltpu.VMEM(masks.shape, jnp.float32),
            pltpu.VMEM(mine.shape, jnp.float32),
            pltpu.VMEM(mine.shape, jnp.float32),
            pltpu.VMEM((cot.shape[0], width), cot.dtype),
            pltpu.VMEM((rank * len(ups), width), cot.dtype),
            pltpu.SemaphoreType.DMA((len(ups) + width // tile + 4,)),
        ],
        compiler_params=params(),
        cost_estimate=cost(microseconds),
        name="score",
    )(*operands)


def finish_kernel(columns, mine_ref, other_ref, place_ref, counts_ref, own_ref, rest_ref):
    pad = place_ref.shape[0]
    total = mine_ref[...] + other_ref[...]
    own = jnp.sum(total[:pad] * place_ref[...], axis=0, keepdims=True) / counts_ref[0:1, :]
    rest = jnp.sum(total[pad:] * place_ref[...], axis=0, keepdims=True) / counts_ref[1:2, :]
    own_ref[...] = own[:, :columns]
    rest_ref[...] = rest[:, :columns]


def finish(mine, other, place, counts, columns):
    shape = jax.ShapeDtypeStruct((1, columns), jnp.float32)
    return pl.pallas_call(
        functools.partial(finish_kernel, columns),
        out_shape=(shape, shape),
        compiler_params=params(),
        cost_estimate=cost(COST),
        name="finish",
    )(mine, other, place, counts)


def rest_of_sum(block):
    parts = lax.axis_size("tensor")
    if parts == 2:
        return lax.ppermute(block, "tensor", [(0, 1), (1, 0)])
    return lax.psum(block, "tensor") - block


def send(block, target, corners=None):
    count = lax.axis_size("skill")
    pairs = [(s, target(s) % count) for s in range(count) if corners is None or s % 4 in corners]
    return lax.ppermute(block, "skill", pairs)


def across(s):
    return s ^ 1


def down(s):
    return s ^ 2


def next_quad(s):
    return s - 4 if s & 2 else s + 4


QUAD_OFFSETS = ((0, 1, 2, -2, -1), (0, -1, 2, -2, 1), (0, 1, -2, 2, -1), (0, -1, -2, 2, 1))


def after(block, *others):
    return lax.optimization_barrier((block, *others))[0]


def spread_ring(block, reach):
    slots, ahead, behind = [block], block, block
    for _ in range(reach):
        ahead = send(ahead, lambda s: s - 1)
        behind = send(behind, lambda s: s + 1)
        slots += [ahead, behind]
    return slots


def on_device(
    stored_inputs,
    stored_output_gradient,
    training_token_index,
    validation_inputs,
    validation_output_gradient,
    validation_row_skill,
    adapter_down_init,
):
    reach = lax.axis_size("skill") // 8
    columns = 2 * reach + 1
    pad = -(-columns // 8) * 8
    my_skill = lax.axis_index("skill")
    corner = my_skill % 4
    ends = (corner == 0) | (corner == 3)
    pick = ends.astype(jnp.int32)[None]
    quads = reach == 2
    factor = adapter_down_init[0].T
    valid_act = validation_inputs[0]
    valid_cot = validation_output_gradient[0]
    cot = stored_output_gradient[0]
    train, hidden = cot.shape

    own_mask = (validation_row_skill == my_skill).astype(jnp.float32)
    masks = jnp.concatenate([own_mask, 1.0 - own_mask], axis=0)
    row_counts = jnp.broadcast_to(
        jnp.maximum(jnp.sum(masks, axis=1, keepdims=True), 1.0), (2, LANES)
    )
    masks = masks.T
    if quads:
        offsets = jnp.array(QUAD_OFFSETS, jnp.int32)[corner]
    else:
        offsets = jnp.array([0] + [o for d in range(reach) for o in (d + 1, -d - 1)], jnp.int32)
    offsets = jnp.pad(offsets, (0, pad - columns), constant_values=columns)
    lane = jnp.arange(LANES, dtype=jnp.int32) - reach
    place = (offsets[:, None] == lane[None, :]).astype(jnp.float32)
    counts = jnp.sum(
        (training_token_index[0][:, None] == jnp.arange(train)[None, :]).astype(jnp.float32),
        axis=0, keepdims=True,
    )

    table = jnp.zeros((2 * pad, LANES), jnp.float32)

    if quads:
        half = hidden // 2
        gather = functools.partial(score, pick=pick, masks=masks, cot=valid_cot)
        down_x = send(factor, across)
        down_y = send(factor, down)
        proj = project(stored_inputs[0], [factor], COST, flip=True)
        proj_rest = rest_of_sum(proj)
        up_a = up_factor(proj, proj_rest, counts, cot, 0, half)
        a_x, a_y = send(up_a, across), send(up_a, down)
        down_z = send(after(down_y, up_a), next_quad)
        near = project(valid_act, [factor, down_x, down_y], COST, up_a)
        near_rest = rest_of_sum(near)
        up_b = up_factor(proj, proj_rest, counts, cot, half, half, near)
        b_x, b_y = send(up_b, across), send(up_b, down)
        a_z = send(after(a_y, up_b), next_quad)
        table = gather(
            table, (0, 1, 2), mine=near, other=near_rest, ups=[up_a, a_x, a_y],
            start=0, microseconds=COST,
        )
        down_w = send(jnp.where(ends, down_y, after(down_z, up_b)), across)
        b_z = send(after(b_y, table), next_quad)
        b_d = send(after(b_x, table), down)
        table = gather(
            table, (0, 1, 2), mine=near, other=near_rest, ups=[up_b, b_x, b_y],
            start=half, microseconds=COST,
        )
        a_w = send(jnp.where(ends, a_y, after(a_z, table)), across)
        far = project(valid_act, [down_z, down_w], COST, table)
        far_rest = rest_of_sum(far)
        b_w = send(after(b_d, far), next_quad, (0, 3))
        table = gather(
            table, (3, 4), mine=far, other=far_rest, ups=[a_z, a_w],
            start=0, microseconds=COST,
        )
        table = gather(
            table, (3, 4), mine=far, other=far_rest, ups=[b_z, b_w, b_d],
            start=half, microseconds=COST,
        )
    else:
        downs = spread_ring(factor, reach)
        proj = project(stored_inputs[0], [factor], COST, flip=True)
        ups = spread_ring(
            up_factor(proj, rest_of_sum(proj), counts, cot, 0, hidden), reach
        )
        for at in range(0, columns, 3):
            slots = range(at, min(at + 3, columns))
            mine = project(valid_act, [downs[s] for s in slots], COST)
            table = score(
                table, slots, pick, masks, mine, rest_of_sum(mine), valid_cot,
                [ups[s] for s in slots], 0, COST,
            )

    return finish(table, rest_of_sum(table), place, row_counts, columns)


def solution(mesh):
    in_specs = (
        P("skill", None, "tensor"),
        P("skill", None, "tensor"),
        P("skill", None),
        P("skill", None, "tensor"),
        P("skill", None, "tensor"),
        P("skill", None),
        P("skill", "tensor", None),
    )
    out_specs = (P("skill", None), P("skill", None))
    return jax.shard_map(
        on_device, mesh=mesh, in_specs=in_specs, out_specs=out_specs, check_vma=False
    )
```

```python
import functools

import jax
import jax.numpy as jnp
from jax import lax
from jax.experimental import pallas as pl
from jax.experimental.pallas import tpu as pltpu
from jax.sharding import PartitionSpec as P

VMEM_LIMIT = 64 * 1024 * 1024
LANES = 128
NT = (((1,), (1,)), ((), ()))
PIECE_ROWS = 128
COST_BYTES = 3_000_000
F32 = jnp.float32


def tile_of(width, most):
    fits = [size for size in range(LANES, min(width, most) + 1, LANES) if width % size == 0]
    return fits[-1] if fits else width


def columns_of(width, most):
    tile = tile_of(width, most)
    return [slice(at, at + tile) for at in range(0, width, tile)]


class Fetches:
    def __init__(self, sems):
        self.sems, self.used = sems, 0

    def start(self, source, target):
        rows = target.shape[0]
        step = PIECE_ROWS if rows % PIECE_ROWS == 0 else rows
        copies = []
        for at in range(0, rows, step):
            part = pl.ds(at, step)
            copies.append(
                pltpu.make_async_copy(source.at[part], target.at[part], self.sems.at[self.used])
            )
            copies[-1].start()
            self.used += 1
        return copies


def wait(copies):
    for copy in copies:
        copy.wait()


def call(kernel, name, operands, out, scratch, copies, scalars=0):
    hbm = pl.BlockSpec(memory_space=pltpu.HBM)
    return pl.pallas_call(
        kernel,
        in_specs=[pl.BlockSpec(memory_space=pltpu.SMEM)] * scalars
        + [hbm] * (len(operands) - scalars),
        out_specs=hbm,
        out_shape=out,
        scratch_shapes=[pltpu.VMEM(out.shape, out.dtype), *scratch]
        + [pltpu.SemaphoreType.DMA((copies,))],
        compiler_params=pltpu.CompilerParams(vmem_limit_bytes=VMEM_LIMIT),
        cost_estimate=pl.CostEstimate(flops=0, bytes_accessed=COST_BYTES, transcendentals=0),
        name=name,
    )(*operands)


def project_kernel(count, flip, *refs):
    rows_ref, factor_refs = refs[0], refs[1 : 1 + count]
    out_ref, out, rows, factors, sems = refs[-5:]
    rank, width = factor_refs[0].shape
    columns = columns_of(width, 1024)
    fetches = Fetches(sems)
    factor_copies = [
        fetches.start(f, factors.at[at * rank : (at + 1) * rank])
        for at, f in enumerate(factor_refs)
    ]
    row_copies = [fetches.start(rows_ref.at[:, c], rows.at[:, c]) for c in columns]
    for copies in factor_copies:
        wait(copies)
    total = None
    for copies, c in zip(row_copies, columns):
        wait(copies)
        ends = (factors[:, c], rows[:, c]) if flip else (rows[:, c], factors[:, c])
        part = lax.dot_general(*ends, NT, preferred_element_type=F32)
        total = part if total is None else total + part
    out[...] = total
    pltpu.sync_copy(out, out_ref)


def project(rows, factors, *after, flip=False):
    n, width = rows.shape
    count, rank = len(factors), factors[0].shape[0]
    return call(
        functools.partial(project_kernel, count, flip),
        "project",
        (rows, *factors, *after),
        jax.ShapeDtypeStruct((rank * count, n) if flip else (n, rank * count), F32),
        [pltpu.VMEM((n, width), rows.dtype), pltpu.VMEM((rank * count, width), rows.dtype)],
        count + len(columns_of(width, 1024)) * max(1, n // PIECE_ROWS),
    )


def up_kernel(scale, start, width, *refs):
    mine_ref, other_ref, counts_ref, cot_ref = refs[:4]
    out_ref, out, mine, other, counts, cot, sems = refs[-7:]
    columns = columns_of(width, 1280)
    fetches = Fetches(sems)
    small = [
        fetches.start(a, b)
        for a, b in ((mine_ref, mine), (other_ref, other), (counts_ref, counts))
    ]
    large = [
        fetches.start(cot_ref.at[:, start + c.start : start + c.stop], cot.at[:, c])
        for c in columns
    ]
    for copies in small:
        wait(copies)
    proj = (mine[...] + other[...]).astype(jnp.bfloat16).astype(F32)
    weighted = proj * counts[...]
    high = weighted.astype(jnp.bfloat16)
    low = (weighted - high.astype(F32)).astype(jnp.bfloat16)
    both = jnp.concatenate([high, low], axis=0)
    rank = proj.shape[0]
    for copies, c in zip(large, columns):
        wait(copies)
        product = jnp.dot(both, cot[:, c], preferred_element_type=F32)
        out[:, c] = ((product[:rank] + product[rank:]) * scale).astype(jnp.bfloat16)
    pltpu.sync_copy(out, out_ref)


def up_factor(mine, other, counts, cot, start, width, *after):
    rank, train = mine.shape
    return call(
        functools.partial(up_kernel, -1.0 / train, start, width),
        "up_factor",
        (mine, other, counts, cot, *after),
        jax.ShapeDtypeStruct((rank, width), jnp.bfloat16),
        [
            pltpu.VMEM(mine.shape, F32),
            pltpu.VMEM(mine.shape, F32),
            pltpu.VMEM(counts.shape, F32),
            pltpu.VMEM((train, width), cot.dtype),
        ],
        3 + len(columns_of(width, 1280)) * max(1, train // PIECE_ROWS),
    )


def score_kernel(slots, picked, pad, start, *refs):
    pick_ref, masks_ref, mine_ref, other_ref, cot_ref, table_ref = refs[:6]
    up_refs = refs[6:-8]
    out_ref, out, masks, mine, other, cot, ups, sems = refs[-8:]
    rank, width = up_refs[0].shape
    columns = columns_of(width, 1280)
    fetches = Fetches(sems)
    up_copies = [
        fetches.start(u, ups.at[at * rank : (at + 1) * rank]) for at, u in enumerate(up_refs)
    ]
    cot_copies = [
        fetches.start(cot_ref.at[:, start + c.start : start + c.stop], cot.at[:, c])
        for c in columns
    ]
    small = [
        fetches.start(a, b)
        for a, b in ((masks_ref, masks), (mine_ref, mine), (other_ref, other), (table_ref, out))
    ]
    for copies in up_copies:
        wait(copies)
    last = (len(slots) - 1) * rank
    total = None
    for copies, c in zip(cot_copies, columns):
        wait(copies)
        factors = ups[: last + rank, c]
        if picked:
            chosen = jnp.where(
                pick_ref[0] > 0, ups[last : last + rank, c], ups[last + rank :, c]
            )
            factors = jnp.concatenate([ups[:last, c], chosen], axis=0)
        part = lax.dot_general(cot[:, c], factors, NT, preferred_element_type=F32)
        total = part if total is None else total + part
    for copies in small:
        wait(copies)
    change = total * (mine[...] + other[...])
    sums = jnp.dot(
        masks[...], change, preferred_element_type=F32, precision=lax.Precision.HIGHEST
    )
    for at, slot in enumerate(slots):
        added = jnp.sum(sums[:, at * rank : (at + 1) * rank], axis=1, keepdims=True)
        for kind in range(2):
            row = kind * pad + slot
            out[row : row + 1, :] += jnp.broadcast_to(added[kind : kind + 1], (1, LANES))
    pltpu.sync_copy(out, out_ref)


def score(table, slots, pick, masks, mine, other, cot, ups, start):
    rank, width = ups[0].shape
    rows = cot.shape[0]
    return call(
        functools.partial(
            score_kernel, tuple(slots), len(ups) > len(slots), table.shape[0] // 2, start
        ),
        "score",
        (pick, masks, mine, other, cot, table, *ups),
        jax.ShapeDtypeStruct(table.shape, F32),
        [
            pltpu.VMEM(masks.shape, F32),
            pltpu.VMEM(mine.shape, F32),
            pltpu.VMEM(mine.shape, F32),
            pltpu.VMEM((rows, width), cot.dtype),
            pltpu.VMEM((rank * len(ups), width), cot.dtype),
        ],
        len(ups) + 2 + (2 + len(columns_of(width, 1280))) * max(1, rows // PIECE_ROWS),
        scalars=1,
    )


def finish_kernel(offsets, reach, corner_ref, mine_ref, other_ref, masks_ref, own_ref, rest_ref):
    pad = mine_ref.shape[0] // 2
    total = mine_ref[...] + other_ref[...]
    counts = jnp.maximum(jnp.sum(masks_ref[...], axis=1, keepdims=True), 1.0)
    lane = lax.broadcasted_iota(jnp.int32, (1, LANES), 1)
    corner = corner_ref[0]
    sums = [jnp.zeros((1, LANES), F32)] * 2
    for slot in range(len(offsets[0])):
        place = offsets[0][slot] + reach
        for other in range(1, len(offsets)):
            place = jnp.where(corner == other, offsets[other][slot] + reach, place)
        for kind in range(2):
            row = kind * pad + slot
            sums[kind] = jnp.where(lane == place, total[row : row + 1, :], sums[kind])
    for kind, ref in enumerate((own_ref, rest_ref)):
        ref[...] = (sums[kind] / counts[kind : kind + 1])[:, : ref.shape[1]]


def finish(mine, other, masks, corner, offsets, reach):
    shape = jax.ShapeDtypeStruct((1, 2 * reach + 1), F32)
    vmem = pl.BlockSpec(memory_space=pltpu.VMEM)
    return pl.pallas_call(
        functools.partial(finish_kernel, offsets, reach),
        in_specs=[pl.BlockSpec(memory_space=pltpu.SMEM), vmem, vmem, vmem],
        out_shape=(shape, shape),
        compiler_params=pltpu.CompilerParams(vmem_limit_bytes=VMEM_LIMIT),
        cost_estimate=pl.CostEstimate(flops=0, bytes_accessed=COST_BYTES, transcendentals=0),
        name="finish",
    )(corner, mine, other, masks)


def rest_of_sum(block):
    parts = lax.axis_size("tensor")
    if parts == 2:
        return lax.ppermute(block, "tensor", [(0, 1), (1, 0)])
    return lax.psum(block, "tensor") - block


def send(block, target, corners=None):
    count = lax.axis_size("skill")
    pairs = [(s, target(s) % count) for s in range(count) if corners is None or s % 4 in corners]
    return lax.ppermute(block, "skill", pairs)


def across(s):
    return s ^ 1


def down(s):
    return s ^ 2


def next_quad(s):
    return s - 4 if s & 2 else s + 4


QUAD_OFFSETS = ((0, 1, 2, -2, -1), (0, -1, 2, -2, 1), (0, 1, -2, 2, -1), (0, -1, -2, 2, 1))


def after(block, *others):
    return lax.optimization_barrier((block, *others))[0]


def spread_ring(block, reach):
    slots, ahead, behind = [block], block, block
    for _ in range(reach):
        ahead = send(ahead, lambda s: s - 1)
        behind = send(behind, lambda s: s + 1)
        slots += [ahead, behind]
    return slots


def on_device(
    stored_inputs,
    stored_output_gradient,
    training_token_index,
    validation_inputs,
    validation_output_gradient,
    validation_row_skill,
    adapter_down_init,
):
    reach = lax.axis_size("skill") // 8
    columns = 2 * reach + 1
    pad = -(-columns // 8) * 8
    my_skill = lax.axis_index("skill")
    corner = my_skill & 3
    ends = (corner == 0) | (corner == 3)
    pick = ends.astype(jnp.int32)[None]
    factor = adapter_down_init[0].T
    valid_act = validation_inputs[0]
    valid_cot = validation_output_gradient[0]
    cot = stored_output_gradient[0]
    train, hidden = cot.shape

    own = validation_row_skill == my_skill
    kind = lax.broadcasted_iota(jnp.int32, (8, own.shape[1]), 0)
    masks = jnp.where(kind < 2, (own == (kind == 0)).astype(F32), 0.0)
    counts = jnp.sum(
        (training_token_index[0][:, None] == jnp.arange(train)[None, :]).astype(F32),
        axis=0, keepdims=True,
    )
    table = jnp.zeros((2 * pad, LANES), F32)
    gather = functools.partial(score, pick=pick, masks=masks, cot=valid_cot)

    if reach == 2:
        half = hidden // 2
        down_x = send(factor, across)
        down_y = send(factor, down)
        proj = project(stored_inputs[0], [factor], flip=True)
        proj_rest = rest_of_sum(proj)
        up_a = up_factor(proj, proj_rest, counts, cot, 0, half)
        a_x, a_y = send(up_a, across), send(up_a, down)
        down_z = send(after(down_y, up_a), next_quad)
        near = project(valid_act, [factor, down_x, down_y], up_a)
        near_rest = rest_of_sum(near)
        up_b = up_factor(proj, proj_rest, counts, cot, half, half, near)
        b_x, b_y = send(up_b, across), send(up_b, down)
        a_z = send(after(a_y, up_b), next_quad)
        near_slots = dict(slots=(0, 1, 2), mine=near, other=near_rest)
        table = gather(table, ups=[up_a, a_x, a_y], start=0, **near_slots)
        down_w = send(jnp.where(ends, down_y, after(down_z, up_b)), across)
        b_z = send(after(b_y, table), next_quad)
        b_d = send(after(b_x, table), down)
        table = gather(table, ups=[up_b, b_x, b_y], start=half, **near_slots)
        a_w = send(jnp.where(ends, a_y, after(a_z, table)), across)
        far = project(valid_act, [down_z, down_w], table)
        far_rest = rest_of_sum(far)
        b_w = send(after(b_d, far), next_quad, (0, 3))
        far_slots = dict(slots=(3, 4), mine=far, other=far_rest)
        table = gather(table, ups=[a_z, a_w], start=0, **far_slots)
        table = gather(table, ups=[b_z, b_w, b_d], start=half, **far_slots)
        offsets = QUAD_OFFSETS
    else:
        downs = spread_ring(factor, reach)
        proj = project(stored_inputs[0], [factor], flip=True)
        up = up_factor(proj, rest_of_sum(proj), counts, cot, 0, hidden)
        ups = spread_ring(up, reach)
        for at in range(0, columns, 3):
            slots = range(at, min(at + 3, columns))
            mine = project(valid_act, [downs[s] for s in slots])
            table = gather(
                table, slots=slots, mine=mine, other=rest_of_sum(mine),
                ups=[ups[s] for s in slots], start=0,
            )
        offsets = ((0, *(o for d in range(reach) for o in (d + 1, -d - 1))),)

    return finish(table, rest_of_sum(table), masks, corner[None], offsets, reach)


def solution(mesh):
    in_specs = (
        P("skill", None, "tensor"),
        P("skill", None, "tensor"),
        P("skill", None),
        P("skill", None, "tensor"),
        P("skill", None, "tensor"),
        P("skill", None),
        P("skill", "tensor", None),
    )
    out_specs = (P("skill", None), P("skill", None))
    return jax.shard_map(
        on_device, mesh=mesh, in_specs=in_specs, out_specs=out_specs, check_vma=False
    )
```

```python
import functools

import jax
import jax.numpy as jnp
from jax import lax
from jax.experimental import pallas as pl
from jax.experimental.pallas import tpu as pltpu
from jax.sharding import PartitionSpec as P

VMEM_LIMIT = 16 * 1024 * 1024
LANES = 128
NT = (((1,), (1,)), ((), ()))
COST_BYTES = 3_000_000
F32 = jnp.float32


def tile_of(width, most):
    fits = [size for size in range(LANES, min(width, most) + 1, LANES) if width % size == 0]
    return fits[-1] if fits else width


def columns_of(width, most):
    tile = tile_of(width, most)
    return [slice(at, at + tile) for at in range(0, width, tile)]


def total_of(parts):
    return functools.reduce(lambda a, b: a + b, parts)


def call(kernel, name, operands, out, scalars=0, tokens=0):
    vmem = pl.BlockSpec(memory_space=pltpu.VMEM)
    return pl.pallas_call(
        kernel,
        in_specs=[pl.BlockSpec(memory_space=pltpu.SMEM)] * scalars
        + [vmem] * (len(operands) - scalars - tokens)
        + [pl.BlockSpec(memory_space=pl.ANY)] * tokens,
        out_specs=vmem,
        out_shape=out,
        compiler_params=pltpu.CompilerParams(vmem_limit_bytes=VMEM_LIMIT),
        cost_estimate=pl.CostEstimate(flops=0, bytes_accessed=COST_BYTES, transcendentals=0),
        name=name,
    )(*operands)


def project_kernel(count, flip, *refs):
    rows_ref, factor_refs, out_ref = refs[0], refs[1 : 1 + count], refs[-1]
    parts = []
    for c in columns_of(rows_ref.shape[1], 2048):
        rows = rows_ref[:, c]
        factors = jnp.concatenate([f[:, c] for f in factor_refs], axis=0)
        ends = (factors, rows) if flip else (rows, factors)
        parts.append(lax.dot_general(*ends, NT, preferred_element_type=F32))
    out_ref[...] = total_of(parts)


def project(rows, factors, *tokens, flip=False):
    n = rows.shape[0]
    count, rank = len(factors), factors[0].shape[0]
    return call(
        functools.partial(project_kernel, count, flip),
        "project",
        (rows, *factors, *tokens),
        jax.ShapeDtypeStruct((rank * count, n) if flip else (n, rank * count), F32),
        tokens=len(tokens),
    )


def up_kernel(scale, start, mine_ref, other_ref, counts_ref, cot_ref, *refs):
    out_ref = refs[-1]
    rank, width = out_ref.shape
    proj = (mine_ref[...] + other_ref[...]).astype(jnp.bfloat16).astype(F32)
    weighted = proj * counts_ref[...]
    high = weighted.astype(jnp.bfloat16)
    low = (weighted - high.astype(F32)).astype(jnp.bfloat16)
    both = jnp.concatenate([high, low], axis=0)
    for c in columns_of(width, 1920):
        cot = cot_ref[:, start + c.start : start + c.stop]
        product = jnp.dot(both, cot, preferred_element_type=F32)
        out_ref[:, c] = ((product[:rank] + product[rank:]) * scale).astype(jnp.bfloat16)


def up_factor(mine, other, counts, cot, start, width, *tokens):
    rank, train = mine.shape
    return call(
        functools.partial(up_kernel, -1.0 / train, start),
        "up_factor",
        (mine, other, counts, cot, *tokens),
        jax.ShapeDtypeStruct((rank, width), jnp.bfloat16),
        tokens=len(tokens),
    )


def score_kernel(slots, picked, pad, start, *refs):
    pick_ref, masks_ref, mine_ref, other_ref, cot_ref, table_ref = refs[:6]
    up_refs, out_ref = refs[6:-1], refs[-1]
    rank, width = up_refs[0].shape
    parts = []
    for c in columns_of(width, 1920):
        factors = [u[:, c] for u in up_refs]
        if picked:
            factors[-2:] = [jnp.where(pick_ref[0] > 0, factors[-2], factors[-1])]
        cot = cot_ref[:, start + c.start : start + c.stop]
        parts.append(
            lax.dot_general(
                cot, jnp.concatenate(factors, axis=0), NT, preferred_element_type=F32
            )
        )
    change = total_of(parts) * (mine_ref[...] + other_ref[...])
    sums = jnp.dot(
        masks_ref[...], change, preferred_element_type=F32, precision=lax.Precision.HIGHEST
    )
    out_ref[...] = table_ref[...]
    for at, slot in enumerate(slots):
        added = jnp.sum(sums[:, at * rank : (at + 1) * rank], axis=1, keepdims=True)
        for kind in range(2):
            row = kind * pad + slot
            out_ref[row : row + 1, :] += jnp.broadcast_to(added[kind : kind + 1], (1, LANES))


def score(table, slots, pick, masks, mine, other, cot, ups, start):
    return call(
        functools.partial(
            score_kernel, tuple(slots), len(ups) > len(slots), table.shape[0] // 2, start
        ),
        "score",
        (pick, masks, mine, other, cot, table, *ups),
        jax.ShapeDtypeStruct(table.shape, F32),
        scalars=1,
    )


def finish_kernel(offsets, reach, corner_ref, mine_ref, other_ref, masks_ref, own_ref, rest_ref):
    pad = mine_ref.shape[0] // 2
    total = mine_ref[...] + other_ref[...]
    counts = jnp.maximum(jnp.sum(masks_ref[...], axis=1, keepdims=True), 1.0)
    lane = lax.broadcasted_iota(jnp.int32, (1, LANES), 1)
    corner = corner_ref[0]
    sums = [jnp.zeros((1, LANES), F32)] * 2
    for slot in range(len(offsets[0])):
        place = offsets[0][slot] + reach
        for other in range(1, len(offsets)):
            place = jnp.where(corner == other, offsets[other][slot] + reach, place)
        for kind in range(2):
            row = kind * pad + slot
            sums[kind] = jnp.where(lane == place, total[row : row + 1, :], sums[kind])
    for kind, ref in enumerate((own_ref, rest_ref)):
        ref[...] = (sums[kind] / counts[kind : kind + 1])[:, : ref.shape[1]]


def finish(mine, other, masks, corner, offsets, reach):
    shape = jax.ShapeDtypeStruct((1, 2 * reach + 1), F32)
    vmem = pl.BlockSpec(memory_space=pltpu.VMEM)
    return pl.pallas_call(
        functools.partial(finish_kernel, offsets, reach),
        in_specs=[pl.BlockSpec(memory_space=pltpu.SMEM), vmem, vmem, vmem],
        out_shape=(shape, shape),
        compiler_params=pltpu.CompilerParams(vmem_limit_bytes=VMEM_LIMIT),
        cost_estimate=pl.CostEstimate(flops=0, bytes_accessed=COST_BYTES, transcendentals=0),
        name="finish",
    )(corner, mine, other, masks)


def rest_of_sum(block):
    parts = lax.axis_size("tensor")
    if parts == 2:
        return lax.ppermute(block, "tensor", [(0, 1), (1, 0)])
    return lax.psum(block, "tensor") - block


def send(block, target, corners=None):
    count = lax.axis_size("skill")
    pairs = [(s, target(s) % count) for s in range(count) if corners is None or s % 4 in corners]
    return lax.ppermute(block, "skill", pairs)


def across(s):
    return s ^ 1


def down(s):
    return s ^ 2


def next_quad(s):
    return s - 4 if s & 2 else s + 4


QUAD_OFFSETS = ((0, 1, 2, -2, -1), (0, -1, 2, -2, 1), (0, 1, -2, 2, -1), (0, -1, -2, 2, 1))


def after(block, *others):
    return lax.optimization_barrier((block, *others))[0]


def spread_ring(block, reach):
    slots, ahead, behind = [block], block, block
    for _ in range(reach):
        ahead = send(ahead, lambda s: s - 1)
        behind = send(behind, lambda s: s + 1)
        slots += [ahead, behind]
    return slots


def on_device(
    stored_inputs,
    stored_output_gradient,
    training_token_index,
    validation_inputs,
    validation_output_gradient,
    validation_row_skill,
    adapter_down_init,
):
    reach = lax.axis_size("skill") // 8
    columns = 2 * reach + 1
    pad = -(-columns // 8) * 8
    my_skill = lax.axis_index("skill")
    corner = my_skill & 3
    ends = (corner == 0) | (corner == 3)
    pick = ends.astype(jnp.int32)[None]
    factor = adapter_down_init[0].T
    valid_act = validation_inputs[0]
    valid_cot = validation_output_gradient[0]
    cot = stored_output_gradient[0]
    train, hidden = cot.shape

    own = validation_row_skill == my_skill
    kind = lax.broadcasted_iota(jnp.int32, (8, own.shape[1]), 0)
    masks = jnp.where(kind < 2, (own == (kind == 0)).astype(F32), 0.0)
    counts = jnp.sum(
        (training_token_index[0][:, None] == jnp.arange(train)[None, :]).astype(F32),
        axis=0, keepdims=True,
    )
    table = jnp.zeros((2 * pad, LANES), F32)
    gather = functools.partial(score, pick=pick, masks=masks, cot=valid_cot)

    if reach == 2:
        half = hidden // 2
        down_x = send(factor, across)
        down_y = send(factor, down)
        proj = project(stored_inputs[0], [factor], flip=True)
        proj_rest = rest_of_sum(proj)
        up_a = up_factor(proj, proj_rest, counts, cot, 0, half)
        a_x, a_y = send(up_a, across), send(up_a, down)
        down_z = send(after(down_y, up_a), next_quad)
        near = project(valid_act, [factor, down_x, down_y], up_a)
        near_rest = rest_of_sum(near)
        up_b = up_factor(proj, proj_rest, counts, cot, half, half, near)
        b_x, b_y = send(up_b, across), send(up_b, down)
        a_z = send(after(a_y, up_b), next_quad)
        near_slots = dict(slots=(0, 1, 2), mine=near, other=near_rest)
        table = gather(table, ups=[up_a, a_x, a_y], start=0, **near_slots)
        down_w = send(jnp.where(ends, down_y, after(down_z, up_b)), across)
        b_z = send(after(b_y, table), next_quad)
        b_d = send(after(b_x, table), down)
        table = gather(table, ups=[up_b, b_x, b_y], start=half, **near_slots)
        a_w = send(jnp.where(ends, a_y, after(a_z, table)), across)
        far = project(valid_act, [down_z, down_w], table)
        far_rest = rest_of_sum(far)
        b_w = send(after(b_d, far), next_quad, (0, 3))
        far_slots = dict(slots=(3, 4), mine=far, other=far_rest)
        table = gather(table, ups=[a_z, a_w], start=0, **far_slots)
        table = gather(table, ups=[b_z, b_w, b_d], start=half, **far_slots)
        offsets = QUAD_OFFSETS
    else:
        downs = spread_ring(factor, reach)
        proj = project(stored_inputs[0], [factor], flip=True)
        up = up_factor(proj, rest_of_sum(proj), counts, cot, 0, hidden)
        ups = spread_ring(up, reach)
        for at in range(0, columns, 3):
            slots = range(at, min(at + 3, columns))
            mine = project(valid_act, [downs[s] for s in slots])
            table = gather(
                table, slots=slots, mine=mine, other=rest_of_sum(mine),
                ups=[ups[s] for s in slots], start=0,
            )
        offsets = ((0, *(o for d in range(reach) for o in (d + 1, -d - 1))),)

    return finish(table, rest_of_sum(table), masks, corner[None], offsets, reach)


def solution(mesh):
    in_specs = (
        P("skill", None, "tensor"),
        P("skill", None, "tensor"),
        P("skill", None),
        P("skill", None, "tensor"),
        P("skill", None, "tensor"),
        P("skill", None),
        P("skill", "tensor", None),
    )
    out_specs = (P("skill", None), P("skill", None))
    return jax.shard_map(
        on_device, mesh=mesh, in_specs=in_specs, out_specs=out_specs, check_vma=False
    )
```

```python
import functools

import jax
import jax.numpy as jnp
from jax import lax
from jax.experimental import pallas as pl
from jax.experimental.pallas import tpu as pltpu
from jax.sharding import PartitionSpec as P

VMEM_LIMIT = 16 * 1024 * 1024
LANES = 128
NT = (((1,), (1,)), ((), ()))
FLOPS = 1_000_000_000
F32 = jnp.float32


def tile_of(width, most):
    fits = [size for size in range(LANES, min(width, most) + 1, LANES) if width % size == 0]
    return fits[-1] if fits else width


def columns_of(width, most):
    tile = tile_of(width, most)
    return [slice(at, at + tile) for at in range(0, width, tile)]


def total_of(parts):
    return functools.reduce(lambda a, b: a + b, parts)


def call(kernel, name, operands, out, flops, scalars=0, tokens=0):
    vmem = pl.BlockSpec(memory_space=pltpu.VMEM)
    return pl.pallas_call(
        kernel,
        in_specs=[pl.BlockSpec(memory_space=pltpu.SMEM)] * scalars
        + [vmem] * (len(operands) - scalars - tokens)
        + [pl.BlockSpec(memory_space=pl.ANY)] * tokens,
        out_specs=jax.tree.map(lambda _: vmem, out),
        out_shape=out,
        compiler_params=pltpu.CompilerParams(vmem_limit_bytes=VMEM_LIMIT),
        cost_estimate=pl.CostEstimate(flops=flops, bytes_accessed=0, transcendentals=0),
        name=name,
    )(*operands)


def project_kernel(count, flip, *refs):
    rows_ref, factor_refs, out_ref = refs[0], refs[1 : 1 + count], refs[-1]
    parts = []
    for c in columns_of(rows_ref.shape[1], 2048):
        rows = rows_ref[:, c]
        factors = jnp.concatenate([f[:, c] for f in factor_refs], axis=0)
        ends = (factors, rows) if flip else (rows, factors)
        parts.append(lax.dot_general(*ends, NT, preferred_element_type=F32))
    out_ref[...] = total_of(parts)


def project(rows, factors, *tokens, flip=False):
    n = rows.shape[0]
    count, rank = len(factors), factors[0].shape[0]
    return call(
        functools.partial(project_kernel, count, flip),
        "project",
        (rows, *factors, *tokens),
        jax.ShapeDtypeStruct((rank * count, n) if flip else (n, rank * count), F32),
        FLOPS,
        tokens=len(tokens),
    )


def up_kernel(scale, mine_ref, other_ref, counts_ref, cot_ref, *out_refs):
    rank, width = out_refs[0].shape
    proj = (mine_ref[...] + other_ref[...]).astype(jnp.bfloat16).astype(F32)
    weighted = proj * counts_ref[...]
    high = weighted.astype(jnp.bfloat16)
    low = (weighted - high.astype(F32)).astype(jnp.bfloat16)
    both = jnp.concatenate([high, low], axis=0)
    for at, out_ref in enumerate(out_refs):
        for c in columns_of(width, 1920):
            cot = cot_ref[:, at * width + c.start : at * width + c.stop]
            product = jnp.dot(both, cot, preferred_element_type=F32)
            out_ref[:, c] = ((product[:rank] + product[rank:]) * scale).astype(jnp.bfloat16)


def up_factor(mine, other, counts, cot, pieces):
    rank, train = mine.shape
    piece = jax.ShapeDtypeStruct((rank, cot.shape[1] // pieces), jnp.bfloat16)
    return call(
        functools.partial(up_kernel, -1.0 / train),
        "up_factor",
        (mine, other, counts, cot),
        (piece,) * pieces,
        FLOPS,
    )


def score_kernel(slots, picked, pad, start, *refs):
    pick_ref, mask_ref, mine_ref, other_ref, cot_ref, table_ref = refs[:6]
    up_refs, out_ref = refs[6:-1], refs[-1]
    rank, width = up_refs[0].shape
    parts = []
    for c in columns_of(width, 1920):
        factors = [u[:, c] for u in up_refs]
        if picked:
            factors[-2:] = [jnp.where(pick_ref[0] > 0, factors[-2], factors[-1])]
        cot = cot_ref[:, start + c.start : start + c.stop]
        parts.append(
            lax.dot_general(
                cot, jnp.concatenate(factors, axis=0), NT, preferred_element_type=F32
            )
        )
    total = total_of(parts)
    out_ref[...] = table_ref[...]
    for start in range(0, total.shape[1], LANES):
        c = slice(start, min(start + LANES, total.shape[1]))
        change = total[:, c] * (mine_ref[:, c] + other_ref[:, c])
        own = change * mask_ref[:, : c.stop - c.start]
        sums = [jnp.sum(part, axis=0, keepdims=True) for part in (own, change - own)]
        for at in range(c.start // rank, c.stop // rank):
            lanes = slice(at * rank - start, (at + 1) * rank - start)
            for kind in range(2):
                row = kind * pad + slots[at]
                added = jnp.sum(sums[kind][:, lanes], axis=1, keepdims=True)
                out_ref[row : row + 1, :] += jnp.broadcast_to(added, (1, LANES))


def score(table, slots, pick, mask, mine, other, cot, ups, start):
    return call(
        functools.partial(
            score_kernel, tuple(slots), len(ups) > len(slots), table.shape[0] // 2, start
        ),
        "score",
        (pick, mask, mine, other, cot, table, *ups),
        jax.ShapeDtypeStruct(table.shape, F32),
        FLOPS,
        scalars=1,
    )


def finish_kernel(offsets, reach, corner_ref, mine_ref, other_ref, mask_ref, own_ref, rest_ref):
    pad = mine_ref.shape[0] // 2
    total = mine_ref[...] + other_ref[...]
    own = jnp.sum(mask_ref[...], axis=1, keepdims=True)
    counts = [jnp.maximum(n, 1.0) for n in (own, mask_ref.shape[1] - own)]
    lane = lax.broadcasted_iota(jnp.int32, (1, LANES), 1)
    corner = corner_ref[0]
    sums = [jnp.zeros((1, LANES), F32)] * 2
    for slot in range(len(offsets[0])):
        place = offsets[0][slot] + reach
        for other in range(1, len(offsets)):
            place = jnp.where(corner == other, offsets[other][slot] + reach, place)
        for kind in range(2):
            row = kind * pad + slot
            sums[kind] = jnp.where(lane == place, total[row : row + 1, :], sums[kind])
    for kind, ref in enumerate((own_ref, rest_ref)):
        ref[...] = (sums[kind] / counts[kind])[:, : ref.shape[1]]


def finish(mine, other, mask, corner, offsets, reach):
    shape = jax.ShapeDtypeStruct((1, 2 * reach + 1), F32)
    vmem = pl.BlockSpec(memory_space=pltpu.VMEM)
    return pl.pallas_call(
        functools.partial(finish_kernel, offsets, reach),
        in_specs=[pl.BlockSpec(memory_space=pltpu.SMEM), vmem, vmem, vmem],
        out_shape=(shape, shape),
        compiler_params=pltpu.CompilerParams(vmem_limit_bytes=VMEM_LIMIT),
        cost_estimate=pl.CostEstimate(flops=FLOPS, bytes_accessed=0, transcendentals=0),
        name="finish",
    )(corner, mine, other, mask)


def rest_of_sum(block):
    parts = lax.axis_size("tensor")
    if parts == 2:
        return lax.ppermute(block, "tensor", [(0, 1), (1, 0)])
    return lax.psum(block, "tensor") - block


def send(block, target, corners=None):
    count = lax.axis_size("skill")
    pairs = [(s, target(s) % count) for s in range(count) if corners is None or s % 4 in corners]
    return lax.ppermute(block, "skill", pairs)


def across(s):
    return s ^ 1


def down(s):
    return s ^ 2


def next_quad(s):
    return s - 4 if s & 2 else s + 4


QUAD_OFFSETS = ((0, 1, 2, -2, -1), (0, -1, 2, -2, 1), (0, 1, -2, 2, -1), (0, -1, -2, 2, 1))


def after(block, *others):
    return lax.optimization_barrier((block, *others))[0]


def spread_ring(block, reach):
    slots, ahead, behind = [block], block, block
    for _ in range(reach):
        ahead = send(ahead, lambda s: s - 1)
        behind = send(behind, lambda s: s + 1)
        slots += [ahead, behind]
    return slots


def on_device(
    stored_inputs,
    stored_output_gradient,
    training_token_index,
    validation_inputs,
    validation_output_gradient,
    validation_row_skill,
    adapter_down_init,
):
    reach = lax.axis_size("skill") // 8
    columns = 2 * reach + 1
    pad = -(-columns // 8) * 8
    my_skill = lax.axis_index("skill")
    corner = my_skill & 3
    ends = (corner == 0) | (corner == 3)
    pick = ends.astype(jnp.int32)[None]
    factor = adapter_down_init[0].T
    valid_act = validation_inputs[0]
    valid_cot = validation_output_gradient[0]
    cot = stored_output_gradient[0]
    train, hidden = cot.shape

    own = (validation_row_skill == my_skill).astype(F32)
    mask = jnp.broadcast_to(own[0][:, None], (own.shape[1], LANES))
    counts = jnp.sum(
        (training_token_index[0][:, None] == jnp.arange(train)[None, :]).astype(F32),
        axis=0, keepdims=True,
    )
    table = jnp.zeros((2 * pad, LANES), F32)
    gather = functools.partial(score, pick=pick, mask=mask, cot=valid_cot)

    if reach == 2:
        half = hidden // 2
        down_x = send(factor, across)
        down_y = send(factor, down)
        proj = project(stored_inputs[0], [factor], flip=True)
        proj_rest = rest_of_sum(proj)
        up_a, up_b = up_factor(proj, proj_rest, counts, cot, 2)
        a_x, a_y = send(up_a, across), send(up_a, down)
        down_z = send(down_y, next_quad)
        near = project(valid_act, [factor, down_x, down_y], up_a)
        near_rest = rest_of_sum(near)
        up_b = after(up_b, near)
        b_x, b_y = send(up_b, across), send(up_b, down)
        a_z = send(after(a_y, a_x), next_quad)
        near_slots = dict(slots=(0, 1, 2), mine=near, other=near_rest)
        down_w = send(jnp.where(ends, down_y, down_z), across)
        b_z = send(b_y, next_quad)
        b_d = send(b_x, down)
        a_w = send(jnp.where(ends, a_y, a_z), across)
        b_w = send(b_d, next_quad, (0, 3))
        table = gather(table, ups=[up_a, a_x, a_y], start=0, **near_slots)
        table = gather(table, ups=[up_b, b_x, b_y], start=half, **near_slots)
        far = project(valid_act, [down_z, down_w], table)
        far_rest = rest_of_sum(far)
        far_slots = dict(slots=(3, 4), mine=far, other=far_rest)
        table = gather(table, ups=[a_z, a_w], start=0, **far_slots)
        table = gather(table, ups=[b_z, b_w, b_d], start=half, **far_slots)
        offsets = QUAD_OFFSETS
    else:
        downs = spread_ring(factor, reach)
        proj = project(stored_inputs[0], [factor], flip=True)
        (up,) = up_factor(proj, rest_of_sum(proj), counts, cot, 1)
        ups = spread_ring(up, reach)
        for at in range(0, columns, 3):
            slots = range(at, min(at + 3, columns))
            mine = project(valid_act, [downs[s] for s in slots])
            table = gather(
                table, slots=slots, mine=mine, other=rest_of_sum(mine),
                ups=[ups[s] for s in slots], start=0,
            )
        offsets = ((0, *(o for d in range(reach) for o in (d + 1, -d - 1))),)

    return finish(table, rest_of_sum(table), own, corner[None], offsets, reach)


def solution(mesh):
    in_specs = (
        P("skill", None, "tensor"),
        P("skill", None, "tensor"),
        P("skill", None),
        P("skill", None, "tensor"),
        P("skill", None, "tensor"),
        P("skill", None),
        P("skill", "tensor", None),
    )
    out_specs = (P("skill", None), P("skill", None))
    return jax.shard_map(
        on_device, mesh=mesh, in_specs=in_specs, out_specs=out_specs, check_vma=False
    )
```

```python
import functools

import jax
import jax.numpy as jnp
from jax import lax
from jax.experimental import pallas as pl
from jax.experimental.pallas import tpu as pltpu
from jax.sharding import PartitionSpec as P

VMEM_LIMIT = 16 * 1024 * 1024
LANES = 128
NT = (((1,), (1,)), ((), ()))
FLOPS = 1_000_000_000
SCORE_FLOPS = 0
F32 = jnp.float32


def tile_of(width, most):
    fits = [size for size in range(LANES, min(width, most) + 1, LANES) if width % size == 0]
    return fits[-1] if fits else width


def columns_of(width, most):
    tile = tile_of(width, most)
    return [slice(at, at + tile) for at in range(0, width, tile)]


def total_of(parts):
    return functools.reduce(lambda a, b: a + b, parts)


def call(kernel, name, operands, out, flops, scalars=0, tokens=0):
    vmem = pl.BlockSpec(memory_space=pltpu.VMEM)
    return pl.pallas_call(
        kernel,
        in_specs=[pl.BlockSpec(memory_space=pltpu.SMEM)] * scalars
        + [vmem] * (len(operands) - scalars - tokens)
        + [pl.BlockSpec(memory_space=pl.ANY)] * tokens,
        out_specs=jax.tree.map(lambda _: vmem, out),
        out_shape=out,
        compiler_params=pltpu.CompilerParams(vmem_limit_bytes=VMEM_LIMIT),
        cost_estimate=pl.CostEstimate(flops=flops, bytes_accessed=0, transcendentals=0),
        name=name,
    )(*operands)


def project_kernel(count, flip, *refs):
    rows_ref, factor_refs, out_ref = refs[0], refs[1 : 1 + count], refs[-1]
    parts = []
    for c in columns_of(rows_ref.shape[1], 2048):
        rows = rows_ref[:, c]
        factors = jnp.concatenate([f[:, c] for f in factor_refs], axis=0)
        ends = (factors, rows) if flip else (rows, factors)
        parts.append(lax.dot_general(*ends, NT, preferred_element_type=F32))
    out_ref[...] = total_of(parts)


def project(rows, factors, *tokens, flip=False):
    n = rows.shape[0]
    count, rank = len(factors), factors[0].shape[0]
    return call(
        functools.partial(project_kernel, count, flip),
        "project",
        (rows, *factors, *tokens),
        jax.ShapeDtypeStruct((rank * count, n) if flip else (n, rank * count), F32),
        FLOPS,
        tokens=len(tokens),
    )


def up_kernel(scale, mine_ref, other_ref, counts_ref, cot_ref, *out_refs):
    rank, width = out_refs[0].shape
    proj = (mine_ref[...] + other_ref[...]).astype(jnp.bfloat16).astype(F32)
    weighted = proj * counts_ref[...]
    high = weighted.astype(jnp.bfloat16)
    low = (weighted - high.astype(F32)).astype(jnp.bfloat16)
    both = jnp.concatenate([high, low], axis=0)
    for at, out_ref in enumerate(out_refs):
        for c in columns_of(width, 1920):
            cot = cot_ref[:, at * width + c.start : at * width + c.stop]
            product = jnp.dot(both, cot, preferred_element_type=F32)
            out_ref[:, c] = ((product[:rank] + product[rank:]) * scale).astype(jnp.bfloat16)


def up_factor(mine, other, counts, cot, pieces):
    rank, train = mine.shape
    piece = jax.ShapeDtypeStruct((rank, cot.shape[1] // pieces), jnp.bfloat16)
    return call(
        functools.partial(up_kernel, -1.0 / train),
        "up_factor",
        (mine, other, counts, cot),
        (piece,) * pieces,
        FLOPS,
    )


def score_kernel(slots, picked, pad, start, *refs):
    pick_ref, mask_ref, mine_ref, other_ref, cot_ref, table_ref = refs[:6]
    up_refs, out_ref = refs[6:-1], refs[-1]
    rank, width = up_refs[0].shape
    parts = []
    for c in columns_of(width, 1920):
        factors = [u[:, c] for u in up_refs]
        if picked:
            factors[-2:] = [jnp.where(pick_ref[0] > 0, factors[-2], factors[-1])]
        cot = cot_ref[:, start + c.start : start + c.stop]
        parts.append(
            lax.dot_general(
                cot, jnp.concatenate(factors, axis=0), NT, preferred_element_type=F32
            )
        )
    total = total_of(parts)
    out_ref[...] = table_ref[...]
    for start in range(0, total.shape[1], LANES):
        c = slice(start, min(start + LANES, total.shape[1]))
        change = total[:, c] * (mine_ref[:, c] + other_ref[:, c])
        own = change * mask_ref[:, : c.stop - c.start]
        sums = [jnp.sum(part, axis=0, keepdims=True) for part in (own, change - own)]
        for at in range(c.start // rank, c.stop // rank):
            lanes = slice(at * rank - start, (at + 1) * rank - start)
            for kind in range(2):
                row = kind * pad + slots[at]
                added = jnp.sum(sums[kind][:, lanes], axis=1, keepdims=True)
                out_ref[row : row + 1, :] += jnp.broadcast_to(added, (1, LANES))


def score(table, slots, pick, mask, mine, other, cot, ups, start):
    return call(
        functools.partial(
            score_kernel, tuple(slots), len(ups) > len(slots), table.shape[0] // 2, start
        ),
        "score",
        (pick, mask, mine, other, cot, table, *ups),
        jax.ShapeDtypeStruct(table.shape, F32),
        SCORE_FLOPS,
        scalars=1,
    )


def finish_kernel(offsets, reach, corner_ref, mine_ref, other_ref, mask_ref, own_ref, rest_ref):
    pad = mine_ref.shape[0] // 2
    total = mine_ref[...] + other_ref[...]
    own = jnp.sum(mask_ref[...], axis=1, keepdims=True)
    counts = [jnp.maximum(n, 1.0) for n in (own, mask_ref.shape[1] - own)]
    lane = lax.broadcasted_iota(jnp.int32, (1, LANES), 1)
    corner = corner_ref[0]
    sums = [jnp.zeros((1, LANES), F32)] * 2
    for slot in range(len(offsets[0])):
        place = offsets[0][slot] + reach
        for other in range(1, len(offsets)):
            place = jnp.where(corner == other, offsets[other][slot] + reach, place)
        for kind in range(2):
            row = kind * pad + slot
            sums[kind] = jnp.where(lane == place, total[row : row + 1, :], sums[kind])
    for kind, ref in enumerate((own_ref, rest_ref)):
        ref[...] = (sums[kind] / counts[kind])[:, : ref.shape[1]]


def finish(mine, other, mask, corner, offsets, reach):
    shape = jax.ShapeDtypeStruct((1, 2 * reach + 1), F32)
    vmem = pl.BlockSpec(memory_space=pltpu.VMEM)
    return pl.pallas_call(
        functools.partial(finish_kernel, offsets, reach),
        in_specs=[pl.BlockSpec(memory_space=pltpu.SMEM), vmem, vmem, vmem],
        out_shape=(shape, shape),
        compiler_params=pltpu.CompilerParams(vmem_limit_bytes=VMEM_LIMIT),
        cost_estimate=pl.CostEstimate(flops=FLOPS, bytes_accessed=0, transcendentals=0),
        name="finish",
    )(corner, mine, other, mask)


def rest_of_sum(block):
    parts = lax.axis_size("tensor")
    if parts == 2:
        return lax.ppermute(block, "tensor", [(0, 1), (1, 0)])
    return lax.psum(block, "tensor") - block


def send(block, target, corners=None):
    count = lax.axis_size("skill")
    pairs = [(s, target(s) % count) for s in range(count) if corners is None or s % 4 in corners]
    return lax.ppermute(block, "skill", pairs)


def across(s):
    return s ^ 1


def down(s):
    return s ^ 2


def next_quad(s):
    return s - 4 if s & 2 else s + 4


QUAD_OFFSETS = ((0, 1, 2, -2, -1), (0, -1, 2, -2, 1), (0, 1, -2, 2, -1), (0, -1, -2, 2, 1))


def after(block, *others):
    return lax.optimization_barrier((block, *others))[0]


def spread_ring(block, reach):
    slots, ahead, behind = [block], block, block
    for _ in range(reach):
        ahead = send(ahead, lambda s: s - 1)
        behind = send(behind, lambda s: s + 1)
        slots += [ahead, behind]
    return slots


def on_device(
    stored_inputs,
    stored_output_gradient,
    training_token_index,
    validation_inputs,
    validation_output_gradient,
    validation_row_skill,
    adapter_down_init,
):
    reach = lax.axis_size("skill") // 8
    columns = 2 * reach + 1
    pad = -(-columns // 8) * 8
    my_skill = lax.axis_index("skill")
    corner = my_skill & 3
    ends = (corner == 0) | (corner == 3)
    pick = ends.astype(jnp.int32)[None]
    factor = adapter_down_init[0].T
    valid_act = validation_inputs[0]
    valid_cot = validation_output_gradient[0]
    cot = stored_output_gradient[0]
    train, hidden = cot.shape

    own = (validation_row_skill == my_skill).astype(F32)
    mask = jnp.broadcast_to(own[0][:, None], (own.shape[1], LANES))
    counts = jnp.sum(
        (training_token_index[0][:, None] == jnp.arange(train)[None, :]).astype(F32),
        axis=0, keepdims=True,
    )
    table = jnp.zeros((2 * pad, LANES), F32)
    gather = functools.partial(score, pick=pick, mask=mask, cot=valid_cot)

    if reach == 2:
        half = hidden // 2
        down_x = send(factor, across)
        down_y = send(factor, down)
        proj = project(stored_inputs[0], [factor], flip=True)
        proj_rest = rest_of_sum(proj)
        up_a, up_b = up_factor(proj, proj_rest, counts, cot, 2)
        a_x, a_y = send(up_a, across), send(up_a, down)
        down_z = send(down_y, next_quad)
        near = project(valid_act, [factor, down_x, down_y], up_a)
        near_rest = rest_of_sum(near)
        up_b = after(up_b, near)
        b_x, b_y = send(up_b, across), send(up_b, down)
        a_z = send(after(a_y, a_x), next_quad)
        near_slots = dict(slots=(0, 1, 2), mine=near, other=near_rest)
        down_w = send(jnp.where(ends, down_y, down_z), across)
        b_z = send(b_y, next_quad)
        b_d = send(b_x, down)
        a_w = send(jnp.where(ends, a_y, a_z), across)
        b_w = send(b_d, next_quad, (0, 3))
        table = gather(table, ups=[up_a, a_x, a_y], start=0, **near_slots)
        table = gather(table, ups=[up_b, b_x, b_y], start=half, **near_slots)
        far = project(valid_act, [down_z, down_w], table)
        far_rest = rest_of_sum(far)
        far_slots = dict(slots=(3, 4), mine=far, other=far_rest)
        table = gather(table, ups=[a_z, a_w], start=0, **far_slots)
        table = gather(table, ups=[b_z, b_w, b_d], start=half, **far_slots)
        offsets = QUAD_OFFSETS
    else:
        downs = spread_ring(factor, reach)
        proj = project(stored_inputs[0], [factor], flip=True)
        (up,) = up_factor(proj, rest_of_sum(proj), counts, cot, 1)
        ups = spread_ring(up, reach)
        for at in range(0, columns, 3):
            slots = range(at, min(at + 3, columns))
            mine = project(valid_act, [downs[s] for s in slots])
            table = gather(
                table, slots=slots, mine=mine, other=rest_of_sum(mine),
                ups=[ups[s] for s in slots], start=0,
            )
        offsets = ((0, *(o for d in range(reach) for o in (d + 1, -d - 1))),)

    return finish(table, rest_of_sum(table), own, corner[None], offsets, reach)


def solution(mesh):
    in_specs = (
        P("skill", None, "tensor"),
        P("skill", None, "tensor"),
        P("skill", None),
        P("skill", None, "tensor"),
        P("skill", None, "tensor"),
        P("skill", None),
        P("skill", "tensor", None),
    )
    out_specs = (P("skill", None), P("skill", None))
    return jax.shard_map(
        on_device, mesh=mesh, in_specs=in_specs, out_specs=out_specs, check_vma=False
    )
```

```python
import functools

import jax
import jax.numpy as jnp
from jax import lax
from jax.experimental import pallas as pl
from jax.experimental.pallas import tpu as pltpu
from jax.sharding import PartitionSpec as P

VMEM_LIMIT = 16 * 1024 * 1024
LANES = 128
NT = (((1,), (1,)), ((), ()))
FLOPS = 1_000_000_000
SCORE_FLOPS = 0
F32 = jnp.float32


def tile_of(width, most):
    fits = [size for size in range(LANES, min(width, most) + 1, LANES) if width % size == 0]
    return fits[-1] if fits else width


def columns_of(width, most):
    tile = tile_of(width, most)
    return [slice(at, at + tile) for at in range(0, width, tile)]


def total_of(parts):
    return functools.reduce(lambda a, b: a + b, parts)


def call(kernel, name, operands, out, flops, scalars=0, tokens=0):
    vmem = pl.BlockSpec(memory_space=pltpu.VMEM)
    return pl.pallas_call(
        kernel,
        in_specs=[pl.BlockSpec(memory_space=pltpu.SMEM)] * scalars
        + [vmem] * (len(operands) - scalars - tokens)
        + [pl.BlockSpec(memory_space=pl.ANY)] * tokens,
        out_specs=jax.tree.map(lambda _: vmem, out),
        out_shape=out,
        compiler_params=pltpu.CompilerParams(vmem_limit_bytes=VMEM_LIMIT),
        cost_estimate=pl.CostEstimate(flops=flops, bytes_accessed=0, transcendentals=0),
        name=name,
    )(*operands)


def project_kernel(count, flip, *refs):
    rows_ref, factor_refs, out_ref = refs[0], refs[1 : 1 + count], refs[-1]
    parts = []
    for c in columns_of(rows_ref.shape[1], 2048):
        rows = rows_ref[:, c]
        factors = jnp.concatenate([f[:, c] for f in factor_refs], axis=0)
        ends = (factors, rows) if flip else (rows, factors)
        parts.append(lax.dot_general(*ends, NT, preferred_element_type=F32))
    out_ref[...] = total_of(parts)


def project(rows, factors, *tokens, flip=False):
    n = rows.shape[0]
    count, rank = len(factors), factors[0].shape[0]
    return call(
        functools.partial(project_kernel, count, flip),
        "project",
        (rows, *factors, *tokens),
        jax.ShapeDtypeStruct((rank * count, n) if flip else (n, rank * count), F32),
        FLOPS,
        tokens=len(tokens),
    )


def up_kernel(scale, mine_ref, other_ref, counts_ref, cot_ref, *out_refs):
    rank, width = out_refs[0].shape
    proj = (mine_ref[...] + other_ref[...]).astype(jnp.bfloat16).astype(F32)
    weighted = proj * counts_ref[...]
    high = weighted.astype(jnp.bfloat16)
    low = (weighted - high.astype(F32)).astype(jnp.bfloat16)
    both = jnp.concatenate([high, low], axis=0)
    for at, out_ref in enumerate(out_refs):
        for c in columns_of(width, 1920):
            cot = cot_ref[:, at * width + c.start : at * width + c.stop]
            product = jnp.dot(both, cot, preferred_element_type=F32)
            out_ref[:, c] = ((product[:rank] + product[rank:]) * scale).astype(jnp.bfloat16)


def up_factor(mine, other, counts, cot, pieces):
    rank, train = mine.shape
    piece = jax.ShapeDtypeStruct((rank, cot.shape[1] // pieces), jnp.bfloat16)
    return call(
        functools.partial(up_kernel, -1.0 / train),
        "up_factor",
        (mine, other, counts, cot),
        (piece,) * pieces,
        FLOPS,
    )


def score_kernel(slots, picked, pad, start, *refs):
    pick_ref, mask_ref, mine_ref, other_ref, cot_ref, table_ref = refs[:6]
    up_refs, out_ref = refs[6:-1], refs[-1]
    rank, width = up_refs[0].shape
    parts = []
    for c in columns_of(width, 1920):
        factors = [u[:, c] for u in up_refs]
        if picked:
            factors[-2:] = [jnp.where(pick_ref[0] > 0, factors[-2], factors[-1])]
        cot = cot_ref[:, start + c.start : start + c.stop]
        parts.append(
            lax.dot_general(
                cot, jnp.concatenate(factors, axis=0), NT, preferred_element_type=F32
            )
        )
    total = total_of(parts)
    out_ref[...] = table_ref[...]
    for start in range(0, total.shape[1], LANES):
        c = slice(start, min(start + LANES, total.shape[1]))
        change = total[:, c] * (mine_ref[:, c] + other_ref[:, c])
        own = change * mask_ref[:, : c.stop - c.start]
        sums = [jnp.sum(part, axis=0, keepdims=True) for part in (own, change - own)]
        for at in range(c.start // rank, c.stop // rank):
            lanes = slice(at * rank - start, (at + 1) * rank - start)
            for kind in range(2):
                row = kind * pad + slots[at]
                added = jnp.sum(sums[kind][:, lanes], axis=1, keepdims=True)
                out_ref[row : row + 1, :] += jnp.broadcast_to(added, (1, LANES))


def score(table, slots, pick, mask, mine, other, cot, ups, start):
    return call(
        functools.partial(
            score_kernel, tuple(slots), len(ups) > len(slots), table.shape[0] // 2, start
        ),
        "score",
        (pick, mask, mine, other, cot, table, *ups),
        jax.ShapeDtypeStruct(table.shape, F32),
        SCORE_FLOPS,
        scalars=1,
    )


def finish_kernel(offsets, reach, corner_ref, mine_ref, other_ref, mask_ref, own_ref, rest_ref):
    pad = mine_ref.shape[0] // 2
    total = mine_ref[...] + other_ref[...]
    own = jnp.sum(mask_ref[...], axis=1, keepdims=True)
    counts = [jnp.maximum(n, 1.0) for n in (own, mask_ref.shape[1] - own)]
    lane = lax.broadcasted_iota(jnp.int32, (1, LANES), 1)
    corner = corner_ref[0]
    sums = [jnp.zeros((1, LANES), F32)] * 2
    for slot in range(len(offsets[0])):
        place = offsets[0][slot] + reach
        for other in range(1, len(offsets)):
            place = jnp.where(corner == other, offsets[other][slot] + reach, place)
        for kind in range(2):
            row = kind * pad + slot
            sums[kind] = jnp.where(lane == place, total[row : row + 1, :], sums[kind])
    for kind, ref in enumerate((own_ref, rest_ref)):
        ref[...] = (sums[kind] / counts[kind])[:, : ref.shape[1]]


def finish(mine, other, mask, corner, offsets, reach):
    shape = jax.ShapeDtypeStruct((1, 2 * reach + 1), F32)
    vmem = pl.BlockSpec(memory_space=pltpu.VMEM)
    return pl.pallas_call(
        functools.partial(finish_kernel, offsets, reach),
        in_specs=[pl.BlockSpec(memory_space=pltpu.SMEM), vmem, vmem, vmem],
        out_shape=(shape, shape),
        compiler_params=pltpu.CompilerParams(vmem_limit_bytes=VMEM_LIMIT),
        cost_estimate=pl.CostEstimate(flops=FLOPS, bytes_accessed=0, transcendentals=0),
        name="finish",
    )(corner, mine, other, mask)


def rest_of_sum(block):
    parts = lax.axis_size("tensor")
    if parts == 2:
        return lax.ppermute(block, "tensor", [(0, 1), (1, 0)])
    return lax.psum(block, "tensor") - block


def send(block, target, corners=None):
    count = lax.axis_size("skill")
    pairs = [(s, target(s) % count) for s in range(count) if corners is None or s % 4 in corners]
    return lax.ppermute(block, "skill", pairs)


def across(s):
    return s ^ 1


def down(s):
    return s ^ 2


def next_quad(s):
    return s - 4 if s & 2 else s + 4


QUAD_OFFSETS = ((0, 1, 2, -2, -1), (0, -1, 2, -2, 1), (0, 1, -2, 2, -1), (0, -1, -2, 2, 1))


def after(block, *others):
    return lax.optimization_barrier((block, *others))[0]


def spread_ring(block, reach):
    slots, ahead, behind = [block], block, block
    for _ in range(reach):
        ahead = send(ahead, lambda s: s - 1)
        behind = send(behind, lambda s: s + 1)
        slots += [ahead, behind]
    return slots


def on_device(
    stored_inputs,
    stored_output_gradient,
    training_token_index,
    validation_inputs,
    validation_output_gradient,
    validation_row_skill,
    adapter_down_init,
):
    reach = lax.axis_size("skill") // 8
    columns = 2 * reach + 1
    pad = -(-columns // 8) * 8
    my_skill = lax.axis_index("skill")
    corner = my_skill & 3
    ends = (corner == 0) | (corner == 3)
    pick = ends.astype(jnp.int32)[None]
    factor = adapter_down_init[0].T
    valid_act = validation_inputs[0]
    valid_cot = validation_output_gradient[0]
    cot = stored_output_gradient[0]
    train, hidden = cot.shape

    own = (validation_row_skill == my_skill).astype(F32)
    mask = jnp.broadcast_to(own[0][:, None], (own.shape[1], LANES))
    counts = jnp.sum(
        (training_token_index[0][:, None] == jnp.arange(train)[None, :]).astype(F32),
        axis=0, keepdims=True,
    )
    table = jnp.zeros((2 * pad, LANES), F32)
    gather = functools.partial(score, pick=pick, mask=mask, cot=valid_cot)

    if reach == 2:
        half = hidden // 2
        down_x = send(factor, across)
        down_y = send(factor, down)
        proj = project(stored_inputs[0], [factor], flip=True)
        proj_rest = rest_of_sum(proj)
        up_a, up_b = up_factor(proj, proj_rest, counts, cot, 2)
        a_x, a_y = send(up_a, across), send(up_a, down)
        down_z = send(down_y, next_quad)
        near = project(valid_act, [factor, down_x, down_y], up_a)
        near_rest = rest_of_sum(near)
        up_b = after(up_b, near)
        b_x, b_y = send(up_b, across), send(up_b, down)
        a_z = send(a_y, next_quad)
        near_slots = dict(slots=(0, 1, 2), mine=near, other=near_rest)
        table = gather(table, ups=[up_a, a_x, a_y], start=0, **near_slots)
        down_w = send(jnp.where(ends, down_y, down_z), across)
        b_z = send(after(b_y, table), next_quad)
        b_d = send(after(b_x, table), down)
        a_w = send(jnp.where(ends, a_y, a_z), across)
        b_w = send(b_d, next_quad, (0, 3))
        table = gather(table, ups=[up_b, b_x, b_y], start=half, **near_slots)
        far = project(valid_act, [down_z, down_w], table, b_z)
        far_rest = rest_of_sum(far)
        far_slots = dict(slots=(3, 4), mine=far, other=far_rest)
        table = gather(table, ups=[a_z, a_w], start=0, **far_slots)
        table = gather(table, ups=[b_z, b_w, b_d], start=half, **far_slots)
        offsets = QUAD_OFFSETS
    else:
        downs = spread_ring(factor, reach)
        proj = project(stored_inputs[0], [factor], flip=True)
        (up,) = up_factor(proj, rest_of_sum(proj), counts, cot, 1)
        ups = spread_ring(up, reach)
        for at in range(0, columns, 3):
            slots = range(at, min(at + 3, columns))
            mine = project(valid_act, [downs[s] for s in slots])
            table = gather(
                table, slots=slots, mine=mine, other=rest_of_sum(mine),
                ups=[ups[s] for s in slots], start=0,
            )
        offsets = ((0, *(o for d in range(reach) for o in (d + 1, -d - 1))),)

    return finish(table, rest_of_sum(table), own, corner[None], offsets, reach)


def solution(mesh):
    in_specs = (
        P("skill", None, "tensor"),
        P("skill", None, "tensor"),
        P("skill", None),
        P("skill", None, "tensor"),
        P("skill", None, "tensor"),
        P("skill", None),
        P("skill", "tensor", None),
    )
    out_specs = (P("skill", None), P("skill", None))
    return jax.shard_map(
        on_device, mesh=mesh, in_specs=in_specs, out_specs=out_specs, check_vma=False
    )
```

```python
import functools

import jax
import jax.numpy as jnp
from jax import lax
from jax.experimental import pallas as pl
from jax.experimental.pallas import tpu as pltpu
from jax.sharding import PartitionSpec as P

VMEM_LIMIT = 16 * 1024 * 1024
LANES = 128
NT = (((1,), (1,)), ((), ()))
FLOPS = 1_000_000_000
SCORE_FLOPS = 0
F32 = jnp.float32


def tile_of(width, most):
    fits = [size for size in range(LANES, min(width, most) + 1, LANES) if width % size == 0]
    return fits[-1] if fits else width


def columns_of(width, most):
    tile = tile_of(width, most)
    return [slice(at, at + tile) for at in range(0, width, tile)]


def total_of(parts):
    return functools.reduce(lambda a, b: a + b, parts)


def call(kernel, name, operands, out, flops, scalars=0, tokens=0):
    vmem = pl.BlockSpec(memory_space=pltpu.VMEM)
    return pl.pallas_call(
        kernel,
        in_specs=[pl.BlockSpec(memory_space=pltpu.SMEM)] * scalars
        + [vmem] * (len(operands) - scalars - tokens)
        + [pl.BlockSpec(memory_space=pl.ANY)] * tokens,
        out_specs=jax.tree.map(lambda _: vmem, out),
        out_shape=out,
        compiler_params=pltpu.CompilerParams(vmem_limit_bytes=VMEM_LIMIT),
        cost_estimate=pl.CostEstimate(flops=flops, bytes_accessed=0, transcendentals=0),
        name=name,
    )(*operands)


def project_kernel(count, flip, *refs):
    rows_ref, factor_refs, out_ref = refs[0], refs[1 : 1 + count], refs[-1]
    parts = []
    for c in columns_of(rows_ref.shape[1], 2048):
        rows = rows_ref[:, c]
        factors = jnp.concatenate([f[:, c] for f in factor_refs], axis=0)
        ends = (factors, rows) if flip else (rows, factors)
        parts.append(lax.dot_general(*ends, NT, preferred_element_type=F32))
    out_ref[...] = total_of(parts)


def project(rows, factors, *tokens, flip=False, flops=None):
    n = rows.shape[0]
    count, rank = len(factors), factors[0].shape[0]
    return call(
        functools.partial(project_kernel, count, flip),
        "project",
        (rows, *factors, *tokens),
        jax.ShapeDtypeStruct((rank * count, n) if flip else (n, rank * count), F32),
        FLOPS if flops is None else flops,
        tokens=len(tokens),
    )


def up_kernel(scale, mine_ref, other_ref, counts_ref, cot_ref, *out_refs):
    rank, width = out_refs[0].shape
    proj = (mine_ref[...] + other_ref[...]).astype(jnp.bfloat16).astype(F32)
    weighted = proj * counts_ref[...]
    high = weighted.astype(jnp.bfloat16)
    low = (weighted - high.astype(F32)).astype(jnp.bfloat16)
    both = jnp.concatenate([high, low], axis=0)
    for at, out_ref in enumerate(out_refs):
        for c in columns_of(width, 1920):
            cot = cot_ref[:, at * width + c.start : at * width + c.stop]
            product = jnp.dot(both, cot, preferred_element_type=F32)
            out_ref[:, c] = ((product[:rank] + product[rank:]) * scale).astype(jnp.bfloat16)


def up_factor(mine, other, counts, cot, pieces):
    rank, train = mine.shape
    piece = jax.ShapeDtypeStruct((rank, cot.shape[1] // pieces), jnp.bfloat16)
    return call(
        functools.partial(up_kernel, -1.0 / train),
        "up_factor",
        (mine, other, counts, cot),
        (piece,) * pieces,
        FLOPS,
    )


def score_kernel(slots, picked, pad, start, *refs):
    pick_ref, mask_ref, mine_ref, other_ref, cot_ref, table_ref = refs[:6]
    up_refs, out_ref = refs[6:-1], refs[-1]
    rank, width = up_refs[0].shape
    parts = []
    for c in columns_of(width, 1920):
        factors = [u[:, c] for u in up_refs]
        if picked:
            factors[-2:] = [jnp.where(pick_ref[0] > 0, factors[-2], factors[-1])]
        cot = cot_ref[:, start + c.start : start + c.stop]
        parts.append(
            lax.dot_general(
                cot, jnp.concatenate(factors, axis=0), NT, preferred_element_type=F32
            )
        )
    total = total_of(parts)
    out_ref[...] = table_ref[...]
    for start in range(0, total.shape[1], LANES):
        c = slice(start, min(start + LANES, total.shape[1]))
        change = total[:, c] * (mine_ref[:, c] + other_ref[:, c])
        own = change * mask_ref[:, : c.stop - c.start]
        sums = [jnp.sum(part, axis=0, keepdims=True) for part in (own, change - own)]
        for at in range(c.start // rank, c.stop // rank):
            lanes = slice(at * rank - start, (at + 1) * rank - start)
            for kind in range(2):
                row = kind * pad + slots[at]
                added = jnp.sum(sums[kind][:, lanes], axis=1, keepdims=True)
                out_ref[row : row + 1, :] += jnp.broadcast_to(added, (1, LANES))


def score(table, slots, pick, mask, mine, other, cot, ups, start):
    return call(
        functools.partial(
            score_kernel, tuple(slots), len(ups) > len(slots), table.shape[0] // 2, start
        ),
        "score",
        (pick, mask, mine, other, cot, table, *ups),
        jax.ShapeDtypeStruct(table.shape, F32),
        SCORE_FLOPS,
        scalars=1,
    )


def finish_kernel(offsets, reach, corner_ref, mine_ref, other_ref, mask_ref, own_ref, rest_ref):
    pad = mine_ref.shape[0] // 2
    total = mine_ref[...] + other_ref[...]
    own = jnp.sum(mask_ref[...], axis=1, keepdims=True)
    counts = [jnp.maximum(n, 1.0) for n in (own, mask_ref.shape[1] - own)]
    lane = lax.broadcasted_iota(jnp.int32, (1, LANES), 1)
    corner = corner_ref[0]
    sums = [jnp.zeros((1, LANES), F32)] * 2
    for slot in range(len(offsets[0])):
        place = offsets[0][slot] + reach
        for other in range(1, len(offsets)):
            place = jnp.where(corner == other, offsets[other][slot] + reach, place)
        for kind in range(2):
            row = kind * pad + slot
            sums[kind] = jnp.where(lane == place, total[row : row + 1, :], sums[kind])
    for kind, ref in enumerate((own_ref, rest_ref)):
        ref[...] = (sums[kind] / counts[kind])[:, : ref.shape[1]]


def finish(mine, other, mask, corner, offsets, reach):
    shape = jax.ShapeDtypeStruct((1, 2 * reach + 1), F32)
    vmem = pl.BlockSpec(memory_space=pltpu.VMEM)
    return pl.pallas_call(
        functools.partial(finish_kernel, offsets, reach),
        in_specs=[pl.BlockSpec(memory_space=pltpu.SMEM), vmem, vmem, vmem],
        out_shape=(shape, shape),
        compiler_params=pltpu.CompilerParams(vmem_limit_bytes=VMEM_LIMIT),
        cost_estimate=pl.CostEstimate(flops=FLOPS, bytes_accessed=0, transcendentals=0),
        name="finish",
    )(corner, mine, other, mask)


def rest_of_sum(block):
    parts = lax.axis_size("tensor")
    if parts == 2:
        return lax.ppermute(block, "tensor", [(0, 1), (1, 0)])
    return lax.psum(block, "tensor") - block


def send(block, target, corners=None):
    count = lax.axis_size("skill")
    pairs = [(s, target(s) % count) for s in range(count) if corners is None or s % 4 in corners]
    return lax.ppermute(block, "skill", pairs)


def across(s):
    return s ^ 1


def down(s):
    return s ^ 2


def next_quad(s):
    return s - 4 if s & 2 else s + 4


QUAD_OFFSETS = ((0, 1, 2, -2, -1), (0, -1, 2, -2, 1), (0, 1, -2, 2, -1), (0, -1, -2, 2, 1))


def after(block, *others):
    return lax.optimization_barrier((block, *others))[0]


def spread_ring(block, reach):
    slots, ahead, behind = [block], block, block
    for _ in range(reach):
        ahead = send(ahead, lambda s: s - 1)
        behind = send(behind, lambda s: s + 1)
        slots += [ahead, behind]
    return slots


def on_device(
    stored_inputs,
    stored_output_gradient,
    training_token_index,
    validation_inputs,
    validation_output_gradient,
    validation_row_skill,
    adapter_down_init,
):
    reach = lax.axis_size("skill") // 8
    columns = 2 * reach + 1
    pad = -(-columns // 8) * 8
    my_skill = lax.axis_index("skill")
    corner = my_skill & 3
    ends = (corner == 0) | (corner == 3)
    pick = ends.astype(jnp.int32)[None]
    factor = adapter_down_init[0].T
    valid_act = validation_inputs[0]
    valid_cot = validation_output_gradient[0]
    cot = stored_output_gradient[0]
    train, hidden = cot.shape

    own = (validation_row_skill == my_skill).astype(F32)
    mask = jnp.broadcast_to(own[0][:, None], (own.shape[1], LANES))
    counts = jnp.sum(
        (training_token_index[0][:, None] == jnp.arange(train)[None, :]).astype(F32),
        axis=0, keepdims=True,
    )
    table = jnp.zeros((2 * pad, LANES), F32)
    gather = functools.partial(score, pick=pick, mask=mask, cot=valid_cot)

    if reach == 2:
        half = hidden // 2
        down_x, down_y = send(factor, across), send(factor, down)
        proj = project(stored_inputs[0], [factor], flip=True)
        proj_rest = rest_of_sum(proj)
        up_a, up_b = up_factor(proj, proj_rest, counts, cot, 2)
        a_x, a_y = send(up_a, across), send(up_a, down)
        down_z = send(after(down_y, up_a), next_quad)
        near = project(valid_act, [factor, down_x, down_y], up_a, flops=3 * FLOPS)
        near_rest = rest_of_sum(near)
        b_x, b_y = send(up_b, across), send(up_b, down)
        a_z = send(after(a_y, up_b), next_quad)
        near_slots = dict(slots=(0, 1, 2), mine=near, other=near_rest)
        table = gather(after(table, down_z), ups=[up_a, a_x, a_y], start=0, **near_slots)
        down_last = jnp.where(ends, down_y, after(down_z, table))
        down_w = send(down_last, across)
        b_z = send(after(b_y, table, down_last), next_quad)
        b_d = send(after(b_x, down_last), down)
        a_w = send(jnp.where(ends, a_y, a_z), across)
        table = gather(table, ups=[up_b, b_x, b_y], start=half, **near_slots)
        b_w = send(after(b_d, table), next_quad, (0, 3))
        far = project(valid_act, [down_z, down_w], table)
        far_rest = rest_of_sum(far)
        far_slots = dict(slots=(3, 4), mine=far, other=far_rest)
        table = gather(table, ups=[a_z, a_w], start=0, **far_slots)
        table = gather(table, ups=[b_z, b_w, b_d], start=half, **far_slots)
        offsets = QUAD_OFFSETS
    else:
        downs = spread_ring(factor, reach)
        proj = project(stored_inputs[0], [factor], flip=True)
        (up,) = up_factor(proj, rest_of_sum(proj), counts, cot, 1)
        ups = spread_ring(up, reach)
        for at in range(0, columns, 3):
            slots = range(at, min(at + 3, columns))
            mine = project(valid_act, [downs[s] for s in slots])
            table = gather(
                table, slots=slots, mine=mine, other=rest_of_sum(mine),
                ups=[ups[s] for s in slots], start=0,
            )
        offsets = ((0, *(o for d in range(reach) for o in (d + 1, -d - 1))),)

    return finish(table, rest_of_sum(table), own, corner[None], offsets, reach)


def solution(mesh):
    in_specs = (
        P("skill", None, "tensor"),
        P("skill", None, "tensor"),
        P("skill", None),
        P("skill", None, "tensor"),
        P("skill", None, "tensor"),
        P("skill", None),
        P("skill", "tensor", None),
    )
    out_specs = (P("skill", None), P("skill", None))
    return jax.shard_map(
        on_device, mesh=mesh, in_specs=in_specs, out_specs=out_specs, check_vma=False
    )
```

```python
import functools

import jax
import jax.numpy as jnp
from jax import lax
from jax.experimental import pallas as pl
from jax.experimental.pallas import tpu as pltpu
from jax.sharding import PartitionSpec as P

VMEM_LIMIT = 16 * 1024 * 1024
LANES = 128
NT = (((1,), (1,)), ((), ()))
FLOPS = 1_000_000_000
SCORE_FLOPS = 0
F32 = jnp.float32


def tile_of(width, most):
    fits = [size for size in range(LANES, min(width, most) + 1, LANES) if width % size == 0]
    return fits[-1] if fits else width


def columns_of(width, most):
    tile = tile_of(width, most)
    return [slice(at, at + tile) for at in range(0, width, tile)]


def total_of(parts):
    return functools.reduce(lambda a, b: a + b, parts)


def call(kernel, name, operands, out, flops, scalars=0, tokens=0):
    vmem = pl.BlockSpec(memory_space=pltpu.VMEM)
    return pl.pallas_call(
        kernel,
        in_specs=[pl.BlockSpec(memory_space=pltpu.SMEM)] * scalars
        + [vmem] * (len(operands) - scalars - tokens)
        + [pl.BlockSpec(memory_space=pl.ANY)] * tokens,
        out_specs=jax.tree.map(lambda _: vmem, out),
        out_shape=out,
        compiler_params=pltpu.CompilerParams(vmem_limit_bytes=VMEM_LIMIT),
        cost_estimate=pl.CostEstimate(flops=flops, bytes_accessed=0, transcendentals=0),
        name=name,
    )(*operands)


def project_kernel(count, flip, *refs):
    rows_ref, factor_refs, out_ref = refs[0], refs[1 : 1 + count], refs[-1]
    parts = []
    for c in columns_of(rows_ref.shape[1], 2048):
        rows = rows_ref[:, c]
        factors = jnp.concatenate([f[:, c] for f in factor_refs], axis=0)
        ends = (factors, rows) if flip else (rows, factors)
        parts.append(lax.dot_general(*ends, NT, preferred_element_type=F32))
    out_ref[...] = total_of(parts)


def project(rows, factors, *tokens, flip=False, flops=None):
    n = rows.shape[0]
    count, rank = len(factors), factors[0].shape[0]
    return call(
        functools.partial(project_kernel, count, flip),
        "project",
        (rows, *factors, *tokens),
        jax.ShapeDtypeStruct((rank * count, n) if flip else (n, rank * count), F32),
        FLOPS if flops is None else flops,
        tokens=len(tokens),
    )


def up_kernel(scale, mine_ref, other_ref, counts_ref, cot_ref, *out_refs):
    rank, width = out_refs[0].shape
    proj = (mine_ref[...] + other_ref[...]).astype(jnp.bfloat16).astype(F32)
    weighted = proj * counts_ref[...]
    high = weighted.astype(jnp.bfloat16)
    low = (weighted - high.astype(F32)).astype(jnp.bfloat16)
    both = jnp.concatenate([high, low], axis=0)
    for at, out_ref in enumerate(out_refs):
        for c in columns_of(width, 1920):
            cot = cot_ref[:, at * width + c.start : at * width + c.stop]
            product = jnp.dot(both, cot, preferred_element_type=F32)
            out_ref[:, c] = ((product[:rank] + product[rank:]) * scale).astype(jnp.bfloat16)


def up_factor(mine, other, counts, cot, pieces):
    rank, train = mine.shape
    piece = jax.ShapeDtypeStruct((rank, cot.shape[1] // pieces), jnp.bfloat16)
    return call(
        functools.partial(up_kernel, -1.0 / train),
        "up_factor",
        (mine, other, counts, cot),
        (piece,) * pieces,
        FLOPS,
    )


def score_kernel(slots, picked, pad, start, *refs):
    pick_ref, mask_ref, mine_ref, other_ref, cot_ref, table_ref = refs[:6]
    up_refs, out_ref = refs[6:-1], refs[-1]
    rank, width = up_refs[0].shape
    parts = []
    for c in columns_of(width, 1920):
        factors = [u[:, c] for u in up_refs]
        if picked:
            factors[-2:] = [jnp.where(pick_ref[0] > 0, factors[-2], factors[-1])]
        cot = cot_ref[:, start + c.start : start + c.stop]
        parts.append(
            lax.dot_general(
                cot, jnp.concatenate(factors, axis=0), NT, preferred_element_type=F32
            )
        )
    total = total_of(parts)
    out_ref[...] = table_ref[...]
    for start in range(0, total.shape[1], LANES):
        c = slice(start, min(start + LANES, total.shape[1]))
        change = total[:, c] * (mine_ref[:, c] + other_ref[:, c])
        own = change * mask_ref[:, : c.stop - c.start]
        sums = [jnp.sum(part, axis=0, keepdims=True) for part in (own, change - own)]
        for at in range(c.start // rank, c.stop // rank):
            lanes = slice(at * rank - start, (at + 1) * rank - start)
            for kind in range(2):
                row = kind * pad + slots[at]
                added = jnp.sum(sums[kind][:, lanes], axis=1, keepdims=True)
                out_ref[row : row + 1, :] += jnp.broadcast_to(added, (1, LANES))


def score(table, slots, pick, mask, mine, other, cot, ups, start):
    return call(
        functools.partial(
            score_kernel, tuple(slots), len(ups) > len(slots), table.shape[0] // 2, start
        ),
        "score",
        (pick, mask, mine, other, cot, table, *ups),
        jax.ShapeDtypeStruct(table.shape, F32),
        SCORE_FLOPS,
        scalars=1,
    )


def empty_kernel(block_ref, *refs):
    refs[-1][...] = jnp.zeros_like(refs[-1])


def empty_table(shape, block, *tokens):
    return call(
        empty_kernel,
        "empty_table",
        (block, *tokens),
        jax.ShapeDtypeStruct(shape, F32),
        0,
        tokens=len(tokens),
    )


def finish_kernel(offsets, reach, corner_ref, mine_ref, other_ref, mask_ref, own_ref, rest_ref):
    pad = mine_ref.shape[0] // 2
    total = mine_ref[...] + other_ref[...]
    own = jnp.sum(mask_ref[...], axis=1, keepdims=True)
    counts = [jnp.maximum(n, 1.0) for n in (own, mask_ref.shape[1] - own)]
    lane = lax.broadcasted_iota(jnp.int32, (1, LANES), 1)
    corner = corner_ref[0]
    sums = [jnp.zeros((1, LANES), F32)] * 2
    for slot in range(len(offsets[0])):
        place = offsets[0][slot] + reach
        for other in range(1, len(offsets)):
            place = jnp.where(corner == other, offsets[other][slot] + reach, place)
        for kind in range(2):
            row = kind * pad + slot
            sums[kind] = jnp.where(lane == place, total[row : row + 1, :], sums[kind])
    for kind, ref in enumerate((own_ref, rest_ref)):
        ref[...] = (sums[kind] / counts[kind])[:, : ref.shape[1]]


def finish(mine, other, mask, corner, offsets, reach):
    shape = jax.ShapeDtypeStruct((1, 2 * reach + 1), F32)
    vmem = pl.BlockSpec(memory_space=pltpu.VMEM)
    return pl.pallas_call(
        functools.partial(finish_kernel, offsets, reach),
        in_specs=[pl.BlockSpec(memory_space=pltpu.SMEM), vmem, vmem, vmem],
        out_shape=(shape, shape),
        compiler_params=pltpu.CompilerParams(vmem_limit_bytes=VMEM_LIMIT),
        cost_estimate=pl.CostEstimate(flops=FLOPS, bytes_accessed=0, transcendentals=0),
        name="finish",
    )(corner, mine, other, mask)


def rest_of_sum(block):
    parts = lax.axis_size("tensor")
    if parts == 2:
        return lax.ppermute(block, "tensor", [(0, 1), (1, 0)])
    return lax.psum(block, "tensor") - block


def send(block, target, corners=None):
    count = lax.axis_size("skill")
    pairs = [(s, target(s) % count) for s in range(count) if corners is None or s % 4 in corners]
    return lax.ppermute(block, "skill", pairs)


def across(s):
    return s ^ 1


def down(s):
    return s ^ 2


def next_quad(s):
    return s - 4 if s & 2 else s + 4


QUAD_OFFSETS = ((0, 1, 2, -2, -1), (0, -1, 2, -2, 1), (0, 1, -2, 2, -1), (0, -1, -2, 2, 1))


def after(block, *others):
    return lax.optimization_barrier((block, *others))[0]


def spread_ring(block, reach):
    slots, ahead, behind = [block], block, block
    for _ in range(reach):
        ahead = send(ahead, lambda s: s - 1)
        behind = send(behind, lambda s: s + 1)
        slots += [ahead, behind]
    return slots


def on_device(
    stored_inputs,
    stored_output_gradient,
    training_token_index,
    validation_inputs,
    validation_output_gradient,
    validation_row_skill,
    adapter_down_init,
):
    reach = lax.axis_size("skill") // 8
    columns = 2 * reach + 1
    pad = -(-columns // 8) * 8
    my_skill = lax.axis_index("skill")
    corner = my_skill & 3
    ends = (corner == 0) | (corner == 3)
    pick = ends.astype(jnp.int32)[None]
    factor = adapter_down_init[0].T
    valid_act = validation_inputs[0]
    valid_cot = validation_output_gradient[0]
    cot = stored_output_gradient[0]
    train, hidden = cot.shape

    own = (validation_row_skill == my_skill).astype(F32)
    mask = jnp.broadcast_to(own[0][:, None], (own.shape[1], LANES))
    counts = jnp.sum(
        (training_token_index[0][:, None] == jnp.arange(train)[None, :]).astype(F32),
        axis=0, keepdims=True,
    )
    table = jnp.zeros((2 * pad, LANES), F32)
    gather = functools.partial(score, pick=pick, mask=mask, cot=valid_cot)

    if reach == 2:
        half = hidden // 2
        down_x, down_y = send(factor, across), send(factor, down)
        proj = project(stored_inputs[0], [factor], flip=True)
        proj_rest = rest_of_sum(proj)
        up_a, up_b = up_factor(proj, proj_rest, counts, cot, 2)
        a_x, a_y = send(up_a, across), send(up_a, down)
        down_z = send(after(down_y, up_a), next_quad)
        near = project(valid_act, [factor, down_x, down_y], flops=3 * FLOPS)
        near_rest = rest_of_sum(near)
        table = empty_table(table.shape, valid_cot, near)
        b_x, b_y = send(up_b, across), send(up_b, down)
        a_z = send(after(a_y, table), next_quad)
        near_slots = dict(slots=(0, 1, 2), mine=near, other=near_rest)
        table = gather(after(table, down_z), ups=[up_a, a_x, a_y], start=0, **near_slots)
        down_last = jnp.where(ends, down_y, after(down_z, table))
        down_w = send(down_last, across)
        b_z = send(after(b_y, table, down_last), next_quad)
        b_d = send(after(b_x, down_last), down)
        a_w = send(jnp.where(ends, a_y, a_z), across)
        table = gather(table, ups=[up_b, b_x, b_y], start=half, **near_slots)
        b_w = send(after(b_d, table), next_quad, (0, 3))
        far = project(valid_act, [down_z, down_w], table)
        far_rest = rest_of_sum(far)
        far_slots = dict(slots=(3, 4), mine=far, other=far_rest)
        table = gather(table, ups=[a_z, a_w], start=0, **far_slots)
        table = gather(table, ups=[b_z, b_w, b_d], start=half, **far_slots)
        offsets = QUAD_OFFSETS
    else:
        downs = spread_ring(factor, reach)
        proj = project(stored_inputs[0], [factor], flip=True)
        (up,) = up_factor(proj, rest_of_sum(proj), counts, cot, 1)
        ups = spread_ring(up, reach)
        for at in range(0, columns, 3):
            slots = range(at, min(at + 3, columns))
            mine = project(valid_act, [downs[s] for s in slots])
            table = gather(
                table, slots=slots, mine=mine, other=rest_of_sum(mine),
                ups=[ups[s] for s in slots], start=0,
            )
        offsets = ((0, *(o for d in range(reach) for o in (d + 1, -d - 1))),)

    return finish(table, rest_of_sum(table), own, corner[None], offsets, reach)


def solution(mesh):
    in_specs = (
        P("skill", None, "tensor"),
        P("skill", None, "tensor"),
        P("skill", None),
        P("skill", None, "tensor"),
        P("skill", None, "tensor"),
        P("skill", None),
        P("skill", "tensor", None),
    )
    out_specs = (P("skill", None), P("skill", None))
    return jax.shard_map(
        on_device, mesh=mesh, in_specs=in_specs, out_specs=out_specs, check_vma=False
    )
```

```python
import functools

import jax
import jax.numpy as jnp
from jax import lax
from jax.experimental import pallas as pl
from jax.experimental.pallas import tpu as pltpu
from jax.sharding import PartitionSpec as P

VMEM_LIMIT = 16 * 1024 * 1024
LANES = 128
NT = (((1,), (1,)), ((), ()))
FLOPS = 1_000_000_000
SCORE_FLOPS = 0
F32 = jnp.float32


def tile_of(width, most):
    fits = [size for size in range(LANES, min(width, most) + 1, LANES) if width % size == 0]
    return fits[-1] if fits else width


def columns_of(width, most):
    tile = tile_of(width, most)
    return [slice(at, at + tile) for at in range(0, width, tile)]


def total_of(parts):
    return functools.reduce(lambda a, b: a + b, parts)


def call(kernel, name, operands, out, flops, scalars=0, tokens=0):
    vmem = pl.BlockSpec(memory_space=pltpu.VMEM)
    return pl.pallas_call(
        kernel,
        in_specs=[pl.BlockSpec(memory_space=pltpu.SMEM)] * scalars
        + [vmem] * (len(operands) - scalars - tokens)
        + [pl.BlockSpec(memory_space=pl.ANY)] * tokens,
        out_specs=jax.tree.map(lambda _: vmem, out),
        out_shape=out,
        compiler_params=pltpu.CompilerParams(vmem_limit_bytes=VMEM_LIMIT),
        cost_estimate=pl.CostEstimate(flops=flops, bytes_accessed=0, transcendentals=0),
        name=name,
    )(*operands)


def project_kernel(count, flip, *refs):
    rows_ref, factor_refs, out_ref = refs[0], refs[1 : 1 + count], refs[-1]
    parts = []
    for c in columns_of(rows_ref.shape[1], 2048):
        rows = rows_ref[:, c]
        factors = jnp.concatenate([f[:, c] for f in factor_refs], axis=0)
        ends = (factors, rows) if flip else (rows, factors)
        parts.append(lax.dot_general(*ends, NT, preferred_element_type=F32))
    out_ref[...] = total_of(parts)


def project(rows, factors, *tokens, flip=False, flops=None):
    n = rows.shape[0]
    count, rank = len(factors), sum(f.shape[0] for f in factors)
    return call(
        functools.partial(project_kernel, count, flip),
        "project",
        (rows, *factors, *tokens),
        jax.ShapeDtypeStruct((rank, n) if flip else (n, rank), F32),
        FLOPS if flops is None else flops,
        tokens=len(tokens),
    )


def up_kernel(scale, mine_ref, other_ref, counts_ref, cot_ref, *out_refs):
    rank, start = out_refs[0].shape[0], 0
    proj = (mine_ref[...] + other_ref[...]).astype(jnp.bfloat16).astype(F32)
    weighted = proj * counts_ref[...]
    high = weighted.astype(jnp.bfloat16)
    low = (weighted - high.astype(F32)).astype(jnp.bfloat16)
    both = jnp.concatenate([high, low], axis=0)
    for out_ref in out_refs:
        for c in columns_of(out_ref.shape[1], 1920):
            cot = cot_ref[:, start + c.start : start + c.stop]
            product = jnp.dot(both, cot, preferred_element_type=F32)
            out_ref[:, c] = ((product[:rank] + product[rank:]) * scale).astype(jnp.bfloat16)
        start += out_ref.shape[1]


def up_factor(mine, other, counts, cot, widths):
    rank, train = mine.shape
    return call(
        functools.partial(up_kernel, -1.0 / train),
        "up_factor",
        (mine, other, counts, cot),
        tuple(jax.ShapeDtypeStruct((rank, width), jnp.bfloat16) for width in widths),
        FLOPS,
    )


def score_kernel(slots, picked, pad, start, *refs):
    pick_ref, mask_ref, mine_ref, other_ref, cot_ref, table_ref = refs[:6]
    up_refs, out_ref = refs[6:-1], refs[-1]
    rank, width = up_refs[0].shape
    parts = []
    for c in columns_of(width, 1920):
        factors = [u[:, c] for u in up_refs]
        if picked:
            factors[-2:] = [jnp.where(pick_ref[0] > 0, factors[-2], factors[-1])]
        cot = cot_ref[:, start + c.start : start + c.stop]
        parts.append(
            lax.dot_general(
                cot, jnp.concatenate(factors, axis=0), NT, preferred_element_type=F32
            )
        )
    total = total_of(parts)
    out_ref[...] = table_ref[...]
    for start in range(0, total.shape[1], LANES):
        c = slice(start, min(start + LANES, total.shape[1]))
        change = total[:, c] * (mine_ref[:, c] + other_ref[:, c])
        own = change * mask_ref[:, : c.stop - c.start]
        sums = [jnp.sum(part, axis=0, keepdims=True) for part in (own, change - own)]
        for at in range(c.start // rank, c.stop // rank):
            lanes = slice(at * rank - start, (at + 1) * rank - start)
            for kind in range(2):
                row = kind * pad + slots[at]
                added = jnp.sum(sums[kind][:, lanes], axis=1, keepdims=True)
                out_ref[row : row + 1, :] += jnp.broadcast_to(added, (1, LANES))


def score(table, slots, pick, mask, mine, other, cot, ups, start):
    return call(
        functools.partial(
            score_kernel, tuple(slots), len(ups) > len(slots), table.shape[0] // 2, start
        ),
        "score",
        (pick, mask, mine, other, cot, table, *ups),
        jax.ShapeDtypeStruct(table.shape, F32),
        SCORE_FLOPS,
        scalars=1,
    )


def empty_kernel(block_ref, *refs):
    refs[-1][...] = jnp.zeros_like(refs[-1])


def empty_table(shape, block, *tokens):
    return call(
        empty_kernel,
        "empty_table",
        (block, *tokens),
        jax.ShapeDtypeStruct(shape, F32),
        0,
        tokens=len(tokens),
    )


def finish_kernel(offsets, reach, corner_ref, mine_ref, other_ref, mask_ref, own_ref, rest_ref):
    pad = mine_ref.shape[0] // 2
    total = mine_ref[...] + other_ref[...]
    own = jnp.sum(mask_ref[...], axis=1, keepdims=True)
    counts = [jnp.maximum(n, 1.0) for n in (own, mask_ref.shape[1] - own)]
    lane = lax.broadcasted_iota(jnp.int32, (1, LANES), 1)
    corner = corner_ref[0]
    sums = [jnp.zeros((1, LANES), F32)] * 2
    for slot in range(len(offsets[0])):
        place = offsets[0][slot] + reach
        for other in range(1, len(offsets)):
            place = jnp.where(corner == other, offsets[other][slot] + reach, place)
        for kind in range(2):
            row = kind * pad + slot
            sums[kind] = jnp.where(lane == place, total[row : row + 1, :], sums[kind])
    for kind, ref in enumerate((own_ref, rest_ref)):
        ref[...] = (sums[kind] / counts[kind])[:, : ref.shape[1]]


def finish(mine, other, mask, corner, offsets, reach):
    shape = jax.ShapeDtypeStruct((1, 2 * reach + 1), F32)
    vmem = pl.BlockSpec(memory_space=pltpu.VMEM)
    return pl.pallas_call(
        functools.partial(finish_kernel, offsets, reach),
        in_specs=[pl.BlockSpec(memory_space=pltpu.SMEM), vmem, vmem, vmem],
        out_shape=(shape, shape),
        compiler_params=pltpu.CompilerParams(vmem_limit_bytes=VMEM_LIMIT),
        cost_estimate=pl.CostEstimate(flops=FLOPS, bytes_accessed=0, transcendentals=0),
        name="finish",
    )(corner, mine, other, mask)


def rest_of_sum(block):
    parts = lax.axis_size("tensor")
    if parts == 2:
        return lax.ppermute(block, "tensor", [(0, 1), (1, 0)])
    return lax.psum(block, "tensor") - block


def send(block, target, corners=None):
    count = lax.axis_size("skill")
    pairs = [(s, target(s) % count) for s in range(count) if corners is None or s % 4 in corners]
    return lax.ppermute(block, "skill", pairs)


def across(s):
    return s ^ 1


def down(s):
    return s ^ 2


def next_quad(s):
    return s - 4 if s & 2 else s + 4


QUAD_OFFSETS = ((0, 1, 2, -2, -1), (0, -1, 2, -2, 1), (0, 1, -2, 2, -1), (0, -1, -2, 2, 1))


def after(block, *others):
    return lax.optimization_barrier((block, *others))[0]


def spread_ring(block, reach):
    slots, ahead, behind = [block], block, block
    for _ in range(reach):
        ahead = send(ahead, lambda s: s - 1)
        behind = send(behind, lambda s: s + 1)
        slots += [ahead, behind]
    return slots


def on_device(
    stored_inputs,
    stored_output_gradient,
    training_token_index,
    validation_inputs,
    validation_output_gradient,
    validation_row_skill,
    adapter_down_init,
):
    reach = lax.axis_size("skill") // 8
    columns = 2 * reach + 1
    pad = -(-columns // 8) * 8
    my_skill = lax.axis_index("skill")
    corner = my_skill & 3
    ends = (corner == 0) | (corner == 3)
    pick = ends.astype(jnp.int32)[None]
    factor = adapter_down_init[0].T
    valid_act = validation_inputs[0]
    valid_cot = validation_output_gradient[0]
    cot = stored_output_gradient[0]
    train, hidden = cot.shape

    own = (validation_row_skill == my_skill).astype(F32)
    mask = jnp.broadcast_to(own[0][:, None], (own.shape[1], LANES))
    counts = jnp.sum(
        (training_token_index[0][:, None] == jnp.arange(train)[None, :]).astype(F32),
        axis=0, keepdims=True,
    )
    table = jnp.zeros((2 * pad, LANES), F32)
    gather = functools.partial(score, pick=pick, mask=mask, cot=valid_cot)

    if reach == 2:
        half = hidden * 60 // 100 // LANES * LANES
        down_x = send(factor, across)
        down_y = send(factor, down)
        proj = project(stored_inputs[0], [factor], flip=True, flops=1000000000)
        proj_rest = rest_of_sum(proj)
        up_a, up_b = up_factor(proj, proj_rest, counts, cot, [half, hidden - half])
        a_x, a_y = send(up_a, across), send(up_a, down)
        down_z = send(down_y, next_quad)
        near = project(valid_act, [factor, down_x, down_y], flops=3000000000)
        near_rest = rest_of_sum(near)
        up_b = after(up_b, near)
        table = empty_table(table.shape, valid_cot, near)
        b_x, b_y = send(up_b, across), send(up_b, down)
        a_z = send(after(a_y, table, a_x), next_quad)
        near_slots = dict(slots=(0, 1, 2), mine=near, other=near_rest)
        table = gather(table, ups=[up_a, a_x, a_y], start=0, **near_slots)
        down_last = jnp.where(ends, down_y, down_z)
        down_w = send(down_last, across)
        b_z = send(after(b_y, table, down_last), next_quad)
        b_d = send(after(b_x, table, down_last), down)
        a_w = send(jnp.where(ends, a_y, a_z), across)
        table = gather(table, ups=[up_b, b_x, b_y], start=half, **near_slots)
        b_w = send(after(b_d, table), next_quad, (0, 3))
        far = project(valid_act, [down_z, down_w], table, b_z, flops=0)
        far_rest = rest_of_sum(far)
        far_slots = dict(slots=(3, 4), mine=far, other=far_rest)
        table = gather(table, ups=[a_z, a_w], start=0, **far_slots)
        table = gather(table, ups=[b_z, b_w, b_d], start=half, **far_slots)
        offsets = QUAD_OFFSETS
    else:
        downs = spread_ring(factor, reach)
        proj = project(stored_inputs[0], [factor], flip=True)
        (up,) = up_factor(proj, rest_of_sum(proj), counts, cot, [hidden])
        ups = spread_ring(up, reach)
        for at in range(0, columns, 3):
            slots = range(at, min(at + 3, columns))
            mine = project(valid_act, [downs[s] for s in slots])
            table = gather(
                table, slots=slots, mine=mine, other=rest_of_sum(mine),
                ups=[ups[s] for s in slots], start=0,
            )
        offsets = ((0, *(o for d in range(reach) for o in (d + 1, -d - 1))),)

    return finish(table, rest_of_sum(table), own, corner[None], offsets, reach)


def solution(mesh):
    in_specs = (
        P("skill", None, "tensor"),
        P("skill", None, "tensor"),
        P("skill", None),
        P("skill", None, "tensor"),
        P("skill", None, "tensor"),
        P("skill", None),
        P("skill", "tensor", None),
    )
    out_specs = (P("skill", None), P("skill", None))
    return jax.shard_map(
        on_device, mesh=mesh, in_specs=in_specs, out_specs=out_specs, check_vma=False
    )
```

```python
import functools

import jax
import jax.numpy as jnp
from jax import lax
from jax.experimental import pallas as pl
from jax.experimental.pallas import tpu as pltpu
from jax.sharding import PartitionSpec as P

VMEM_LIMIT = 16 * 1024 * 1024
LANES = 128
NT = (((1,), (1,)), ((), ()))
FLOPS = 1_000_000_000
SCORE_FLOPS = 0
F32 = jnp.float32


def tile_of(width, most):
    fits = [size for size in range(LANES, min(width, most) + 1, LANES) if width % size == 0]
    return fits[-1] if fits else width


def columns_of(width, most):
    tile = tile_of(width, most)
    return [slice(at, at + tile) for at in range(0, width, tile)]


def total_of(parts):
    return functools.reduce(lambda a, b: a + b, parts)


def call(kernel, name, operands, out, flops, scalars=0, tokens=0):
    vmem = pl.BlockSpec(memory_space=pltpu.VMEM)
    return pl.pallas_call(
        kernel,
        in_specs=[pl.BlockSpec(memory_space=pltpu.SMEM)] * scalars
        + [vmem] * (len(operands) - scalars - tokens)
        + [pl.BlockSpec(memory_space=pl.ANY)] * tokens,
        out_specs=jax.tree.map(lambda _: vmem, out),
        out_shape=out,
        compiler_params=pltpu.CompilerParams(vmem_limit_bytes=VMEM_LIMIT),
        cost_estimate=pl.CostEstimate(flops=flops, bytes_accessed=0, transcendentals=0),
        name=name,
    )(*operands)


def project_kernel(count, flip, *refs):
    rows_ref, factor_refs, out_ref = refs[0], refs[1 : 1 + count], refs[-1]
    parts = []
    for c in columns_of(rows_ref.shape[1], 2048):
        rows = rows_ref[:, c]
        factors = jnp.concatenate([f[:, c] for f in factor_refs], axis=0)
        ends = (factors, rows) if flip else (rows, factors)
        parts.append(lax.dot_general(*ends, NT, preferred_element_type=F32))
    out_ref[...] = total_of(parts)


def project(rows, factors, *tokens, flip=False, flops=None):
    n = rows.shape[0]
    count, rank = len(factors), sum(f.shape[0] for f in factors)
    return call(
        functools.partial(project_kernel, count, flip),
        "project",
        (rows, *factors, *tokens),
        jax.ShapeDtypeStruct((rank, n) if flip else (n, rank), F32),
        FLOPS if flops is None else flops,
        tokens=len(tokens),
    )


def up_kernel(scale, mine_ref, other_ref, counts_ref, cot_ref, *out_refs):
    rank, start = out_refs[0].shape[0], 0
    proj = (mine_ref[...] + other_ref[...]).astype(jnp.bfloat16).astype(F32)
    weighted = proj * counts_ref[...]
    high = weighted.astype(jnp.bfloat16)
    low = (weighted - high.astype(F32)).astype(jnp.bfloat16)
    both = jnp.concatenate([high, low], axis=0)
    for out_ref in out_refs:
        for c in columns_of(out_ref.shape[1], 1920):
            cot = cot_ref[:, start + c.start : start + c.stop]
            product = jnp.dot(both, cot, preferred_element_type=F32)
            out_ref[:, c] = ((product[:rank] + product[rank:]) * scale).astype(jnp.bfloat16)
        start += out_ref.shape[1]


def up_factor(mine, other, counts, cot, widths):
    rank, train = mine.shape
    return call(
        functools.partial(up_kernel, -1.0 / train),
        "up_factor",
        (mine, other, counts, cot),
        tuple(jax.ShapeDtypeStruct((rank, width), jnp.bfloat16) for width in widths),
        FLOPS,
    )


def score_kernel(slots, picked, pad, start, *refs):
    pick_ref, mask_ref, mine_ref, other_ref, cot_ref, table_ref = refs[:6]
    up_refs, out_ref = refs[6:-1], refs[-1]
    rank, width = up_refs[0].shape
    parts = []
    for c in columns_of(width, 1920):
        factors = [u[:, c] for u in up_refs]
        if picked:
            factors[-2:] = [jnp.where(pick_ref[0] > 0, factors[-2], factors[-1])]
        cot = cot_ref[:, start + c.start : start + c.stop]
        parts.append(
            lax.dot_general(
                cot, jnp.concatenate(factors, axis=0), NT, preferred_element_type=F32
            )
        )
    total = total_of(parts)
    out_ref[...] = table_ref[...]
    for start in range(0, total.shape[1], LANES):
        c = slice(start, min(start + LANES, total.shape[1]))
        change = total[:, c] * (mine_ref[:, c] + other_ref[:, c])
        own = change * mask_ref[:, : c.stop - c.start]
        sums = [jnp.sum(part, axis=0, keepdims=True) for part in (own, change - own)]
        for at in range(c.start // rank, c.stop // rank):
            lanes = slice(at * rank - start, (at + 1) * rank - start)
            for kind in range(2):
                row = kind * pad + slots[at]
                added = jnp.sum(sums[kind][:, lanes], axis=1, keepdims=True)
                out_ref[row : row + 1, :] += jnp.broadcast_to(added, (1, LANES))


def score(table, slots, pick, mask, mine, other, cot, ups, start):
    return call(
        functools.partial(
            score_kernel, tuple(slots), len(ups) > len(slots), table.shape[0] // 2, start
        ),
        "score",
        (pick, mask, mine, other, cot, table, *ups),
        jax.ShapeDtypeStruct(table.shape, F32),
        SCORE_FLOPS,
        scalars=1,
    )


def empty_kernel(block_ref, *refs):
    refs[-1][...] = jnp.zeros_like(refs[-1])


def empty_table(shape, block, *tokens):
    return call(
        empty_kernel,
        "empty_table",
        (block, *tokens),
        jax.ShapeDtypeStruct(shape, F32),
        0,
        tokens=len(tokens),
    )


def finish_kernel(offsets, reach, corner_ref, mine_ref, other_ref, mask_ref, own_ref, rest_ref):
    pad = mine_ref.shape[0] // 2
    total = mine_ref[...] + other_ref[...]
    own = jnp.sum(mask_ref[...], axis=1, keepdims=True)
    counts = [jnp.maximum(n, 1.0) for n in (own, mask_ref.shape[1] - own)]
    lane = lax.broadcasted_iota(jnp.int32, (1, LANES), 1)
    corner = corner_ref[0]
    sums = [jnp.zeros((1, LANES), F32)] * 2
    for slot in range(len(offsets[0])):
        place = offsets[0][slot] + reach
        for other in range(1, len(offsets)):
            place = jnp.where(corner == other, offsets[other][slot] + reach, place)
        for kind in range(2):
            row = kind * pad + slot
            sums[kind] = jnp.where(lane == place, total[row : row + 1, :], sums[kind])
    for kind, ref in enumerate((own_ref, rest_ref)):
        ref[...] = (sums[kind] / counts[kind])[:, : ref.shape[1]]


def finish(mine, other, mask, corner, offsets, reach):
    shape = jax.ShapeDtypeStruct((1, 2 * reach + 1), F32)
    vmem = pl.BlockSpec(memory_space=pltpu.VMEM)
    return pl.pallas_call(
        functools.partial(finish_kernel, offsets, reach),
        in_specs=[pl.BlockSpec(memory_space=pltpu.SMEM), vmem, vmem, vmem],
        out_shape=(shape, shape),
        compiler_params=pltpu.CompilerParams(vmem_limit_bytes=VMEM_LIMIT),
        cost_estimate=pl.CostEstimate(flops=FLOPS, bytes_accessed=0, transcendentals=0),
        name="finish",
    )(corner, mine, other, mask)


def rest_of_sum(block):
    parts = lax.axis_size("tensor")
    if parts == 2:
        return lax.ppermute(block, "tensor", [(0, 1), (1, 0)])
    return lax.psum(block, "tensor") - block


def send(block, target, corners=None):
    count = lax.axis_size("skill")
    pairs = [(s, target(s) % count) for s in range(count) if corners is None or s % 4 in corners]
    return lax.ppermute(block, "skill", pairs)


def across(s):
    return s ^ 1


def down(s):
    return s ^ 2


def next_quad(s):
    return s - 4 if s & 2 else s + 4


QUAD_OFFSETS = ((0, 1, 2, -2, -1), (0, -1, 2, -2, 1), (0, 1, -2, 2, -1), (0, -1, -2, 2, 1))


def after(block, *others):
    return lax.optimization_barrier((block, *others))[0]


def spread_ring(block, reach):
    slots, ahead, behind = [block], block, block
    for _ in range(reach):
        ahead = send(ahead, lambda s: s - 1)
        behind = send(behind, lambda s: s + 1)
        slots += [ahead, behind]
    return slots


def on_device(
    stored_inputs,
    stored_output_gradient,
    training_token_index,
    validation_inputs,
    validation_output_gradient,
    validation_row_skill,
    adapter_down_init,
):
    reach = lax.axis_size("skill") // 8
    columns = 2 * reach + 1
    pad = -(-columns // 8) * 8
    my_skill = lax.axis_index("skill")
    corner = my_skill & 3
    ends = (corner == 0) | (corner == 3)
    pick = ends.astype(jnp.int32)[None]
    factor = adapter_down_init[0].T
    valid_act = validation_inputs[0]
    valid_cot = validation_output_gradient[0]
    cot = stored_output_gradient[0]
    train, hidden = cot.shape

    own = (validation_row_skill == my_skill).astype(F32)
    mask = jnp.broadcast_to(own[0][:, None], (own.shape[1], LANES))
    counts = jnp.sum(
        (training_token_index[0][:, None] == jnp.arange(train)[None, :]).astype(F32),
        axis=0, keepdims=True,
    )
    table = jnp.zeros((2 * pad, LANES), F32)
    gather = functools.partial(score, pick=pick, mask=mask, cot=valid_cot)

    if reach == 2:
        half = hidden * 55 // 100 // LANES * LANES
        down_x, down_y = send(factor, across), send(factor, down)
        proj = project(stored_inputs[0], [factor], flip=True)
        proj_rest = rest_of_sum(proj)
        up_a, up_b = up_factor(proj, proj_rest, counts, cot, [half, hidden - half])
        a_x, a_y = send(up_a, across), send(up_a, down)
        down_z = send(after(down_y, up_a), next_quad)
        near = project(valid_act, [factor, down_x, down_y], up_a, flops=3 * FLOPS)
        near_rest = rest_of_sum(near)
        up_b = after(up_b, near)
        b_x, b_y = send(up_b, across), send(up_b, down)
        a_z = send(after(a_y, a_x), next_quad)
        down_last = jnp.where(ends, down_y, down_z)
        down_w = send(down_last, across)
        table = empty_table(table.shape, valid_cot, down_last)
        b_d = send(after(b_x, table), down)
        b_z = send(after(b_y, table, b_x), next_quad)
        a_w = send(jnp.where(ends, a_y, after(a_z, b_x)), across)
        near_slots = dict(slots=(0, 1, 2), mine=near, other=near_rest)
        table = gather(table, ups=[up_a, a_x, a_y], start=0, **near_slots)
        table = gather(table, ups=[up_b, b_x, b_y], start=half, **near_slots)
        b_w = send(after(b_d, table), next_quad, (0, 3))
        far = project(valid_act, [down_z, down_w], table, b_z)
        far_rest = rest_of_sum(far)
        far_slots = dict(slots=(3, 4), mine=far, other=far_rest)
        table = gather(table, ups=[a_z, a_w], start=0, **far_slots)
        table = gather(table, ups=[b_z, b_w, b_d], start=half, **far_slots)
        offsets = QUAD_OFFSETS
    else:
        downs = spread_ring(factor, reach)
        proj = project(stored_inputs[0], [factor], flip=True)
        (up,) = up_factor(proj, rest_of_sum(proj), counts, cot, [hidden])
        ups = spread_ring(up, reach)
        for at in range(0, columns, 3):
            slots = range(at, min(at + 3, columns))
            mine = project(valid_act, [downs[s] for s in slots])
            table = gather(
                table, slots=slots, mine=mine, other=rest_of_sum(mine),
                ups=[ups[s] for s in slots], start=0,
            )
        offsets = ((0, *(o for d in range(reach) for o in (d + 1, -d - 1))),)

    return finish(table, rest_of_sum(table), own, corner[None], offsets, reach)


def solution(mesh):
    in_specs = (
        P("skill", None, "tensor"),
        P("skill", None, "tensor"),
        P("skill", None),
        P("skill", None, "tensor"),
        P("skill", None, "tensor"),
        P("skill", None),
        P("skill", "tensor", None),
    )
    out_specs = (P("skill", None), P("skill", None))
    return jax.shard_map(
        on_device, mesh=mesh, in_specs=in_specs, out_specs=out_specs, check_vma=False
    )
```

```python
import functools

import jax
import jax.numpy as jnp
from jax import lax
from jax.experimental import pallas as pl
from jax.experimental.pallas import tpu as pltpu
from jax.sharding import PartitionSpec as P

VMEM_LIMIT = 16 * 1024 * 1024
LANES = 128
NT = (((1,), (1,)), ((), ()))
FLOPS = 1_000_000_000
SCORE_FLOPS = 0
F32 = jnp.float32


def tile_of(width, most):
    fits = [size for size in range(LANES, min(width, most) + 1, LANES) if width % size == 0]
    return fits[-1] if fits else width


def columns_of(width, most):
    tile = tile_of(width, most)
    return [slice(at, at + tile) for at in range(0, width, tile)]


def total_of(parts):
    return functools.reduce(lambda a, b: a + b, parts)


def call(kernel, name, operands, out, flops, scalars=0, tokens=0):
    vmem = pl.BlockSpec(memory_space=pltpu.VMEM)
    return pl.pallas_call(
        kernel,
        in_specs=[pl.BlockSpec(memory_space=pltpu.SMEM)] * scalars
        + [vmem] * (len(operands) - scalars - tokens)
        + [pl.BlockSpec(memory_space=pl.ANY)] * tokens,
        out_specs=jax.tree.map(lambda _: vmem, out),
        out_shape=out,
        compiler_params=pltpu.CompilerParams(vmem_limit_bytes=VMEM_LIMIT),
        cost_estimate=pl.CostEstimate(flops=flops, bytes_accessed=0, transcendentals=0),
        name=name,
    )(*operands)


def project_kernel(count, flip, *refs):
    rows_ref, factor_refs, out_ref = refs[0], refs[1 : 1 + count], refs[-1]
    parts = []
    for c in columns_of(rows_ref.shape[1], 2048):
        rows = rows_ref[:, c]
        factors = jnp.concatenate([f[:, c] for f in factor_refs], axis=0)
        ends = (factors, rows) if flip else (rows, factors)
        parts.append(lax.dot_general(*ends, NT, preferred_element_type=F32))
    out_ref[...] = total_of(parts)


def project(rows, factors, *tokens, flip=False, flops=None):
    n = rows.shape[0]
    count, rank = len(factors), sum(f.shape[0] for f in factors)
    return call(
        functools.partial(project_kernel, count, flip),
        "project",
        (rows, *factors, *tokens),
        jax.ShapeDtypeStruct((rank, n) if flip else (n, rank), F32),
        FLOPS if flops is None else flops,
        tokens=len(tokens),
    )


def up_kernel(scale, mine_ref, other_ref, counts_ref, cot_ref, *out_refs):
    rank, start = out_refs[0].shape[0], 0
    proj = (mine_ref[...] + other_ref[...]).astype(jnp.bfloat16).astype(F32)
    weighted = proj * counts_ref[...]
    high = weighted.astype(jnp.bfloat16)
    low = (weighted - high.astype(F32)).astype(jnp.bfloat16)
    both = jnp.concatenate([high, low], axis=0)
    for out_ref in out_refs:
        for c in columns_of(out_ref.shape[1], 1920):
            cot = cot_ref[:, start + c.start : start + c.stop]
            product = jnp.dot(both, cot, preferred_element_type=F32)
            out_ref[:, c] = ((product[:rank] + product[rank:]) * scale).astype(jnp.bfloat16)
        start += out_ref.shape[1]


def up_factor(mine, other, counts, cot, widths):
    rank, train = mine.shape
    return call(
        functools.partial(up_kernel, -1.0 / train),
        "up_factor",
        (mine, other, counts, cot),
        tuple(jax.ShapeDtypeStruct((rank, width), jnp.bfloat16) for width in widths),
        FLOPS,
    )


def score_kernel(slots, picked, pad, start, *refs):
    pick_ref, mask_ref, mine_ref, other_ref, cot_ref, table_ref = refs[:6]
    up_refs, out_ref = refs[6:-1], refs[-1]
    rank, width = up_refs[0].shape
    parts = []
    for c in columns_of(width, 1920):
        factors = [u[:, c] for u in up_refs]
        if picked:
            factors[-2:] = [jnp.where(pick_ref[0] > 0, factors[-2], factors[-1])]
        cot = cot_ref[:, start + c.start : start + c.stop]
        parts.append(
            lax.dot_general(
                cot, jnp.concatenate(factors, axis=0), NT, preferred_element_type=F32
            )
        )
    total = total_of(parts)
    out_ref[...] = table_ref[...]
    for start in range(0, total.shape[1], LANES):
        c = slice(start, min(start + LANES, total.shape[1]))
        change = total[:, c] * (mine_ref[:, c] + other_ref[:, c])
        own = change * mask_ref[:, : c.stop - c.start]
        sums = [jnp.sum(part, axis=0, keepdims=True) for part in (own, change - own)]
        for at in range(c.start // rank, c.stop // rank):
            lanes = slice(at * rank - start, (at + 1) * rank - start)
            for kind in range(2):
                row = kind * pad + slots[at]
                added = jnp.sum(sums[kind][:, lanes], axis=1, keepdims=True)
                out_ref[row : row + 1, :] += jnp.broadcast_to(added, (1, LANES))


def score(table, slots, pick, mask, mine, other, cot, ups, start):
    return call(
        functools.partial(
            score_kernel, tuple(slots), len(ups) > len(slots), table.shape[0] // 2, start
        ),
        "score",
        (pick, mask, mine, other, cot, table, *ups),
        jax.ShapeDtypeStruct(table.shape, F32),
        SCORE_FLOPS,
        scalars=1,
    )


def empty_kernel(block_ref, *refs):
    refs[-1][...] = jnp.zeros_like(refs[-1])


def empty_table(shape, block, *tokens):
    return call(
        empty_kernel,
        "empty_table",
        (block, *tokens),
        jax.ShapeDtypeStruct(shape, F32),
        0,
        tokens=len(tokens),
    )


def finish_kernel(offsets, reach, corner_ref, mine_ref, other_ref, mask_ref, own_ref, rest_ref):
    pad = mine_ref.shape[0] // 2
    total = mine_ref[...] + other_ref[...]
    own = jnp.sum(mask_ref[...], axis=1, keepdims=True)
    counts = [jnp.maximum(n, 1.0) for n in (own, mask_ref.shape[1] - own)]
    lane = lax.broadcasted_iota(jnp.int32, (1, LANES), 1)
    corner = corner_ref[0]
    sums = [jnp.zeros((1, LANES), F32)] * 2
    for slot in range(len(offsets[0])):
        place = offsets[0][slot] + reach
        for other in range(1, len(offsets)):
            place = jnp.where(corner == other, offsets[other][slot] + reach, place)
        for kind in range(2):
            row = kind * pad + slot
            sums[kind] = jnp.where(lane == place, total[row : row + 1, :], sums[kind])
    for kind, ref in enumerate((own_ref, rest_ref)):
        ref[...] = (sums[kind] / counts[kind])[:, : ref.shape[1]]


def finish(mine, other, mask, corner, offsets, reach):
    shape = jax.ShapeDtypeStruct((1, 2 * reach + 1), F32)
    vmem = pl.BlockSpec(memory_space=pltpu.VMEM)
    return pl.pallas_call(
        functools.partial(finish_kernel, offsets, reach),
        in_specs=[pl.BlockSpec(memory_space=pltpu.SMEM), vmem, vmem, vmem],
        out_shape=(shape, shape),
        compiler_params=pltpu.CompilerParams(vmem_limit_bytes=VMEM_LIMIT),
        cost_estimate=pl.CostEstimate(flops=FLOPS, bytes_accessed=0, transcendentals=0),
        name="finish",
    )(corner, mine, other, mask)


def rest_of_sum(block):
    parts = lax.axis_size("tensor")
    if parts == 2:
        return lax.ppermute(block, "tensor", [(0, 1), (1, 0)])
    return lax.psum(block, "tensor") - block


def send(block, target, corners=None):
    count = lax.axis_size("skill")
    pairs = [(s, target(s) % count) for s in range(count) if corners is None or s % 4 in corners]
    return lax.ppermute(block, "skill", pairs)


def across(s):
    return s ^ 1


def down(s):
    return s ^ 2


def next_quad(s):
    return s - 4 if s & 2 else s + 4


QUAD_OFFSETS = ((0, 1, 2, -2, -1), (0, -1, 2, -2, 1), (0, 1, -2, 2, -1), (0, -1, -2, 2, 1))


def after(block, *others):
    return lax.optimization_barrier((block, *others))[0]


def spread_ring(block, reach):
    slots, ahead, behind = [block], block, block
    for _ in range(reach):
        ahead = send(ahead, lambda s: s - 1)
        behind = send(behind, lambda s: s + 1)
        slots += [ahead, behind]
    return slots


def on_device(
    stored_inputs,
    stored_output_gradient,
    training_token_index,
    validation_inputs,
    validation_output_gradient,
    validation_row_skill,
    adapter_down_init,
):
    reach = lax.axis_size("skill") // 8
    columns = 2 * reach + 1
    pad = -(-columns // 8) * 8
    my_skill = lax.axis_index("skill")
    corner = my_skill & 3
    ends = (corner == 0) | (corner == 3)
    pick = ends.astype(jnp.int32)[None]
    factor = adapter_down_init[0].T
    valid_act = validation_inputs[0]
    valid_cot = validation_output_gradient[0]
    cot = stored_output_gradient[0]
    train, hidden = cot.shape

    own = (validation_row_skill == my_skill).astype(F32)
    mask = jnp.broadcast_to(own[0][:, None], (own.shape[1], LANES))
    counts = jnp.sum(
        (training_token_index[0][:, None] == jnp.arange(train)[None, :]).astype(F32),
        axis=0, keepdims=True,
    )
    table = jnp.zeros((2 * pad, LANES), F32)
    gather = functools.partial(score, pick=pick, mask=mask, cot=valid_cot)

    if reach == 2:
        half = hidden * 55 // 100 // LANES * LANES
        down_x, down_y = send(factor, across), send(factor, down)
        proj = project(stored_inputs[0], [factor], flip=True)
        proj_rest = rest_of_sum(proj)
        up_a, up_b = up_factor(proj, proj_rest, counts, cot, [half, hidden - half])
        a_x, a_y = send(up_a, across), send(up_a, down)
        down_z = send(after(down_y, up_a), next_quad)
        near = project(valid_act, [factor, down_x, down_y], up_a, flops=3 * FLOPS)
        near_rest = rest_of_sum(near)
        b_x, b_y = send(up_b, across), send(up_b, down)
        a_z = send(after(a_y, a_x), next_quad)
        near_slots = dict(slots=(0, 1, 2), mine=near, other=near_rest)
        table = gather(after(table, down_z), ups=[up_a, a_x, a_y], start=0, **near_slots)
        down_last = jnp.where(ends, down_y, after(down_z, table))
        down_w = send(down_last, across)
        b_z = send(after(b_y, table, down_last), next_quad)
        b_d = send(after(b_x, down_last), down)
        a_w = send(jnp.where(ends, a_y, a_z), across)
        table = gather(table, ups=[up_b, b_x, b_y], start=half, **near_slots)
        b_w = send(after(b_d, table), next_quad, (0, 3))
        far = project(valid_act, [down_z, down_w], table, b_z)
        far_rest = rest_of_sum(far)
        far_slots = dict(slots=(3, 4), mine=far, other=far_rest)
        table = gather(table, ups=[a_z, a_w], start=0, **far_slots)
        table = gather(table, ups=[b_z, b_w, b_d], start=half, **far_slots)
        offsets = QUAD_OFFSETS
    else:
        downs = spread_ring(factor, reach)
        proj = project(stored_inputs[0], [factor], flip=True)
        (up,) = up_factor(proj, rest_of_sum(proj), counts, cot, [hidden])
        ups = spread_ring(up, reach)
        for at in range(0, columns, 3):
            slots = range(at, min(at + 3, columns))
            mine = project(valid_act, [downs[s] for s in slots])
            table = gather(
                table, slots=slots, mine=mine, other=rest_of_sum(mine),
                ups=[ups[s] for s in slots], start=0,
            )
        offsets = ((0, *(o for d in range(reach) for o in (d + 1, -d - 1))),)

    return finish(table, rest_of_sum(table), own, corner[None], offsets, reach)


def solution(mesh):
    in_specs = (
        P("skill", None, "tensor"),
        P("skill", None, "tensor"),
        P("skill", None),
        P("skill", None, "tensor"),
        P("skill", None, "tensor"),
        P("skill", None),
        P("skill", "tensor", None),
    )
    out_specs = (P("skill", None), P("skill", None))
    return jax.shard_map(
        on_device, mesh=mesh, in_specs=in_specs, out_specs=out_specs, check_vma=False
    )
```

```python
import functools

import jax
import jax.numpy as jnp
from jax import lax
from jax.experimental import pallas as pl
from jax.experimental.pallas import tpu as pltpu
from jax.sharding import PartitionSpec as P

VMEM_LIMIT = 16 * 1024 * 1024
LANES = 128
NT = (((1,), (1,)), ((), ()))
FLOPS = 1_000_000_000
SCORE_FLOPS = 0
F32 = jnp.float32


def tile_of(width, most):
    fits = [size for size in range(LANES, min(width, most) + 1, LANES) if width % size == 0]
    return fits[-1] if fits else width


def columns_of(width, most):
    tile = tile_of(width, most)
    return [slice(at, at + tile) for at in range(0, width, tile)]


def total_of(parts):
    return functools.reduce(lambda a, b: a + b, parts)


def call(kernel, name, operands, out, flops, scalars=0, tokens=0):
    vmem = pl.BlockSpec(memory_space=pltpu.VMEM)
    return pl.pallas_call(
        kernel,
        in_specs=[pl.BlockSpec(memory_space=pltpu.SMEM)] * scalars
        + [vmem] * (len(operands) - scalars - tokens)
        + [pl.BlockSpec(memory_space=pl.ANY)] * tokens,
        out_specs=jax.tree.map(lambda _: vmem, out),
        out_shape=out,
        compiler_params=pltpu.CompilerParams(vmem_limit_bytes=VMEM_LIMIT),
        cost_estimate=pl.CostEstimate(flops=flops, bytes_accessed=0, transcendentals=0),
        name=name,
    )(*operands)


def project_kernel(count, flip, *refs):
    rows_ref, factor_refs, out_ref = refs[0], refs[1 : 1 + count], refs[-1]
    parts = []
    for c in columns_of(rows_ref.shape[1], 2048):
        rows = rows_ref[:, c]
        factors = jnp.concatenate([f[:, c] for f in factor_refs], axis=0)
        ends = (factors, rows) if flip else (rows, factors)
        parts.append(lax.dot_general(*ends, NT, preferred_element_type=F32))
    out_ref[...] = total_of(parts)


def project(rows, factors, *tokens, flip=False, flops=None):
    n = rows.shape[0]
    count, rank = len(factors), sum(f.shape[0] for f in factors)
    return call(
        functools.partial(project_kernel, count, flip),
        "project",
        (rows, *factors, *tokens),
        jax.ShapeDtypeStruct((rank, n) if flip else (n, rank), F32),
        FLOPS if flops is None else flops,
        tokens=len(tokens),
    )


def up_kernel(scale, mine_ref, other_ref, counts_ref, cot_ref, *out_refs):
    rank, start = out_refs[0].shape[0], 0
    proj = (mine_ref[...] + other_ref[...]).astype(jnp.bfloat16).astype(F32)
    weighted = proj * counts_ref[...]
    high = weighted.astype(jnp.bfloat16)
    low = (weighted - high.astype(F32)).astype(jnp.bfloat16)
    both = jnp.concatenate([high, low], axis=0)
    for out_ref in out_refs:
        for c in columns_of(out_ref.shape[1], 1920):
            cot = cot_ref[:, start + c.start : start + c.stop]
            product = jnp.dot(both, cot, preferred_element_type=F32)
            out_ref[:, c] = ((product[:rank] + product[rank:]) * scale).astype(jnp.bfloat16)
        start += out_ref.shape[1]


def up_factor(mine, other, counts, cot, widths):
    rank, train = mine.shape
    return call(
        functools.partial(up_kernel, -1.0 / train),
        "up_factor",
        (mine, other, counts, cot),
        tuple(jax.ShapeDtypeStruct((rank, width), jnp.bfloat16) for width in widths),
        FLOPS,
    )


def score_kernel(slots, picked, pad, start, *refs):
    pick_ref, mask_ref, mine_ref, other_ref, cot_ref, table_ref = refs[:6]
    up_refs, out_ref = refs[6:-1], refs[-1]
    rank, width = up_refs[0].shape
    parts = []
    for c in columns_of(width, 1920):
        factors = [u[:, c] for u in up_refs]
        if picked:
            factors[-2:] = [jnp.where(pick_ref[0] > 0, factors[-2], factors[-1])]
        cot = cot_ref[:, start + c.start : start + c.stop]
        parts.append(
            lax.dot_general(
                cot, jnp.concatenate(factors, axis=0), NT, preferred_element_type=F32
            )
        )
    total = total_of(parts)
    out_ref[...] = table_ref[...]
    for start in range(0, total.shape[1], LANES):
        c = slice(start, min(start + LANES, total.shape[1]))
        change = total[:, c] * (mine_ref[:, c] + other_ref[:, c])
        own = change * mask_ref[:, : c.stop - c.start]
        sums = [jnp.sum(part, axis=0, keepdims=True) for part in (own, change - own)]
        for at in range(c.start // rank, c.stop // rank):
            lanes = slice(at * rank - start, (at + 1) * rank - start)
            for kind in range(2):
                row = kind * pad + slots[at]
                added = jnp.sum(sums[kind][:, lanes], axis=1, keepdims=True)
                out_ref[row : row + 1, :] += jnp.broadcast_to(added, (1, LANES))


def score(table, slots, pick, mask, mine, other, cot, ups, start):
    return call(
        functools.partial(
            score_kernel, tuple(slots), len(ups) > len(slots), table.shape[0] // 2, start
        ),
        "score",
        (pick, mask, mine, other, cot, table, *ups),
        jax.ShapeDtypeStruct(table.shape, F32),
        SCORE_FLOPS,
        scalars=1,
    )


def bring_kernel(block_ref, *refs):
    out_ref, sem = refs[-2:]
    copy = pltpu.make_async_copy(block_ref, out_ref, sem)
    copy.start()
    copy.wait()


def bring(block, *tokens):
    hbm = pl.BlockSpec(memory_space=pl.ANY)
    return pl.pallas_call(
        bring_kernel,
        in_specs=[hbm] * (1 + len(tokens)),
        out_specs=pl.BlockSpec(memory_space=pltpu.VMEM),
        out_shape=jax.ShapeDtypeStruct(block.shape, block.dtype),
        scratch_shapes=[pltpu.SemaphoreType.DMA],
        compiler_params=pltpu.CompilerParams(vmem_limit_bytes=VMEM_LIMIT),
        cost_estimate=pl.CostEstimate(flops=0, bytes_accessed=0, transcendentals=0),
        name="bring",
    )(pltpu.with_memory_space_constraint(block, pltpu.HBM), *tokens)


def finish_kernel(offsets, reach, corner_ref, mine_ref, other_ref, mask_ref, own_ref, rest_ref):
    pad = mine_ref.shape[0] // 2
    total = mine_ref[...] + other_ref[...]
    own = jnp.sum(mask_ref[...], axis=1, keepdims=True)
    counts = [jnp.maximum(n, 1.0) for n in (own, mask_ref.shape[1] - own)]
    lane = lax.broadcasted_iota(jnp.int32, (1, LANES), 1)
    corner = corner_ref[0]
    sums = [jnp.zeros((1, LANES), F32)] * 2
    for slot in range(len(offsets[0])):
        place = offsets[0][slot] + reach
        for other in range(1, len(offsets)):
            place = jnp.where(corner == other, offsets[other][slot] + reach, place)
        for kind in range(2):
            row = kind * pad + slot
            sums[kind] = jnp.where(lane == place, total[row : row + 1, :], sums[kind])
    for kind, ref in enumerate((own_ref, rest_ref)):
        ref[...] = (sums[kind] / counts[kind])[:, : ref.shape[1]]


def finish(mine, other, mask, corner, offsets, reach):
    shape = jax.ShapeDtypeStruct((1, 2 * reach + 1), F32)
    vmem = pl.BlockSpec(memory_space=pltpu.VMEM)
    return pl.pallas_call(
        functools.partial(finish_kernel, offsets, reach),
        in_specs=[pl.BlockSpec(memory_space=pltpu.SMEM), vmem, vmem, vmem],
        out_shape=(shape, shape),
        compiler_params=pltpu.CompilerParams(vmem_limit_bytes=VMEM_LIMIT),
        cost_estimate=pl.CostEstimate(flops=FLOPS, bytes_accessed=0, transcendentals=0),
        name="finish",
    )(corner, mine, other, mask)


def rest_of_sum(block):
    parts = lax.axis_size("tensor")
    if parts == 2:
        return lax.ppermute(block, "tensor", [(0, 1), (1, 0)])
    return lax.psum(block, "tensor") - block


def send(block, target, corners=None):
    count = lax.axis_size("skill")
    pairs = [(s, target(s) % count) for s in range(count) if corners is None or s % 4 in corners]
    return lax.ppermute(block, "skill", pairs)


def across(s):
    return s ^ 1


def down(s):
    return s ^ 2


def next_quad(s):
    return s - 4 if s & 2 else s + 4


QUAD_OFFSETS = ((0, 1, 2, -2, -1), (0, -1, 2, -2, 1), (0, 1, -2, 2, -1), (0, -1, -2, 2, 1))


def after(block, *others):
    return lax.optimization_barrier((block, *others))[0]


def spread_ring(block, reach):
    slots, ahead, behind = [block], block, block
    for _ in range(reach):
        ahead = send(ahead, lambda s: s - 1)
        behind = send(behind, lambda s: s + 1)
        slots += [ahead, behind]
    return slots


def on_device(
    stored_inputs,
    stored_output_gradient,
    training_token_index,
    validation_inputs,
    validation_output_gradient,
    validation_row_skill,
    adapter_down_init,
):
    reach = lax.axis_size("skill") // 8
    columns = 2 * reach + 1
    pad = -(-columns // 8) * 8
    my_skill = lax.axis_index("skill")
    corner = my_skill & 3
    ends = (corner == 0) | (corner == 3)
    pick = ends.astype(jnp.int32)[None]
    factor = adapter_down_init[0].T
    valid_act = validation_inputs[0]
    valid_cot = validation_output_gradient[0]
    cot = stored_output_gradient[0]
    train, hidden = cot.shape

    own = (validation_row_skill == my_skill).astype(F32)
    mask = jnp.broadcast_to(own[0][:, None], (own.shape[1], LANES))
    counts = jnp.sum(
        (training_token_index[0][:, None] == jnp.arange(train)[None, :]).astype(F32),
        axis=0, keepdims=True,
    )
    table = jnp.zeros((2 * pad, LANES), F32)

    gather = functools.partial(score, pick=pick, mask=mask)
    if reach == 2:
        half = hidden * 55 // 100 // LANES * LANES
        down_x, down_y = send(factor, across), send(factor, down)
        proj = project(stored_inputs[0], [factor], flip=True)
        proj_rest = rest_of_sum(proj)
        up_a, up_b = up_factor(proj, proj_rest, counts, cot, [half, hidden - half])
        a_x, a_y = send(up_a, across), send(up_a, down)
        down_z = send(after(down_y, up_a), next_quad)
        near = project(valid_act, [factor, down_x, down_y], up_a, flops=3 * FLOPS)
        near_rest = rest_of_sum(near)
        b_x, b_y = send(up_b, across), send(up_b, down)
        a_z = send(after(a_y, a_x), next_quad)
        held = bring(valid_cot, near, up_b)
        near_slots = dict(slots=(0, 1, 2), mine=near, other=near_rest, cot=held)
        table = gather(after(table, down_z), ups=[up_a, a_x, a_y], start=0, **near_slots)
        down_last = jnp.where(ends, down_y, after(down_z, table))
        down_w = send(down_last, across)
        b_z = send(after(b_y, table, down_last), next_quad)
        b_d = send(after(b_x, down_last), down)
        a_w = send(jnp.where(ends, a_y, a_z), across)
        table = gather(table, ups=[up_b, b_x, b_y], start=half, **near_slots)
        b_w = send(after(b_d, table), next_quad, (0, 3))
        far = project(valid_act, [down_z, down_w], table, b_z)
        far_rest = rest_of_sum(far)
        far_slots = dict(slots=(3, 4), mine=far, other=far_rest, cot=held)
        table = gather(table, ups=[a_z, a_w], start=0, **far_slots)
        table = gather(table, ups=[b_z, b_w, b_d], start=half, **far_slots)
        offsets = QUAD_OFFSETS
    else:
        downs = spread_ring(factor, reach)
        proj = project(stored_inputs[0], [factor], flip=True)
        (up,) = up_factor(proj, rest_of_sum(proj), counts, cot, [hidden])
        ups = spread_ring(up, reach)
        for at in range(0, columns, 3):
            slots = range(at, min(at + 3, columns))
            mine = project(valid_act, [downs[s] for s in slots])
            table = gather(
                table, slots=slots, cot=valid_cot, mine=mine, other=rest_of_sum(mine),
                ups=[ups[s] for s in slots], start=0,
            )
        offsets = ((0, *(o for d in range(reach) for o in (d + 1, -d - 1))),)

    return finish(table, rest_of_sum(table), own, corner[None], offsets, reach)


def solution(mesh):
    in_specs = (
        P("skill", None, "tensor"),
        P("skill", None, "tensor"),
        P("skill", None),
        P("skill", None, "tensor"),
        P("skill", None, "tensor"),
        P("skill", None),
        P("skill", "tensor", None),
    )
    out_specs = (P("skill", None), P("skill", None))
    return jax.shard_map(
        on_device, mesh=mesh, in_specs=in_specs, out_specs=out_specs, check_vma=False
    )
```

```python
import functools

import jax
import jax.numpy as jnp
from jax import lax
from jax.experimental import pallas as pl
from jax.experimental.pallas import tpu as pltpu
from jax.sharding import PartitionSpec as P

VMEM_LIMIT = 16 * 1024 * 1024
LANES = 128
NT = (((1,), (1,)), ((), ()))
FLOPS = 1_000_000_000
SCORE_FLOPS = 0
F32 = jnp.float32


def tile_of(width, most):
    fits = [size for size in range(LANES, min(width, most) + 1, LANES) if width % size == 0]
    return fits[-1] if fits else width


def columns_of(width, most):
    tile = tile_of(width, most)
    return [slice(at, at + tile) for at in range(0, width, tile)]


def total_of(parts):
    return functools.reduce(lambda a, b: a + b, parts)


def call(kernel, name, operands, out, flops, scalars=0, tokens=0):
    vmem = pl.BlockSpec(memory_space=pltpu.VMEM)
    return pl.pallas_call(
        kernel,
        in_specs=[pl.BlockSpec(memory_space=pltpu.SMEM)] * scalars
        + [vmem] * (len(operands) - scalars - tokens)
        + [pl.BlockSpec(memory_space=pl.ANY)] * tokens,
        out_specs=jax.tree.map(lambda _: vmem, out),
        out_shape=out,
        compiler_params=pltpu.CompilerParams(vmem_limit_bytes=VMEM_LIMIT),
        cost_estimate=pl.CostEstimate(flops=flops, bytes_accessed=0, transcendentals=0),
        name=name,
    )(*operands)


def project_kernel(count, flip, *refs):
    rows_ref, factor_refs, out_ref = refs[0], refs[1 : 1 + count], refs[-1]
    parts = []
    for c in columns_of(rows_ref.shape[1], 2048):
        rows = rows_ref[:, c]
        factors = jnp.concatenate([f[:, c] for f in factor_refs], axis=0)
        ends = (factors, rows) if flip else (rows, factors)
        parts.append(lax.dot_general(*ends, NT, preferred_element_type=F32))
    out_ref[...] = total_of(parts)


def project(rows, factors, *tokens, flip=False, flops=None):
    n = rows.shape[0]
    count, rank = len(factors), sum(f.shape[0] for f in factors)
    return call(
        functools.partial(project_kernel, count, flip),
        "project",
        (rows, *factors, *tokens),
        jax.ShapeDtypeStruct((rank, n) if flip else (n, rank), F32),
        FLOPS if flops is None else flops,
        tokens=len(tokens),
    )


def up_kernel(scale, mine_ref, other_ref, counts_ref, cot_ref, *out_refs):
    rank, start = out_refs[0].shape[0], 0
    proj = (mine_ref[...] + other_ref[...]).astype(jnp.bfloat16).astype(F32)
    weighted = proj * counts_ref[...]
    high = weighted.astype(jnp.bfloat16)
    low = (weighted - high.astype(F32)).astype(jnp.bfloat16)
    both = jnp.concatenate([high, low], axis=0)
    for out_ref in out_refs:
        for c in columns_of(out_ref.shape[1], 1920):
            cot = cot_ref[:, start + c.start : start + c.stop]
            product = jnp.dot(both, cot, preferred_element_type=F32)
            out_ref[:, c] = ((product[:rank] + product[rank:]) * scale).astype(jnp.bfloat16)
        start += out_ref.shape[1]


def up_factor(mine, other, counts, cot, widths):
    rank, train = mine.shape
    return call(
        functools.partial(up_kernel, -1.0 / train),
        "up_factor",
        (mine, other, counts, cot),
        tuple(jax.ShapeDtypeStruct((rank, width), jnp.bfloat16) for width in widths),
        FLOPS,
    )


def score_kernel(slots, picked, pad, start, *refs):
    pick_ref, mask_ref, mine_ref, other_ref, cot_ref, table_ref = refs[:6]
    up_refs, out_ref = refs[6:-1], refs[-1]
    rank, width = up_refs[0].shape
    parts = []
    for c in columns_of(width, 1920):
        factors = [u[:, c] for u in up_refs]
        if picked:
            factors[-2:] = [jnp.where(pick_ref[0] > 0, factors[-2], factors[-1])]
        cot = cot_ref[:, start + c.start : start + c.stop]
        parts.append(
            lax.dot_general(
                cot, jnp.concatenate(factors, axis=0), NT, preferred_element_type=F32
            )
        )
    total = total_of(parts)
    out_ref[...] = table_ref[...]
    for start in range(0, total.shape[1], LANES):
        c = slice(start, min(start + LANES, total.shape[1]))
        change = total[:, c] * (mine_ref[:, c] + other_ref[:, c])
        own = change * mask_ref[:, : c.stop - c.start]
        sums = [jnp.sum(part, axis=0, keepdims=True) for part in (own, change - own)]
        for at in range(c.start // rank, c.stop // rank):
            lanes = slice(at * rank - start, (at + 1) * rank - start)
            for kind in range(2):
                row = kind * pad + slots[at]
                added = jnp.sum(sums[kind][:, lanes], axis=1, keepdims=True)
                out_ref[row : row + 1, :] += jnp.broadcast_to(added, (1, LANES))


def score(table, slots, pick, mask, mine, other, cot, ups, start):
    return call(
        functools.partial(
            score_kernel, tuple(slots), len(ups) > len(slots), table.shape[0] // 2, start
        ),
        "score",
        (pick, mask, mine, other, cot, table, *ups),
        jax.ShapeDtypeStruct(table.shape, F32),
        SCORE_FLOPS,
        scalars=1,
    )


def bring_kernel(block_ref, *refs):
    out_ref, sem = refs[-2:]
    copy = pltpu.make_async_copy(block_ref, out_ref, sem)
    copy.start()
    copy.wait()


def bring(block, *tokens):
    hbm = pl.BlockSpec(memory_space=pl.ANY)
    return pl.pallas_call(
        bring_kernel,
        in_specs=[hbm] * (1 + len(tokens)),
        out_specs=pl.BlockSpec(memory_space=pltpu.VMEM),
        out_shape=jax.ShapeDtypeStruct(block.shape, block.dtype),
        scratch_shapes=[pltpu.SemaphoreType.DMA],
        compiler_params=pltpu.CompilerParams(vmem_limit_bytes=VMEM_LIMIT),
        cost_estimate=pl.CostEstimate(flops=0, bytes_accessed=0, transcendentals=0),
        name="bring",
    )(pltpu.with_memory_space_constraint(block, pltpu.HBM), *tokens)


def pull_kernel(rank, mask_ref, mine_ref, other_ref, cot_ref, *refs):
    out_ref = refs[-1]
    proj = mine_ref[:, rank : 2 * rank] + other_ref[:, rank : 2 * rank]
    own = proj * mask_ref[:, :rank]
    both = jnp.concatenate([own, proj - own], axis=1)
    high = both.astype(jnp.bfloat16)
    low = (both - high.astype(F32)).astype(jnp.bfloat16)
    left = jnp.concatenate([high, low], axis=1).T
    for c in columns_of(out_ref.shape[1], 1920):
        product = jnp.dot(left, cot_ref[:, c], preferred_element_type=F32)
        out_ref[:, c] = product[: 2 * rank] + product[2 * rank :]


def pull(mask, mine, other, cot, *tokens):
    rank = mine.shape[1] // 2
    return call(
        functools.partial(pull_kernel, rank),
        "pull",
        (mask, mine, other, cot, *tokens),
        jax.ShapeDtypeStruct((2 * rank, cot.shape[1]), F32),
        0,
        tokens=len(tokens),
    )


def dot_kernel(slot, pad, start, pick_ref, table_ref, pulled_ref, *refs):
    up_refs, out_ref = refs[:-1], refs[-1]
    rank, width = up_refs[0].shape
    out_ref[...] = table_ref[...]
    totals = [jnp.zeros((rank, LANES), F32)] * 2
    for at in range(0, width, LANES):
        blocks = [u[:, at : at + LANES] for u in up_refs]
        up = blocks[0] if len(blocks) == 1 else jnp.where(pick_ref[0] > 0, *blocks)
        up = up.astype(F32)
        for kind in range(2):
            rows = slice(kind * rank, (kind + 1) * rank)
            totals[kind] += up * pulled_ref[rows, start + at : start + at + LANES]
    for kind in range(2):
        row = kind * pad + slot
        sums = jnp.sum(jnp.sum(totals[kind], axis=0, keepdims=True), axis=1, keepdims=True)
        out_ref[row : row + 1, :] += jnp.broadcast_to(sums, (1, LANES))


def dot(table, slot, pick, pulled, ups, start):
    return call(
        functools.partial(dot_kernel, slot, table.shape[0] // 2, start),
        "dot",
        (pick, table, pulled, *ups),
        jax.ShapeDtypeStruct(table.shape, F32),
        0,
        scalars=1,
    )


def finish_kernel(offsets, reach, corner_ref, mine_ref, other_ref, mask_ref, own_ref, rest_ref):
    pad = mine_ref.shape[0] // 2
    total = mine_ref[...] + other_ref[...]
    own = jnp.sum(mask_ref[...], axis=1, keepdims=True)
    counts = [jnp.maximum(n, 1.0) for n in (own, mask_ref.shape[1] - own)]
    lane = lax.broadcasted_iota(jnp.int32, (1, LANES), 1)
    corner = corner_ref[0]
    sums = [jnp.zeros((1, LANES), F32)] * 2
    for slot in range(len(offsets[0])):
        place = offsets[0][slot] + reach
        for other in range(1, len(offsets)):
            place = jnp.where(corner == other, offsets[other][slot] + reach, place)
        for kind in range(2):
            row = kind * pad + slot
            sums[kind] = jnp.where(lane == place, total[row : row + 1, :], sums[kind])
    for kind, ref in enumerate((own_ref, rest_ref)):
        ref[...] = (sums[kind] / counts[kind])[:, : ref.shape[1]]


def finish(mine, other, mask, corner, offsets, reach):
    shape = jax.ShapeDtypeStruct((1, 2 * reach + 1), F32)
    vmem = pl.BlockSpec(memory_space=pltpu.VMEM)
    return pl.pallas_call(
        functools.partial(finish_kernel, offsets, reach),
        in_specs=[pl.BlockSpec(memory_space=pltpu.SMEM), vmem, vmem, vmem],
        out_shape=(shape, shape),
        compiler_params=pltpu.CompilerParams(vmem_limit_bytes=VMEM_LIMIT),
        cost_estimate=pl.CostEstimate(flops=FLOPS, bytes_accessed=0, transcendentals=0),
        name="finish",
    )(corner, mine, other, mask)


def rest_of_sum(block):
    parts = lax.axis_size("tensor")
    if parts == 2:
        return lax.ppermute(block, "tensor", [(0, 1), (1, 0)])
    return lax.psum(block, "tensor") - block


def send(block, target, corners=None):
    count = lax.axis_size("skill")
    pairs = [(s, target(s) % count) for s in range(count) if corners is None or s % 4 in corners]
    return lax.ppermute(block, "skill", pairs)


def across(s):
    return s ^ 1


def down(s):
    return s ^ 2


def next_quad(s):
    return s - 4 if s & 2 else s + 4


QUAD_OFFSETS = ((0, 1, 2, -2, -1), (0, -1, 2, -2, 1), (0, 1, -2, 2, -1), (0, -1, -2, 2, 1))


def after(block, *others):
    return lax.optimization_barrier((block, *others))[0]


def spread_ring(block, reach):
    slots, ahead, behind = [block], block, block
    for _ in range(reach):
        ahead = send(ahead, lambda s: s - 1)
        behind = send(behind, lambda s: s + 1)
        slots += [ahead, behind]
    return slots


def on_device(
    stored_inputs,
    stored_output_gradient,
    training_token_index,
    validation_inputs,
    validation_output_gradient,
    validation_row_skill,
    adapter_down_init,
):
    reach = lax.axis_size("skill") // 8
    columns = 2 * reach + 1
    pad = -(-columns // 8) * 8
    my_skill = lax.axis_index("skill")
    corner = my_skill & 3
    ends = (corner == 0) | (corner == 3)
    pick = ends.astype(jnp.int32)[None]
    factor = adapter_down_init[0].T
    valid_act = validation_inputs[0]
    valid_cot = validation_output_gradient[0]
    cot = stored_output_gradient[0]
    train, hidden = cot.shape

    own = (validation_row_skill == my_skill).astype(F32)
    mask = jnp.broadcast_to(own[0][:, None], (own.shape[1], LANES))
    counts = jnp.sum(
        (training_token_index[0][:, None] == jnp.arange(train)[None, :]).astype(F32),
        axis=0, keepdims=True,
    )
    table = jnp.zeros((2 * pad, LANES), F32)

    gather = functools.partial(score, pick=pick, mask=mask)
    if reach == 2:
        half = hidden * 55 // 100 // LANES * LANES
        down_x, down_y = send(factor, across), send(factor, down)
        proj = project(stored_inputs[0], [factor], flip=True)
        proj_rest = rest_of_sum(proj)
        up_a, up_b = up_factor(proj, proj_rest, counts, cot, [half, hidden - half])
        a_x, a_y = send(up_a, across), send(up_a, down)
        down_z = send(after(down_y, up_a), next_quad)
        near = project(valid_act, [factor, down_x, down_y], up_a, flops=3 * FLOPS)
        near_rest = rest_of_sum(near)
        b_x, b_y = send(up_b, across), send(after(up_b, a_y), down)
        a_z = send(after(a_y, a_x), next_quad)
        held = bring(valid_cot, near, up_b)
        near_slots = dict(slots=(0, 1, 2), mine=near, other=near_rest, cot=held)
        table = gather(after(table, down_z), ups=[up_a, a_x, a_y], start=0, **near_slots)
        down_last = jnp.where(ends, down_y, after(down_z, table))
        down_w = send(down_last, across)
        b_z = send(after(b_y, table), next_quad)
        b_d = send(after(b_x, down_last), down)
        a_w = send(jnp.where(ends, a_y, a_z), across)
        table = gather(table, ups=[up_b, b_x, b_y], start=half, **near_slots)
        b_w = send(after(b_d, table), next_quad, (0, 3))
        far = project(valid_act, [down_z, down_w], table, b_z)
        far_rest = rest_of_sum(far)
        far_slot = dict(slots=(3,), mine=far, other=far_rest, cot=held)
        table = gather(table, ups=[a_z], start=0, **far_slot)
        pulled = pull(mask, far, far_rest, held, table)
        table = gather(table, ups=[b_z], start=half, **far_slot)
        table = dot(table, 4, pick, pulled, [a_w], 0)
        table = dot(table, 4, pick, pulled, [b_w, b_d], half)
        offsets = QUAD_OFFSETS
    else:
        downs = spread_ring(factor, reach)
        proj = project(stored_inputs[0], [factor], flip=True)
        (up,) = up_factor(proj, rest_of_sum(proj), counts, cot, [hidden])
        ups = spread_ring(up, reach)
        for at in range(0, columns, 3):
            slots = range(at, min(at + 3, columns))
            mine = project(valid_act, [downs[s] for s in slots])
            table = gather(
                table, slots=slots, cot=valid_cot, mine=mine, other=rest_of_sum(mine),
                ups=[ups[s] for s in slots], start=0,
            )
        offsets = ((0, *(o for d in range(reach) for o in (d + 1, -d - 1))),)

    return finish(table, rest_of_sum(table), own, corner[None], offsets, reach)


def solution(mesh):
    in_specs = (
        P("skill", None, "tensor"),
        P("skill", None, "tensor"),
        P("skill", None),
        P("skill", None, "tensor"),
        P("skill", None, "tensor"),
        P("skill", None),
        P("skill", "tensor", None),
    )
    out_specs = (P("skill", None), P("skill", None))
    return jax.shard_map(
        on_device, mesh=mesh, in_specs=in_specs, out_specs=out_specs, check_vma=False
    )
```

```python
import functools

import jax
import jax.numpy as jnp
from jax import lax
from jax.experimental import pallas as pl
from jax.experimental.pallas import tpu as pltpu
from jax.sharding import PartitionSpec as P

VMEM_LIMIT = 16 * 1024 * 1024
LANES = 128
NT = (((1,), (1,)), ((), ()))
FLOPS = 1_000_000_000
SCORE_FLOPS = 0
F32 = jnp.float32


def tile_of(width, most):
    fits = [size for size in range(LANES, min(width, most) + 1, LANES) if width % size == 0]
    return fits[-1] if fits else width


def columns_of(width, most):
    tile = tile_of(width, most)
    return [slice(at, at + tile) for at in range(0, width, tile)]


def total_of(parts):
    return functools.reduce(lambda a, b: a + b, parts)


def call(kernel, name, operands, out, flops, scalars=0, tokens=0):
    vmem = pl.BlockSpec(memory_space=pltpu.VMEM)
    return pl.pallas_call(
        kernel,
        in_specs=[pl.BlockSpec(memory_space=pltpu.SMEM)] * scalars
        + [vmem] * (len(operands) - scalars - tokens)
        + [pl.BlockSpec(memory_space=pl.ANY)] * tokens,
        out_specs=jax.tree.map(lambda _: vmem, out),
        out_shape=out,
        compiler_params=pltpu.CompilerParams(vmem_limit_bytes=VMEM_LIMIT),
        cost_estimate=pl.CostEstimate(flops=flops, bytes_accessed=0, transcendentals=0),
        name=name,
    )(*operands)


def project_kernel(count, flip, *refs):
    rows_ref, factor_refs, out_ref = refs[0], refs[1 : 1 + count], refs[-1]
    parts = []
    for c in columns_of(rows_ref.shape[1], 2048):
        rows = rows_ref[:, c]
        factors = jnp.concatenate([f[:, c] for f in factor_refs], axis=0)
        ends = (factors, rows) if flip else (rows, factors)
        parts.append(lax.dot_general(*ends, NT, preferred_element_type=F32))
    out_ref[...] = total_of(parts)


def project(rows, factors, *tokens, flip=False, flops=None):
    n = rows.shape[0]
    count, rank = len(factors), sum(f.shape[0] for f in factors)
    return call(
        functools.partial(project_kernel, count, flip),
        "project",
        (rows, *factors, *tokens),
        jax.ShapeDtypeStruct((rank, n) if flip else (n, rank), F32),
        FLOPS if flops is None else flops,
        tokens=len(tokens),
    )


def up_kernel(scale, mine_ref, other_ref, counts_ref, cot_ref, *out_refs):
    rank, start = out_refs[0].shape[0], 0
    proj = (mine_ref[...] + other_ref[...]).astype(jnp.bfloat16).astype(F32)
    weighted = proj * counts_ref[...]
    high = weighted.astype(jnp.bfloat16)
    low = (weighted - high.astype(F32)).astype(jnp.bfloat16)
    both = jnp.concatenate([high, low], axis=0)
    for out_ref in out_refs:
        for c in columns_of(out_ref.shape[1], 1920):
            cot = cot_ref[:, start + c.start : start + c.stop]
            product = jnp.dot(both, cot, preferred_element_type=F32)
            out_ref[:, c] = ((product[:rank] + product[rank:]) * scale).astype(jnp.bfloat16)
        start += out_ref.shape[1]


def up_factor(mine, other, counts, cot, widths):
    rank, train = mine.shape
    return call(
        functools.partial(up_kernel, -1.0 / train),
        "up_factor",
        (mine, other, counts, cot),
        tuple(jax.ShapeDtypeStruct((rank, width), jnp.bfloat16) for width in widths),
        FLOPS,
    )


def score_kernel(slots, picked, pad, start, *refs):
    pick_ref, mask_ref, mine_ref, other_ref, cot_ref, table_ref = refs[:6]
    up_refs, out_ref = refs[6:-1], refs[-1]
    rank, width = up_refs[0].shape
    parts = []
    for c in columns_of(width, 1920):
        factors = [u[:, c] for u in up_refs]
        if picked:
            factors[-2:] = [jnp.where(pick_ref[0] > 0, factors[-2], factors[-1])]
        cot = cot_ref[:, start + c.start : start + c.stop]
        parts.append(
            lax.dot_general(
                cot, jnp.concatenate(factors, axis=0), NT, preferred_element_type=F32
            )
        )
    total = total_of(parts)
    out_ref[...] = table_ref[...]
    for start in range(0, total.shape[1], LANES):
        c = slice(start, min(start + LANES, total.shape[1]))
        change = total[:, c] * (mine_ref[:, c] + other_ref[:, c])
        own = change * mask_ref[:, : c.stop - c.start]
        sums = [jnp.sum(part, axis=0, keepdims=True) for part in (own, change - own)]
        for at in range(c.start // rank, c.stop // rank):
            lanes = slice(at * rank - start, (at + 1) * rank - start)
            for kind in range(2):
                row = kind * pad + slots[at]
                added = jnp.sum(sums[kind][:, lanes], axis=1, keepdims=True)
                out_ref[row : row + 1, :] += jnp.broadcast_to(added, (1, LANES))


def score(table, slots, pick, mask, mine, other, cot, ups, start):
    return call(
        functools.partial(
            score_kernel, tuple(slots), len(ups) > len(slots), table.shape[0] // 2, start
        ),
        "score",
        (pick, mask, mine, other, cot, table, *ups),
        jax.ShapeDtypeStruct(table.shape, F32),
        SCORE_FLOPS,
        scalars=1,
    )


def bring_kernel(block_ref, *refs):
    out_ref, sem = refs[-2:]
    copy = pltpu.make_async_copy(block_ref, out_ref, sem)
    copy.start()
    copy.wait()


def bring(block, *tokens):
    hbm = pl.BlockSpec(memory_space=pl.ANY)
    return pl.pallas_call(
        bring_kernel,
        in_specs=[hbm] * (1 + len(tokens)),
        out_specs=pl.BlockSpec(memory_space=pltpu.VMEM),
        out_shape=jax.ShapeDtypeStruct(block.shape, block.dtype),
        scratch_shapes=[pltpu.SemaphoreType.DMA],
        compiler_params=pltpu.CompilerParams(vmem_limit_bytes=VMEM_LIMIT),
        cost_estimate=pl.CostEstimate(flops=0, bytes_accessed=0, transcendentals=0),
        name="bring",
    )(pltpu.with_memory_space_constraint(block, pltpu.HBM), *tokens)


def pull_kernel(rank, mask_ref, mine_ref, other_ref, cot_ref, *refs):
    out_ref = refs[-1]
    proj = mine_ref[:, rank : 2 * rank] + other_ref[:, rank : 2 * rank]
    own = proj * mask_ref[:, :rank]
    both = jnp.concatenate([own, proj - own], axis=1)
    high = both.astype(jnp.bfloat16)
    low = (both - high.astype(F32)).astype(jnp.bfloat16)
    left = jnp.concatenate([high, low], axis=1).T
    for c in columns_of(out_ref.shape[1], 1920):
        product = jnp.dot(left, cot_ref[:, c], preferred_element_type=F32)
        out_ref[:, c] = product[: 2 * rank] + product[2 * rank :]


def pull(mask, mine, other, cot, *tokens):
    rank = mine.shape[1] // 2
    return call(
        functools.partial(pull_kernel, rank),
        "pull",
        (mask, mine, other, cot, *tokens),
        jax.ShapeDtypeStruct((2 * rank, cot.shape[1]), F32),
        0,
        tokens=len(tokens),
    )


def dot_kernel(slot, pad, start, pick_ref, table_ref, pulled_ref, *refs):
    up_refs, out_ref = refs[:-1], refs[-1]
    rank, width = up_refs[0].shape
    out_ref[...] = table_ref[...]
    totals = [jnp.zeros((rank, LANES), F32)] * 2
    for at in range(0, width, LANES):
        blocks = [u[:, at : at + LANES] for u in up_refs]
        up = blocks[0] if len(blocks) == 1 else jnp.where(pick_ref[0] > 0, *blocks)
        up = up.astype(F32)
        for kind in range(2):
            rows = slice(kind * rank, (kind + 1) * rank)
            totals[kind] += up * pulled_ref[rows, start + at : start + at + LANES]
    for kind in range(2):
        row = kind * pad + slot
        sums = jnp.sum(jnp.sum(totals[kind], axis=0, keepdims=True), axis=1, keepdims=True)
        out_ref[row : row + 1, :] += jnp.broadcast_to(sums, (1, LANES))


def dot(table, slot, pick, pulled, ups, start):
    return call(
        functools.partial(dot_kernel, slot, table.shape[0] // 2, start),
        "dot",
        (pick, table, pulled, *ups),
        jax.ShapeDtypeStruct(table.shape, F32),
        0,
        scalars=1,
    )


def finish_kernel(offsets, reach, corner_ref, mine_ref, other_ref, mask_ref, own_ref, rest_ref):
    pad = mine_ref.shape[0] // 2
    total = mine_ref[...] + other_ref[...]
    own = jnp.sum(mask_ref[...], axis=1, keepdims=True)
    counts = [jnp.maximum(n, 1.0) for n in (own, mask_ref.shape[1] - own)]
    lane = lax.broadcasted_iota(jnp.int32, (1, LANES), 1)
    corner = corner_ref[0]
    sums = [jnp.zeros((1, LANES), F32)] * 2
    for slot in range(len(offsets[0])):
        place = offsets[0][slot] + reach
        for other in range(1, len(offsets)):
            place = jnp.where(corner == other, offsets[other][slot] + reach, place)
        for kind in range(2):
            row = kind * pad + slot
            sums[kind] = jnp.where(lane == place, total[row : row + 1, :], sums[kind])
    for kind, ref in enumerate((own_ref, rest_ref)):
        ref[...] = (sums[kind] / counts[kind])[:, : ref.shape[1]]


def finish(mine, other, mask, corner, offsets, reach):
    shape = jax.ShapeDtypeStruct((1, 2 * reach + 1), F32)
    vmem = pl.BlockSpec(memory_space=pltpu.VMEM)
    return pl.pallas_call(
        functools.partial(finish_kernel, offsets, reach),
        in_specs=[pl.BlockSpec(memory_space=pltpu.SMEM), vmem, vmem, vmem],
        out_shape=(shape, shape),
        compiler_params=pltpu.CompilerParams(vmem_limit_bytes=VMEM_LIMIT),
        cost_estimate=pl.CostEstimate(flops=FLOPS, bytes_accessed=0, transcendentals=0),
        name="finish",
    )(corner, mine, other, mask)


def rest_of_sum(block):
    parts = lax.axis_size("tensor")
    if parts == 2:
        return lax.ppermute(block, "tensor", [(0, 1), (1, 0)])
    return lax.psum(block, "tensor") - block


def send(block, target, corners=None):
    count = lax.axis_size("skill")
    pairs = [(s, target(s) % count) for s in range(count) if corners is None or s % 4 in corners]
    return lax.ppermute(block, "skill", pairs)


def across(s):
    return s ^ 1


def down(s):
    return s ^ 2


def next_quad(s):
    return s - 4 if s & 2 else s + 4


QUAD_OFFSETS = ((0, 1, 2, -2, -1), (0, -1, 2, -2, 1), (0, 1, -2, 2, -1), (0, -1, -2, 2, 1))


def after(block, *others):
    return lax.optimization_barrier((block, *others))[0]


def spread_ring(block, reach):
    slots, ahead, behind = [block], block, block
    for _ in range(reach):
        ahead = send(ahead, lambda s: s - 1)
        behind = send(behind, lambda s: s + 1)
        slots += [ahead, behind]
    return slots


def on_device(
    stored_inputs,
    stored_output_gradient,
    training_token_index,
    validation_inputs,
    validation_output_gradient,
    validation_row_skill,
    adapter_down_init,
):
    reach = lax.axis_size("skill") // 8
    columns = 2 * reach + 1
    pad = -(-columns // 8) * 8
    my_skill = lax.axis_index("skill")
    corner = my_skill & 3
    ends = (corner == 0) | (corner == 3)
    pick = ends.astype(jnp.int32)[None]
    factor = adapter_down_init[0].T
    valid_act = validation_inputs[0]
    valid_cot = validation_output_gradient[0]
    cot = stored_output_gradient[0]
    train, hidden = cot.shape

    own = (validation_row_skill == my_skill).astype(F32)
    mask = jnp.broadcast_to(own[0][:, None], (own.shape[1], LANES))
    counts = jnp.sum(
        (training_token_index[0][:, None] == jnp.arange(train)[None, :]).astype(F32),
        axis=0, keepdims=True,
    )
    table = jnp.zeros((2 * pad, LANES), F32)

    gather = functools.partial(score, pick=pick, mask=mask)
    if reach == 2:
        half = hidden * 55 // 100 // LANES * LANES
        down_x, down_y = send(factor, across), send(factor, down)
        proj = project(stored_inputs[0], [factor], flip=True)
        proj_rest = rest_of_sum(proj)
        up_a, up_b = up_factor(proj, proj_rest, counts, cot, [half, hidden - half])
        a_x, a_y = send(up_a, across), send(up_a, down)
        down_z = send(after(down_y, up_a), next_quad)
        near = project(valid_act, [factor, down_x, down_y], up_a, flops=3 * FLOPS)
        near_rest = rest_of_sum(near)
        b_x, b_y = send(up_b, across), send(after(up_b, a_y), down)
        a_z = send(after(a_y, up_b), next_quad)
        held = bring(valid_cot, near, a_x)
        near_slots = dict(slots=(0, 1, 2), mine=near, other=near_rest, cot=held)
        table = gather(table, ups=[up_a, a_x, a_y], start=0, **near_slots)
        down_last = jnp.where(ends, down_y, down_z)
        down_w = send(down_last, across)
        b_z = send(after(b_y, table), next_quad)
        b_d = send(after(b_x, down_last), down)
        a_w = send(jnp.where(ends, a_y, a_z), across)
        table = gather(table, ups=[up_b, b_x, b_y], start=half, **near_slots)
        b_w = send(after(b_d, table), next_quad, (0, 3))
        far = project(valid_act, [down_z, down_w], table, b_z, flops=0)
        far_rest = rest_of_sum(far)
        far_slot = dict(slots=(3,), mine=far, other=far_rest, cot=held)
        table = gather(table, ups=[a_z], start=0, **far_slot)
        pulled = pull(mask, far, far_rest, held, table, b_z)
        table = gather(table, ups=[b_z], start=half, **far_slot)
        table = dot(table, 4, pick, pulled, [a_w], 0)
        table = dot(table, 4, pick, pulled, [b_w, b_d], half)
        offsets = QUAD_OFFSETS
    else:
        downs = spread_ring(factor, reach)
        proj = project(stored_inputs[0], [factor], flip=True)
        (up,) = up_factor(proj, rest_of_sum(proj), counts, cot, [hidden])
        ups = spread_ring(up, reach)
        for at in range(0, columns, 3):
            slots = range(at, min(at + 3, columns))
            mine = project(valid_act, [downs[s] for s in slots])
            table = gather(
                table, slots=slots, cot=valid_cot, mine=mine, other=rest_of_sum(mine),
                ups=[ups[s] for s in slots], start=0,
            )
        offsets = ((0, *(o for d in range(reach) for o in (d + 1, -d - 1))),)

    return finish(table, rest_of_sum(table), own, corner[None], offsets, reach)


def solution(mesh):
    in_specs = (
        P("skill", None, "tensor"),
        P("skill", None, "tensor"),
        P("skill", None),
        P("skill", None, "tensor"),
        P("skill", None, "tensor"),
        P("skill", None),
        P("skill", "tensor", None),
    )
    out_specs = (P("skill", None), P("skill", None))
    return jax.shard_map(
        on_device, mesh=mesh, in_specs=in_specs, out_specs=out_specs, check_vma=False
    )
```

```python
import functools

import jax
import jax.numpy as jnp
from jax import lax
from jax.experimental import pallas as pl
from jax.experimental.pallas import tpu as pltpu
from jax.sharding import PartitionSpec as P

VMEM_LIMIT = 16 * 1024 * 1024
LANES = 128
NT = (((1,), (1,)), ((), ()))
FLOPS = 1_000_000_000
SCORE_FLOPS = 0
F32 = jnp.float32


def tile_of(width, most):
    fits = [size for size in range(LANES, min(width, most) + 1, LANES) if width % size == 0]
    return fits[-1] if fits else width


def columns_of(width, most):
    tile = tile_of(width, most)
    return [slice(at, at + tile) for at in range(0, width, tile)]


def total_of(parts):
    return functools.reduce(lambda a, b: a + b, parts)


def call(kernel, name, operands, out, flops, scalars=0, tokens=0):
    vmem = pl.BlockSpec(memory_space=pltpu.VMEM)
    return pl.pallas_call(
        kernel,
        in_specs=[pl.BlockSpec(memory_space=pltpu.SMEM)] * scalars
        + [vmem] * (len(operands) - scalars - tokens)
        + [pl.BlockSpec(memory_space=pl.ANY)] * tokens,
        out_specs=jax.tree.map(lambda _: vmem, out),
        out_shape=out,
        compiler_params=pltpu.CompilerParams(vmem_limit_bytes=VMEM_LIMIT),
        cost_estimate=pl.CostEstimate(flops=flops, bytes_accessed=0, transcendentals=0),
        name=name,
    )(*operands)


def project_kernel(count, flip, *refs):
    rows_ref, factor_refs, out_ref = refs[0], refs[1 : 1 + count], refs[-1]
    parts = []
    for c in columns_of(rows_ref.shape[1], 2048):
        rows = rows_ref[:, c]
        factors = jnp.concatenate([f[:, c] for f in factor_refs], axis=0)
        ends = (factors, rows) if flip else (rows, factors)
        parts.append(lax.dot_general(*ends, NT, preferred_element_type=F32))
    out_ref[...] = total_of(parts)


def project(rows, factors, *tokens, flip=False, flops=None):
    n = rows.shape[0]
    count, rank = len(factors), sum(f.shape[0] for f in factors)
    return call(
        functools.partial(project_kernel, count, flip),
        "project",
        (rows, *factors, *tokens),
        jax.ShapeDtypeStruct((rank, n) if flip else (n, rank), F32),
        FLOPS if flops is None else flops,
        tokens=len(tokens),
    )


def up_kernel(scale, mine_ref, other_ref, counts_ref, cot_ref, *out_refs):
    rank, start = out_refs[0].shape[0], 0
    proj = (mine_ref[...] + other_ref[...]).astype(jnp.bfloat16).astype(F32)
    weighted = proj * counts_ref[...]
    high = weighted.astype(jnp.bfloat16)
    low = (weighted - high.astype(F32)).astype(jnp.bfloat16)
    both = jnp.concatenate([high, low], axis=0)
    for out_ref in out_refs:
        for c in columns_of(out_ref.shape[1], 1920):
            cot = cot_ref[:, start + c.start : start + c.stop]
            product = jnp.dot(both, cot, preferred_element_type=F32)
            out_ref[:, c] = ((product[:rank] + product[rank:]) * scale).astype(jnp.bfloat16)
        start += out_ref.shape[1]


def up_factor(mine, other, counts, cot, widths):
    rank, train = mine.shape
    return call(
        functools.partial(up_kernel, -1.0 / train),
        "up_factor",
        (mine, other, counts, cot),
        tuple(jax.ShapeDtypeStruct((rank, width), jnp.bfloat16) for width in widths),
        FLOPS,
    )


def score_kernel(slots, picked, pad, start, *refs):
    pick_ref, mask_ref, mine_ref, other_ref, cot_ref, table_ref = refs[:6]
    up_refs, out_ref = refs[6:-1], refs[-1]
    rank, width = up_refs[0].shape
    parts = []
    for c in columns_of(width, 1920):
        factors = [u[:, c] for u in up_refs]
        if picked:
            factors[-2:] = [jnp.where(pick_ref[0] > 0, factors[-2], factors[-1])]
        cot = cot_ref[:, start + c.start : start + c.stop]
        parts.append(
            lax.dot_general(
                cot, jnp.concatenate(factors, axis=0), NT, preferred_element_type=F32
            )
        )
    total = total_of(parts)
    out_ref[...] = table_ref[...]
    for start in range(0, total.shape[1], LANES):
        c = slice(start, min(start + LANES, total.shape[1]))
        change = total[:, c] * (mine_ref[:, c] + other_ref[:, c])
        own = change * mask_ref[:, : c.stop - c.start]
        sums = [jnp.sum(part, axis=0, keepdims=True) for part in (own, change - own)]
        for at in range(c.start // rank, c.stop // rank):
            lanes = slice(at * rank - start, (at + 1) * rank - start)
            for kind in range(2):
                row = kind * pad + slots[at]
                added = jnp.sum(sums[kind][:, lanes], axis=1, keepdims=True)
                out_ref[row : row + 1, :] += jnp.broadcast_to(added, (1, LANES))


def score(table, slots, pick, mask, mine, other, cot, ups, start):
    return call(
        functools.partial(
            score_kernel, tuple(slots), len(ups) > len(slots), table.shape[0] // 2, start
        ),
        "score",
        (pick, mask, mine, other, cot, table, *ups),
        jax.ShapeDtypeStruct(table.shape, F32),
        SCORE_FLOPS,
        scalars=1,
    )


def bring_kernel(block_ref, *refs):
    out_ref, sem = refs[-2:]
    copy = pltpu.make_async_copy(block_ref, out_ref, sem)
    copy.start()
    copy.wait()


def bring(block, *tokens):
    hbm = pl.BlockSpec(memory_space=pl.ANY)
    return pl.pallas_call(
        bring_kernel,
        in_specs=[hbm] * (1 + len(tokens)),
        out_specs=pl.BlockSpec(memory_space=pltpu.VMEM),
        out_shape=jax.ShapeDtypeStruct(block.shape, block.dtype),
        scratch_shapes=[pltpu.SemaphoreType.DMA],
        compiler_params=pltpu.CompilerParams(vmem_limit_bytes=VMEM_LIMIT),
        cost_estimate=pl.CostEstimate(flops=0, bytes_accessed=0, transcendentals=0),
        name="bring",
    )(pltpu.with_memory_space_constraint(block, pltpu.HBM), *tokens)


def pull_kernel(mask_ref, mine_ref, other_ref, cot_ref, *refs):
    out_ref = refs[-1]
    proj = mine_ref[...] + other_ref[...]
    own = proj * mask_ref[:, : proj.shape[1]]
    left = jnp.concatenate([own, proj - own], axis=1).astype(jnp.bfloat16).T
    for c in columns_of(out_ref.shape[1], 1920):
        out_ref[:, c] = jnp.dot(left, cot_ref[:, c], preferred_element_type=F32)


def pull(mask, mine, other, cot, *tokens):
    return call(
        pull_kernel,
        "pull",
        (mask, mine, other, cot, *tokens),
        jax.ShapeDtypeStruct((2 * mine.shape[1], cot.shape[1]), F32),
        0,
        tokens=len(tokens),
    )


def dot_kernel(slot, place, pad, start, pick_ref, table_ref, pulled_ref, *refs):
    up_refs, out_ref = refs[:-1], refs[-1]
    rank, width = up_refs[0].shape
    out_ref[...] = table_ref[...]
    first = [place * rank, pulled_ref.shape[0] // 2 + place * rank]
    totals = [jnp.zeros((rank, LANES), F32)] * 2
    for at in range(0, width, LANES):
        blocks = [u[:, at : at + LANES] for u in up_refs]
        up = blocks[0] if len(blocks) == 1 else jnp.where(pick_ref[0] > 0, *blocks)
        up = up.astype(F32)
        for kind in range(2):
            rows = slice(first[kind], first[kind] + rank)
            totals[kind] += up * pulled_ref[rows, start + at : start + at + LANES]
    for kind in range(2):
        row = kind * pad + slot
        sums = jnp.sum(jnp.sum(totals[kind], axis=0, keepdims=True), axis=1, keepdims=True)
        out_ref[row : row + 1, :] += jnp.broadcast_to(sums, (1, LANES))


def dot(table, slot, place, pick, pulled, ups, start):
    return call(
        functools.partial(dot_kernel, slot, place, table.shape[0] // 2, start),
        "dot",
        (pick, table, pulled, *ups),
        jax.ShapeDtypeStruct(table.shape, F32),
        0,
        scalars=1,
    )


def finish_kernel(offsets, reach, corner_ref, mine_ref, other_ref, mask_ref, own_ref, rest_ref):
    pad = mine_ref.shape[0] // 2
    total = mine_ref[...] + other_ref[...]
    own = jnp.sum(mask_ref[...], axis=1, keepdims=True)
    counts = [jnp.maximum(n, 1.0) for n in (own, mask_ref.shape[1] - own)]
    lane = lax.broadcasted_iota(jnp.int32, (1, LANES), 1)
    corner = corner_ref[0]
    sums = [jnp.zeros((1, LANES), F32)] * 2
    for slot in range(len(offsets[0])):
        place = offsets[0][slot] + reach
        for other in range(1, len(offsets)):
            place = jnp.where(corner == other, offsets[other][slot] + reach, place)
        for kind in range(2):
            row = kind * pad + slot
            sums[kind] = jnp.where(lane == place, total[row : row + 1, :], sums[kind])
    for kind, ref in enumerate((own_ref, rest_ref)):
        ref[...] = (sums[kind] / counts[kind])[:, : ref.shape[1]]


def finish(mine, other, mask, corner, offsets, reach):
    shape = jax.ShapeDtypeStruct((1, 2 * reach + 1), F32)
    vmem = pl.BlockSpec(memory_space=pltpu.VMEM)
    return pl.pallas_call(
        functools.partial(finish_kernel, offsets, reach),
        in_specs=[pl.BlockSpec(memory_space=pltpu.SMEM), vmem, vmem, vmem],
        out_shape=(shape, shape),
        compiler_params=pltpu.CompilerParams(vmem_limit_bytes=VMEM_LIMIT),
        cost_estimate=pl.CostEstimate(flops=FLOPS, bytes_accessed=0, transcendentals=0),
        name="finish",
    )(corner, mine, other, mask)


def rest_of_sum(block):
    parts = lax.axis_size("tensor")
    if parts == 2:
        return lax.ppermute(block, "tensor", [(0, 1), (1, 0)])
    return lax.psum(block, "tensor") - block


def send(block, target, corners=None):
    count = lax.axis_size("skill")
    pairs = [(s, target(s) % count) for s in range(count) if corners is None or s % 4 in corners]
    return lax.ppermute(block, "skill", pairs)


def across(s):
    return s ^ 1


def down(s):
    return s ^ 2


def next_quad(s):
    return s - 4 if s & 2 else s + 4


QUAD_OFFSETS = ((0, 1, 2, -2, -1), (0, -1, 2, -2, 1), (0, 1, -2, 2, -1), (0, -1, -2, 2, 1))


def after(block, *others):
    return lax.optimization_barrier((block, *others))[0]


def spread_ring(block, reach):
    slots, ahead, behind = [block], block, block
    for _ in range(reach):
        ahead = send(ahead, lambda s: s - 1)
        behind = send(behind, lambda s: s + 1)
        slots += [ahead, behind]
    return slots


def on_device(
    stored_inputs,
    stored_output_gradient,
    training_token_index,
    validation_inputs,
    validation_output_gradient,
    validation_row_skill,
    adapter_down_init,
):
    reach = lax.axis_size("skill") // 8
    columns = 2 * reach + 1
    pad = -(-columns // 8) * 8
    my_skill = lax.axis_index("skill")
    corner = my_skill & 3
    ends = (corner == 0) | (corner == 3)
    pick = ends.astype(jnp.int32)[None]
    factor = adapter_down_init[0].T
    valid_act = validation_inputs[0]
    valid_cot = validation_output_gradient[0]
    cot = stored_output_gradient[0]
    train, hidden = cot.shape

    own = (validation_row_skill == my_skill).astype(F32)
    mask = jnp.broadcast_to(own[0][:, None], (own.shape[1], LANES))
    counts = jnp.sum(
        (training_token_index[0][:, None] == jnp.arange(train)[None, :]).astype(F32),
        axis=0, keepdims=True,
    )
    table = jnp.zeros((2 * pad, LANES), F32)

    gather = functools.partial(score, pick=pick, mask=mask)
    if reach == 2:
        half = hidden * 55 // 100 // LANES * LANES
        down_x, down_y = send(factor, across), send(factor, down)
        proj = project(stored_inputs[0], [factor], flip=True)
        proj_rest = rest_of_sum(proj)
        up_a, up_b = up_factor(proj, proj_rest, counts, cot, [half, hidden - half])
        a_x, a_y = send(up_a, across), send(up_a, down)
        down_z = send(after(down_y, up_a), next_quad)
        near = project(valid_act, [factor, down_x, down_y], up_a, flops=3 * FLOPS)
        near_rest = rest_of_sum(near)
        b_x, b_y = send(up_b, across), send(after(up_b, a_y), down)
        a_z = send(after(a_y, up_b), next_quad)
        held = bring(valid_cot, near, a_x)
        near_slots = dict(slots=(0, 1, 2), mine=near, other=near_rest, cot=held)
        table = gather(table, ups=[up_a, a_x, a_y], start=0, **near_slots)
        down_last = jnp.where(ends, down_y, down_z)
        down_w = send(down_last, across)
        b_z = send(after(b_y, table), next_quad)
        b_d = send(after(b_x, down_last), down)
        a_w = send(jnp.where(ends, a_y, a_z), across)
        table = gather(table, ups=[up_b, b_x, b_y], start=half, **near_slots)
        b_w = send(after(b_d, table), next_quad, (0, 3))
        far = project(valid_act, [down_z, down_w], table, b_z, flops=0)
        far_rest = rest_of_sum(far)
        pulled = pull(mask, far, far_rest, held, table, b_z)
        table = dot(table, 3, 0, pick, pulled, [a_z], 0)
        table = dot(table, 3, 0, pick, pulled, [b_z], half)
        table = dot(table, 4, 1, pick, pulled, [a_w], 0)
        table = dot(table, 4, 1, pick, pulled, [b_w, b_d], half)
        offsets = QUAD_OFFSETS
    else:
        downs = spread_ring(factor, reach)
        proj = project(stored_inputs[0], [factor], flip=True)
        (up,) = up_factor(proj, rest_of_sum(proj), counts, cot, [hidden])
        ups = spread_ring(up, reach)
        for at in range(0, columns, 3):
            slots = range(at, min(at + 3, columns))
            mine = project(valid_act, [downs[s] for s in slots])
            table = gather(
                table, slots=slots, cot=valid_cot, mine=mine, other=rest_of_sum(mine),
                ups=[ups[s] for s in slots], start=0,
            )
        offsets = ((0, *(o for d in range(reach) for o in (d + 1, -d - 1))),)

    return finish(table, rest_of_sum(table), own, corner[None], offsets, reach)


def solution(mesh):
    in_specs = (
        P("skill", None, "tensor"),
        P("skill", None, "tensor"),
        P("skill", None),
        P("skill", None, "tensor"),
        P("skill", None, "tensor"),
        P("skill", None),
        P("skill", "tensor", None),
    )
    out_specs = (P("skill", None), P("skill", None))
    return jax.shard_map(
        on_device, mesh=mesh, in_specs=in_specs, out_specs=out_specs, check_vma=False
    )
```

```python
import functools

import jax
import jax.numpy as jnp
from jax import lax
from jax.experimental import pallas as pl
from jax.experimental.pallas import tpu as pltpu
from jax.sharding import PartitionSpec as P

VMEM_LIMIT = 16 * 1024 * 1024
LANES = 128
NT = (((1,), (1,)), ((), ()))
FLOPS = 1_000_000_000
SCORE_FLOPS = 0
F32 = jnp.float32


def tile_of(width, most):
    fits = [size for size in range(LANES, min(width, most) + 1, LANES) if width % size == 0]
    return fits[-1] if fits else width


def columns_of(width, most):
    tile = tile_of(width, most)
    return [slice(at, at + tile) for at in range(0, width, tile)]


def total_of(parts):
    return functools.reduce(lambda a, b: a + b, parts)


def call(kernel, name, operands, out, flops, scalars=0, tokens=0):
    vmem = pl.BlockSpec(memory_space=pltpu.VMEM)
    return pl.pallas_call(
        kernel,
        in_specs=[pl.BlockSpec(memory_space=pltpu.SMEM)] * scalars
        + [vmem] * (len(operands) - scalars - tokens)
        + [pl.BlockSpec(memory_space=pl.ANY)] * tokens,
        out_specs=jax.tree.map(lambda _: vmem, out),
        out_shape=out,
        compiler_params=pltpu.CompilerParams(vmem_limit_bytes=VMEM_LIMIT),
        cost_estimate=pl.CostEstimate(flops=flops, bytes_accessed=0, transcendentals=0),
        name=name,
    )(*operands)


def project_kernel(count, flip, *refs):
    rows_ref, factor_refs, out_ref = refs[0], refs[1 : 1 + count], refs[-1]
    parts = []
    for c in columns_of(rows_ref.shape[1], 2048):
        rows = rows_ref[:, c]
        factors = jnp.concatenate([f[:, c] for f in factor_refs], axis=0)
        ends = (factors, rows) if flip else (rows, factors)
        parts.append(lax.dot_general(*ends, NT, preferred_element_type=F32))
    out_ref[...] = total_of(parts)


def project(rows, factors, *tokens, flip=False, flops=None):
    n = rows.shape[0]
    count, rank = len(factors), sum(f.shape[0] for f in factors)
    return call(
        functools.partial(project_kernel, count, flip),
        "project",
        (rows, *factors, *tokens),
        jax.ShapeDtypeStruct((rank, n) if flip else (n, rank), F32),
        FLOPS if flops is None else flops,
        tokens=len(tokens),
    )


def up_kernel(scale, mine_ref, other_ref, counts_ref, cot_ref, *out_refs):
    rank, start = out_refs[0].shape[0], 0
    proj = (mine_ref[...] + other_ref[...]).astype(jnp.bfloat16).astype(F32)
    weighted = proj * counts_ref[...]
    high = weighted.astype(jnp.bfloat16)
    low = (weighted - high.astype(F32)).astype(jnp.bfloat16)
    both = jnp.concatenate([high, low], axis=0)
    for out_ref in out_refs:
        for c in columns_of(out_ref.shape[1], 1920):
            cot = cot_ref[:, start + c.start : start + c.stop]
            product = jnp.dot(both, cot, preferred_element_type=F32)
            out_ref[:, c] = ((product[:rank] + product[rank:]) * scale).astype(jnp.bfloat16)
        start += out_ref.shape[1]


def up_factor(mine, other, counts, cot, widths):
    rank, train = mine.shape
    return call(
        functools.partial(up_kernel, -1.0 / train),
        "up_factor",
        (mine, other, counts, cot),
        tuple(jax.ShapeDtypeStruct((rank, width), jnp.bfloat16) for width in widths),
        FLOPS,
    )


def score_kernel(slots, picked, pad, start, *refs):
    pick_ref, mask_ref, mine_ref, other_ref, cot_ref, table_ref = refs[:6]
    up_refs, out_ref = refs[6:-1], refs[-1]
    rank, width = up_refs[0].shape
    parts = []
    for c in columns_of(width, 1920):
        factors = [u[:, c] for u in up_refs]
        if picked:
            factors[-2:] = [jnp.where(pick_ref[0] > 0, factors[-2], factors[-1])]
        cot = cot_ref[:, start + c.start : start + c.stop]
        parts.append(
            lax.dot_general(
                cot, jnp.concatenate(factors, axis=0), NT, preferred_element_type=F32
            )
        )
    total = total_of(parts)
    out_ref[...] = table_ref[...]
    for start in range(0, total.shape[1], LANES):
        c = slice(start, min(start + LANES, total.shape[1]))
        change = total[:, c] * (mine_ref[:, c] + other_ref[:, c])
        own = change * mask_ref[:, : c.stop - c.start]
        sums = [jnp.sum(part, axis=0, keepdims=True) for part in (own, change - own)]
        for at in range(c.start // rank, c.stop // rank):
            lanes = slice(at * rank - start, (at + 1) * rank - start)
            for kind in range(2):
                row = kind * pad + slots[at]
                added = jnp.sum(sums[kind][:, lanes], axis=1, keepdims=True)
                out_ref[row : row + 1, :] += jnp.broadcast_to(added, (1, LANES))


def score(table, slots, pick, mask, mine, other, cot, ups, start):
    return call(
        functools.partial(
            score_kernel, tuple(slots), len(ups) > len(slots), table.shape[0] // 2, start
        ),
        "score",
        (pick, mask, mine, other, cot, table, *ups),
        jax.ShapeDtypeStruct(table.shape, F32),
        SCORE_FLOPS,
        scalars=1,
    )


def bring_kernel(block_ref, *refs):
    out_ref, sem = refs[-2:]
    copy = pltpu.make_async_copy(block_ref, out_ref, sem)
    copy.start()
    copy.wait()


def bring(block, *tokens):
    hbm = pl.BlockSpec(memory_space=pl.ANY)
    return pl.pallas_call(
        bring_kernel,
        in_specs=[hbm] * (1 + len(tokens)),
        out_specs=pl.BlockSpec(memory_space=pltpu.VMEM),
        out_shape=jax.ShapeDtypeStruct(block.shape, block.dtype),
        scratch_shapes=[pltpu.SemaphoreType.DMA],
        compiler_params=pltpu.CompilerParams(vmem_limit_bytes=VMEM_LIMIT),
        cost_estimate=pl.CostEstimate(flops=0, bytes_accessed=0, transcendentals=0),
        name="bring",
    )(pltpu.with_memory_space_constraint(block, pltpu.HBM), *tokens)


def pull_kernel(rank, mask_ref, mine_ref, other_ref, cot_ref, *refs):
    out_ref = refs[-1]
    proj = mine_ref[:, rank : 2 * rank] + other_ref[:, rank : 2 * rank]
    own = proj * mask_ref[:, :rank]
    both = jnp.concatenate([own, proj - own], axis=1)
    left = both.astype(jnp.bfloat16).T
    for c in columns_of(out_ref.shape[1], 1920):
        out_ref[:, c] = jnp.dot(left, cot_ref[:, c], preferred_element_type=F32)


def pull(mask, mine, other, cot, *tokens):
    rank = mine.shape[1] // 2
    return call(
        functools.partial(pull_kernel, rank),
        "pull",
        (mask, mine, other, cot, *tokens),
        jax.ShapeDtypeStruct((2 * rank, cot.shape[1]), F32),
        0,
        tokens=len(tokens),
    )


def dot_kernel(slot, pad, start, pick_ref, table_ref, pulled_ref, *refs):
    up_refs, out_ref = refs[:-1], refs[-1]
    rank, width = up_refs[0].shape
    out_ref[...] = table_ref[...]
    totals = [jnp.zeros((rank, LANES), F32)] * 2
    for at in range(0, width, LANES):
        blocks = [u[:, at : at + LANES] for u in up_refs]
        up = blocks[0] if len(blocks) == 1 else jnp.where(pick_ref[0] > 0, *blocks)
        up = up.astype(F32)
        for kind in range(2):
            rows = slice(kind * rank, (kind + 1) * rank)
            totals[kind] += up * pulled_ref[rows, start + at : start + at + LANES]
    for kind in range(2):
        row = kind * pad + slot
        sums = jnp.sum(jnp.sum(totals[kind], axis=0, keepdims=True), axis=1, keepdims=True)
        out_ref[row : row + 1, :] += jnp.broadcast_to(sums, (1, LANES))


def dot(table, slot, pick, pulled, ups, start):
    return call(
        functools.partial(dot_kernel, slot, table.shape[0] // 2, start),
        "dot",
        (pick, table, pulled, *ups),
        jax.ShapeDtypeStruct(table.shape, F32),
        0,
        scalars=1,
    )


def finish_kernel(offsets, reach, corner_ref, mine_ref, other_ref, mask_ref, own_ref, rest_ref):
    pad = mine_ref.shape[0] // 2
    total = mine_ref[...] + other_ref[...]
    own = jnp.sum(mask_ref[...], axis=1, keepdims=True)
    counts = [jnp.maximum(n, 1.0) for n in (own, mask_ref.shape[1] - own)]
    lane = lax.broadcasted_iota(jnp.int32, (1, LANES), 1)
    corner = corner_ref[0]
    sums = [jnp.zeros((1, LANES), F32)] * 2
    for slot in range(len(offsets[0])):
        place = offsets[0][slot] + reach
        for other in range(1, len(offsets)):
            place = jnp.where(corner == other, offsets[other][slot] + reach, place)
        for kind in range(2):
            row = kind * pad + slot
            sums[kind] = jnp.where(lane == place, total[row : row + 1, :], sums[kind])
    for kind, ref in enumerate((own_ref, rest_ref)):
        ref[...] = (sums[kind] / counts[kind])[:, : ref.shape[1]]


def finish(mine, other, mask, corner, offsets, reach):
    shape = jax.ShapeDtypeStruct((1, 2 * reach + 1), F32)
    vmem = pl.BlockSpec(memory_space=pltpu.VMEM)
    return pl.pallas_call(
        functools.partial(finish_kernel, offsets, reach),
        in_specs=[pl.BlockSpec(memory_space=pltpu.SMEM), vmem, vmem, vmem],
        out_shape=(shape, shape),
        compiler_params=pltpu.CompilerParams(vmem_limit_bytes=VMEM_LIMIT),
        cost_estimate=pl.CostEstimate(flops=FLOPS, bytes_accessed=0, transcendentals=0),
        name="finish",
    )(corner, mine, other, mask)


def rest_of_sum(block):
    parts = lax.axis_size("tensor")
    if parts == 2:
        return lax.ppermute(block, "tensor", [(0, 1), (1, 0)])
    return lax.psum(block, "tensor") - block


def send(block, target, corners=None):
    count = lax.axis_size("skill")
    pairs = [(s, target(s) % count) for s in range(count) if corners is None or s % 4 in corners]
    return lax.ppermute(block, "skill", pairs)


def across(s):
    return s ^ 1


def down(s):
    return s ^ 2


def next_quad(s):
    return s - 4 if s & 2 else s + 4


QUAD_OFFSETS = ((0, 1, 2, -2, -1), (0, -1, 2, -2, 1), (0, 1, -2, 2, -1), (0, -1, -2, 2, 1))


def after(block, *others):
    return lax.optimization_barrier((block, *others))[0]


def spread_ring(block, reach):
    slots, ahead, behind = [block], block, block
    for _ in range(reach):
        ahead = send(ahead, lambda s: s - 1)
        behind = send(behind, lambda s: s + 1)
        slots += [ahead, behind]
    return slots


def on_device(
    stored_inputs,
    stored_output_gradient,
    training_token_index,
    validation_inputs,
    validation_output_gradient,
    validation_row_skill,
    adapter_down_init,
):
    reach = lax.axis_size("skill") // 8
    columns = 2 * reach + 1
    pad = -(-columns // 8) * 8
    my_skill = lax.axis_index("skill")
    corner = my_skill & 3
    ends = (corner == 0) | (corner == 3)
    pick = ends.astype(jnp.int32)[None]
    factor = adapter_down_init[0].T
    valid_act = validation_inputs[0]
    valid_cot = validation_output_gradient[0]
    cot = stored_output_gradient[0]
    train, hidden = cot.shape

    own = (validation_row_skill == my_skill).astype(F32)
    mask = jnp.broadcast_to(own[0][:, None], (own.shape[1], LANES))
    counts = jnp.sum(
        (training_token_index[0][:, None] == jnp.arange(train)[None, :]).astype(F32),
        axis=0, keepdims=True,
    )
    table = jnp.zeros((2 * pad, LANES), F32)

    gather = functools.partial(score, pick=pick, mask=mask)
    if reach == 2:
        half = hidden * 55 // 100 // LANES * LANES
        down_x, down_y = send(factor, across), send(factor, down)
        proj = project(stored_inputs[0], [factor], flip=True)
        proj_rest = rest_of_sum(proj)
        up_a, up_b = up_factor(proj, proj_rest, counts, cot, [half, hidden - half])
        a_x, a_y = send(up_a, across), send(up_a, down)
        down_z = send(after(down_y, up_a), next_quad)
        near = project(valid_act, [factor, down_x, down_y], up_a, flops=3 * FLOPS)
        near_rest = rest_of_sum(near)
        b_x, b_y = send(up_b, across), send(after(up_b, a_y), down)
        a_z = send(after(a_y, up_b), next_quad)
        held = bring(valid_cot, near, a_x)
        near_slots = dict(slots=(0, 1, 2), mine=near, other=near_rest, cot=held)
        table = gather(table, ups=[up_a, a_x, a_y], start=0, **near_slots)
        down_last = jnp.where(ends, down_y, down_z)
        down_w = send(down_last, across)
        b_z = send(after(b_y, table), next_quad)
        b_d = send(after(b_x, down_last), down)
        a_w = send(jnp.where(ends, a_y, a_z), across)
        table = gather(table, ups=[up_b, b_x, b_y], start=half, **near_slots)
        b_w = send(after(b_d, table), next_quad, (0, 3))
        far = project(valid_act, [down_z, down_w], table, b_z, flops=0)
        far_rest = rest_of_sum(far)
        far_slot = dict(slots=(3,), mine=far, other=far_rest, cot=held)
        table = gather(table, ups=[a_z], start=0, **far_slot)
        pulled = pull(mask, far, far_rest, held, table, b_z)
        table = gather(table, ups=[b_z], start=half, **far_slot)
        table = dot(table, 4, pick, pulled, [a_w], 0)
        table = dot(table, 4, pick, pulled, [b_w, b_d], half)
        offsets = QUAD_OFFSETS
    else:
        downs = spread_ring(factor, reach)
        proj = project(stored_inputs[0], [factor], flip=True)
        (up,) = up_factor(proj, rest_of_sum(proj), counts, cot, [hidden])
        ups = spread_ring(up, reach)
        for at in range(0, columns, 3):
            slots = range(at, min(at + 3, columns))
            mine = project(valid_act, [downs[s] for s in slots])
            table = gather(
                table, slots=slots, cot=valid_cot, mine=mine, other=rest_of_sum(mine),
                ups=[ups[s] for s in slots], start=0,
            )
        offsets = ((0, *(o for d in range(reach) for o in (d + 1, -d - 1))),)

    return finish(table, rest_of_sum(table), own, corner[None], offsets, reach)


def solution(mesh):
    in_specs = (
        P("skill", None, "tensor"),
        P("skill", None, "tensor"),
        P("skill", None),
        P("skill", None, "tensor"),
        P("skill", None, "tensor"),
        P("skill", None),
        P("skill", "tensor", None),
    )
    out_specs = (P("skill", None), P("skill", None))
    return jax.shard_map(
        on_device, mesh=mesh, in_specs=in_specs, out_specs=out_specs, check_vma=False
    )
```
